32 devices in a mesh: rows: 8 (over z, y), grp: 4 (over x, core).
Axes of the slice: x: 2, y: 2, z: 4, core: 2. Of those that a mesh axis runs over, the one named last changes fastest.
Arguments:
- features: bfloat16 [15456, 512], P('rows', 'grp'), may hold values from -40 to 40
- image_group: int32 [6], replicated, may hold values from 0 to 2, as said below
- switches: int32 [3864], P('rows'), may hold values from 0 to 3
- enc_weight: bfloat16 [3, 9, 512, 512], P(None, None, 'rows', 'grp'), may hold values from -0.09375 to 0.09375
- dec_weight: bfloat16 [3, 9, 512, 512], P(None, None, 'rows', 'grp'), may hold values from -0.09375 to 0.09375
- enc_gain: float32 [3, 512], P(None, 'grp'), may hold values from 0.25 to 1.75
- enc_bias: float32 [3, 512], P(None, 'grp'), may hold values from -2 to 2
- dec_gain: float32 [3, 512], P(None, 'grp'), may hold values from 0.25 to 1.75
- dec_bias: float32 [3, 512], P(None, 'grp'), may hold values from -2 to 2
- d_decoded: bfloat16 [15456, 512], P('rows', 'grp'), may hold values from -6 to 6
Outputs:
- decoded: bfloat16 [15456, 512], P('rows', 'grp')
- features_grad: bfloat16 [15456, 512], P('rows', 'grp')
- enc_weight_grad: float32 [3, 9, 512, 512], P(None, None, 'rows', 'grp')
- dec_weight_grad: float32 [3, 9, 512, 512], P(None, None, 'rows', 'grp')
- enc_gain_grad: float32 [3, 512], P(None, 'grp')
- enc_bias_grad: float32 [3, 512], P(None, 'grp')
- dec_gain_grad: float32 [3, 512], P(None, 'grp')
- dec_bias_grad: float32 [3, 512], P(None, 'grp')
The draws below stay inside these ranges and needn't reach their ends.
Inputs may be any that keep to these rules, and one draw needn't show every extreme that they name: `image_group`: each of the three sizes names exactly 2 images.
All inputs are finite; a program needn't handle non-finite values.
Results may differ from the reference program's by a relative error of at most 0.033.
Values may be sent and summed in bfloat16 or wider, within the bound.
A program may use at most 320 MiB of HBM per device.

```python
import jax
import jax.numpy as jnp
from jax import lax

C = 512
H1 = 15
W1 = 20
H2 = 18
W2 = 24
H3 = 30
W3 = 40
NIMG = 6
WINDOWS = 3864
PIX = 15456


def draw_features(key, part):
    key = jax.random.fold_in(key, 11)
    key_scale, key_values = jax.random.split(key, 2)
    position = jnp.arange(PIX, dtype=jnp.float32) / PIX
    rough = jax.random.uniform(key_scale, (PIX,), jnp.float32)
    scale = 10.0 ** (0.5 * position + 0.5 * rough)
    values = jnp.clip(jax.random.normal(key_values, (PIX, C), jnp.float32), -4.0, 4.0)
    return (scale[:, None] * values).astype(jnp.bfloat16)


def draw_image_group(key, part):
    key = jax.random.fold_in(key, 5)
    return jax.random.permutation(key, jnp.arange(NIMG, dtype=jnp.int32) % 3).astype(jnp.int32)


def set_ends(entries, own_key, smallest, largest):
    longest = entries.shape.index(max(entries.shape))
    spots = []
    for shift in (0, 1):
        where = [jax.random.randint(jax.random.fold_in(own_key, axis), (), 0, length) for axis, length in enumerate(entries.shape)]
        where[longest] = (where[longest] + shift) % entries.shape[longest]
        spots.append(tuple(where))
    return entries.at[spots[0]].set(smallest).at[spots[1]].set(largest)


def shard_levels(own_key, dims, shards, least, largest):
    level = 1.0
    for axis_at, parts in shards:
        steps = jax.random.uniform(jax.random.fold_in(jax.random.fold_in(own_key, 6), axis_at), (parts,), jnp.float32, least / len(shards), largest / len(shards))
        level = level * jnp.repeat(jnp.exp(steps), dims[axis_at] // parts).reshape((-1,) + (1,) * (len(dims) - 1 - axis_at))
    return level


def noise(stream_key, dims, width, most, pieces=(), kind=jnp.bfloat16):
    entries = width * jax.random.normal(stream_key, dims, jnp.float32)
    if pieces:
        entries = entries * shard_levels(stream_key, dims, pieces, -0.22, 0.18)
    return jnp.clip(entries, -most, most).astype(kind)


def setup_inputs(seed: int = 0) -> dict:
    key_list = jax.random.split(jax.random.key(seed), 11)
    return {
        "features": draw_features(jax.random.fold_in(key_list[10], 71), 0),
        "image_group": draw_image_group(jax.random.fold_in(key_list[10], 71), 0),
        "switches": set_ends(jax.random.randint(key_list[2], (WINDOWS,), 0, 4), jax.random.fold_in(key_list[2], 1), 0, 3).astype(jnp.int32),
        "enc_weight": noise(key_list[3], (3, 9, C, C), (9 * C) ** -0.5, 0.09375, ((2, 8), (3, 4))),
        "dec_weight": noise(key_list[4], (3, 9, C, C), (9 * C) ** -0.5, 0.09375, ((2, 8), (3, 4))),
        "enc_gain": jnp.clip(1.0 + 0.15 * jax.random.normal(key_list[5], (3, C), jnp.float32), 0.25, 1.75),
        "enc_bias": noise(key_list[6], (3, C), 0.5, 2.0, ((1, 4),), jnp.float32),
        "dec_gain": jnp.clip(1.0 + 0.15 * jax.random.normal(key_list[7], (3, C), jnp.float32), 0.25, 1.75),
        "dec_bias": noise(key_list[8], (3, C), 0.5, 2.0, ((1, 4),), jnp.float32),
        "d_decoded": noise(key_list[9], (PIX, C), 1.0, 6.0, ((0, 8), (1, 4))),
    }


@jax.custom_vjp
def low(v):
    return lax.optimization_barrier(v.astype(jnp.bfloat16)).astype(jnp.float32)

@jax.custom_vjp
def low_back(v):
    return v

def low_keep(v):
    return (low(v), None)

def low_pass(kept, grad):
    return (grad,)

def back_keep(v):
    return (v, None)

def back_low(kept, grad):
    return (low(grad),)
low.defvjp(low_keep, low_pass)
low_back.defvjp(back_keep, back_low)
EPSILON = 1e-05

def neighbours(image_group, first_window, window_count):
    choices_table = jnp.arange(3, dtype=jnp.int32)
    selected = (image_group[:, None] == choices_table[None, :]).astype(jnp.int32)
    heights = lax.optimization_barrier(jnp.sum(selected * jnp.array([H1, H2, H3], jnp.int32)[None, :], axis=1))
    widths = lax.optimization_barrier(jnp.sum(selected * jnp.array([W1, W2, W3], jnp.int32)[None, :], axis=1))
    window_areas = heights * widths
    image_ends = jnp.cumsum(window_areas).astype(jnp.int32)
    image_starts = image_ends - window_areas
    windows = first_window + jnp.arange(window_count, dtype=jnp.int32)
    membership = ((windows[:, None] >= image_starts[None, :]) & (windows[:, None] < image_ends[None, :])).astype(jnp.int32)
    image_base = lax.optimization_barrier(jnp.sum(membership * image_starts[None, :], axis=1))
    image_height = lax.optimization_barrier(jnp.sum(membership * heights[None, :], axis=1))
    image_width = lax.optimization_barrier(jnp.sum(membership * widths[None, :], axis=1))
    local_pos = windows - image_base
    pool_row = local_pos // image_width
    pool_column = local_pos % image_width
    quarter = jnp.arange(4, dtype=jnp.int32)
    pixel_row = (2 * pool_row[:, None] + quarter[None, :] // 2).reshape(-1)
    pixel_column = (2 * pool_column[:, None] + quarter[None, :] % 2).reshape(-1)
    pixel_height = jnp.repeat(2 * image_height, 4)
    pixel_width = jnp.repeat(2 * image_width, 4)
    pixel_base = jnp.repeat(image_base, 4)
    tap_list = []
    for row_step in (-1, 0, 1):
        for column_step in (-1, 0, 1):
            next_row = pixel_row + row_step
            next_column = pixel_column + column_step
            inside = (next_row >= 0) & (next_row < pixel_height) & (next_column >= 0) & (next_column < pixel_width)
            target = 4 * (pixel_base + next_row // 2 * (pixel_width // 2) + next_column // 2) + 2 * (next_row % 2) + next_column % 2
            tap_list.append(jnp.where(inside, target, -1).astype(jnp.int32))
    return jnp.stack(tap_list)

def convolve(field, kernels, tap_index):
    total = jnp.zeros((field.shape[0], kernels.shape[2]), jnp.float32)
    for tap_number in range(9):
        product = jnp.dot(field, kernels[tap_number], precision=lax.Precision.HIGHEST)
        total = total + jnp.take(product, tap_index[tap_number], axis=0, mode='fill', fill_value=0.0)
    return total

def norm_silu(conv_out, gain, shift_bias):
    average = lax.optimization_barrier(jnp.mean(conv_out, axis=0))
    spread_sq = lax.optimization_barrier(jnp.mean(conv_out * conv_out, axis=0)) - average * average
    normed = (conv_out - average) * lax.rsqrt(spread_sq + EPSILON)
    return jax.nn.silu(gain * normed + shift_bias)

def reference(features, image_group, switches, enc_weight, dec_weight, enc_gain, enc_bias, dec_gain, dec_bias, d_decoded):
    raw_index = neighbours(image_group, jnp.int32(0), WINDOWS)
    tap_index = jnp.where(raw_index < 0, PIX, raw_index).astype(jnp.int32)
    hits = (switches[:, None] == jnp.arange(4, dtype=jnp.int32)[None, :]).astype(jnp.float32)

    def forward(feat, enc_kernels, dec_kernels, enc_gains, enc_shifts, dec_gains, dec_shifts):
        field = low(feat)
        for layer_number in range(3):
            conv_out = low_back(convolve(field, enc_kernels[layer_number], tap_index))
            activation = norm_silu(conv_out, enc_gains[layer_number], enc_shifts[layer_number])
            field = low(activation) if layer_number < 2 else activation
        blocks = field.reshape(WINDOWS, 4, -1)
        pooled = jnp.log(lax.optimization_barrier(jnp.mean(jnp.exp(blocks), axis=1)))
        field = low((pooled[:, None, :] * hits[:, :, None]).reshape(PIX, -1))
        for layer_number in range(3):
            conv_out = low_back(convolve(field, dec_kernels[layer_number], tap_index))
            activation = norm_silu(conv_out, dec_gains[layer_number], dec_shifts[layer_number])
            field = low(activation) if layer_number < 2 else activation
        return field
    primals = (features.astype(jnp.float32), enc_weight.astype(jnp.float32), dec_weight.astype(jnp.float32), enc_gain, enc_bias, dec_gain, dec_bias)
    decoded, pullback = jax.vjp(forward, *primals)
    grads = pullback(d_decoded.astype(jnp.float32))
    return (decoded.astype(jnp.bfloat16), grads[0].astype(jnp.bfloat16), grads[1], grads[2], grads[3], grads[4], grads[5], grads[6])
```

```python
import functools

import jax
import jax.numpy as jnp
from jax import lax
from jax.experimental import pallas as pl
from jax.experimental.pallas import tpu as pltpu
from jax.sharding import PartitionSpec as P

SIZES = ((15, 20), (18, 24), (30, 40))
WIDTHS = tuple(w for _, w in SIZES)
EDGE = 48
EPSILON = 1e-05
MESH = pl.DeviceIdType.MESH
F32 = jnp.float32
BF16 = jnp.bfloat16
LANE = 128
(M_W0, M_W1, M_UP, M_DOWN, M_LEFT, M_RIGHT, M_VALID) = range(7)


def ceil_to(value, step):
    return -(-value // step) * step


def window_masks(image_group, first_window, count, padded):
    chosen = (image_group[:, None] == jnp.arange(3, dtype=jnp.int32)[None, :]).astype(jnp.int32)
    heights = jnp.sum(chosen * jnp.array([h for h, _ in SIZES], jnp.int32)[None, :], axis=1)
    widths = jnp.sum(chosen * jnp.array(WIDTHS, jnp.int32)[None, :], axis=1)
    areas = heights * widths
    ends = jnp.cumsum(areas)
    starts = ends - areas
    local = jnp.arange(padded + 2 * EDGE, dtype=jnp.int32) - EDGE
    windows = local + first_window
    member = ((windows[:, None] >= starts[None, :]) & (windows[:, None] < ends[None, :])).astype(jnp.int32)
    base = jnp.sum(member * starts[None, :], axis=1)
    height = jnp.sum(member * heights[None, :], axis=1)
    width = jnp.sum(member * widths[None, :], axis=1)
    inside = width > 0
    position = windows - base
    safe = jnp.maximum(width, 1)
    row = position // safe
    column = position - row * safe
    masks = [
        width == WIDTHS[0],
        width == WIDTHS[1],
        inside & (row > 0),
        inside & (row < height - 1),
        inside & (column > 0),
        inside & (column < width - 1),
        (local >= 0) & (local < count),
    ]
    table = jnp.stack([m.astype(F32) for m in masks], axis=1)
    return jnp.pad(table, ((0, 0), (0, LANE - len(masks))))


def to_planes(stream, count, padded):
    planes = jnp.transpose(stream.reshape(count, 4, stream.shape[1]), (1, 0, 2))
    return jnp.pad(planes, ((0, 0), (0, padded - count), (0, 0)))


def to_stream(planes, count):
    return jnp.transpose(planes[:, :count], (1, 0, 2)).reshape(4 * count, planes.shape[2])


def mask_of(mask_ref, which, low, count):
    return mask_ref[low : low + count, which : which + 1] > 0.5


def by_width(mask_ref, low, count, shifted):
    return jnp.where(
        mask_of(mask_ref, M_W0, low, count),
        shifted(WIDTHS[0]),
        jnp.where(mask_of(mask_ref, M_W1, low, count), shifted(WIDTHS[1]), shifted(WIDTHS[2])),
    )


def row_peers(rows):
    here = lax.axis_index("rows")
    there = lax.axis_index("grp")
    return [(lax.rem(here + k, rows), there) for k in range(1, rows)]


def grp_peers():
    here = lax.axis_index("rows")
    mine = lax.axis_index("grp")
    half, core = mine // 2, lax.rem(mine, 2)
    return (here, half * 2 + 1 - core), (here, (1 - half) * 2 + core)


def greet(peers):
    barrier = pltpu.get_barrier_semaphore()
    for peer in peers:
        pl.semaphore_signal(barrier, inc=1, device_id=peer, device_id_type=MESH)
    pl.semaphore_wait(barrier, len(peers))


def remote(src, dst, send, recv, peer):
    return pltpu.make_async_remote_copy(
        src_ref=src, dst_ref=dst, send_sem=send, recv_sem=recv, device_id=peer, device_id_type=MESH
    )


def exchange_sums(rows, own, buf, send, recv):
    peers = row_peers(rows)
    buf[0] = own
    copies = []
    for k, peer in enumerate(peers):
        copy = remote(buf.at[0], buf.at[k + 1], send.at[k], recv.at[k], peer)
        copy.start()
        copies.append(copy)
    for copy in copies:
        copy.wait()
    total = buf[0]
    for k in range(1, rows):
        total = total + buf[k]
    return total


def row_parts(padded, count):
    tail = (count - EDGE) // 16 * 16
    parts = [(0, EDGE), (tail, padded - tail)]
    inner = tail - EDGE
    start = EDGE
    steps = 3
    for k in range(steps):
        size = ceil_to(-(-(tail - start) // (steps - k)), 16)
        size = min(size, tail - start)
        parts.append((start, size))
        start += size
    return parts


def forward_kernel(
    rows, count, padded, pixels,
    v_ref, w_ref, gb_ref, mask_ref,
    next_ref, z_ref, stat_ref, full_ref,
    vbuf, yext, over, under, to_next, to_prev, from_prev, from_next, sums,
    core_s, core_r, x_s, x_r, fwd_s, fwd_r, halo_s, halo_r, sum_s, sum_r, out_sem,
):
    mine = lax.axis_index("grp")
    here = lax.axis_index("rows")
    half = mine // 2
    partner, across = grp_peers()
    greet([partner, across] + row_peers(rows))
    parts = row_parts(padded, count)

    own_lanes = pl.ds(pl.multiple_of(mine * LANE, LANE), LANE)
    far_lanes = pl.ds(pl.multiple_of(across[1] * LANE, LANE), LANE)
    x_copies = []
    for k, (low, size) in enumerate(parts):
        piece = pl.ds(low, size)
        copy = remote(
            v_ref.at[:, piece, :], vbuf.at[:, piece, own_lanes], x_s.at[k], x_r.at[k], across
        )
        copy.start()
        x_copies.append(copy)
    core_copy = remote(v_ref, vbuf.at[:, :, own_lanes], core_s, core_r, partner)
    core_copy.start()
    vbuf[:, :, own_lanes] = v_ref[...]
    yext[EDGE + padded :, :] = jnp.zeros((EDGE, yext.shape[1]), F32)
    core_copy.wait_recv()

    def add_products(low, size, base, touched):
        for q in range(4):
            a, b = q // 2, q % 2
            left = vbuf[q, low : low + size, pl.ds(base, 2 * LANE)]
            for step in range(3):
                right = w_ref[pl.ds(base, 2 * LANE), step * 3 * LANE : (step + 1) * 3 * LANE]
                product = jnp.dot(left, right, preferred_element_type=F32)
                for column in range(3):
                    spot = (a + step) * 4 + b + column
                    block = product[:, column * LANE : (column + 1) * LANE]
                    where = (slice(EDGE + low, EDGE + low + size), slice(spot * LANE, (spot + 1) * LANE))
                    if spot in touched:
                        yext[where] += block
                    else:
                        yext[where] = block
                        touched.add(spot)

    own_base = pl.multiple_of(half * 2 * LANE, 2 * LANE)
    far_base = pl.multiple_of((1 - half) * 2 * LANE, 2 * LANE)
    add_products(0, padded, own_base, set())

    full = set(range(16))
    forwards = []
    for k, (low, size) in enumerate(parts):
        piece = pl.ds(low, size)
        x_copies[k].wait_recv()
        far = vbuf.at[:, piece, far_lanes]
        copy = remote(far, far, fwd_s.at[k], fwd_r.at[k], partner)
        copy.start()
        forwards.append(copy)
    halos = []
    for k, (low, size) in enumerate(parts):
        forwards[k].wait_recv()
        add_products(low, size, far_base, full)
        if k == 1:
            last = EDGE + count - EDGE
            to_next[:, : 4 * LANE] = yext[last : last + EDGE, 12 * LANE :]
            to_next[:, 4 * LANE : 5 * LANE] = yext[last : last + EDGE, 7 * LANE : 8 * LANE]
            to_next[:, 5 * LANE :] = yext[last : last + EDGE, 11 * LANE : 12 * LANE]
            to_prev[:, : 4 * LANE] = yext[EDGE : 2 * EDGE, : 4 * LANE]
            to_prev[:, 4 * LANE : 5 * LANE] = yext[EDGE : 2 * EDGE, 4 * LANE : 5 * LANE]
            to_prev[:, 5 * LANE :] = yext[EDGE : 2 * EDGE, 8 * LANE : 9 * LANE]
            after = (lax.rem(here + 1, rows), mine)
            before = (lax.rem(here + rows - 1, rows), mine)
            halos = [
                remote(to_next, from_prev, halo_s.at[0], halo_r.at[0], after),
                remote(to_prev, from_next, halo_s.at[1], halo_r.at[1], before),
            ]
            for copy in halos:
                copy.start()
    out_copy = pltpu.make_async_copy(vbuf, full_ref, out_sem)
    out_copy.start()
    for copy in halos:
        copy.wait_recv()
    yext[:EDGE, 12 * LANE :] = from_prev[:, : 4 * LANE]
    yext[:EDGE, 7 * LANE : 8 * LANE] = from_prev[:, 4 * LANE : 5 * LANE]
    yext[:EDGE, 11 * LANE : 12 * LANE] = from_prev[:, 5 * LANE :]
    after_own = slice(EDGE + count, 2 * EDGE + count)
    yext[after_own, : 4 * LANE] = from_next[:, : 4 * LANE]
    yext[after_own, 4 * LANE : 5 * LANE] = from_next[:, 4 * LANE : 5 * LANE]
    yext[after_own, 8 * LANE : 9 * LANE] = from_next[:, 5 * LANE :]

    def at(low, size, spot):
        return yext[low : low + size, spot * LANE : (spot + 1) * LANE]

    low, size = 8, padded + 2 * EDGE - 16
    go_left = mask_of(mask_ref, M_LEFT, low, size)
    go_right = mask_of(mask_ref, M_RIGHT, low, size)
    for kept, first in ((over, 12), (under, 0)):
        kept[low : low + size, :LANE] = at(low, size, first + 1) + jnp.where(
            go_left, at(low - 1, size, first + 3), 0.0
        )
        kept[low : low + size, LANE:] = at(low, size, first + 2) + jnp.where(
            go_right, at(low + 1, size, first), 0.0
        )
    go_left = mask_of(mask_ref, M_LEFT, EDGE, padded)
    go_right = mask_of(mask_ref, M_RIGHT, EDGE, padded)
    valid = mask_of(mask_ref, M_VALID, EDGE, padded)
    total = jnp.zeros((1, LANE), F32)
    squares = jnp.zeros((1, LANE), F32)
    for q in range(4):
        a, b = q // 2, q % 2
        lanes = slice(b * LANE, (b + 1) * LANE)
        kept, sign = (over, -1) if a == 0 else (under, 1)
        rowwise = by_width(
            mask_ref, EDGE, padded,
            lambda w: kept[EDGE + sign * w : EDGE + sign * w + padded, lanes],
        )
        z = at(EDGE, padded, (a + 1) * 4 + b + 1)
        z = z + jnp.where(mask_of(mask_ref, (M_UP, M_DOWN)[a], EDGE, padded), rowwise, 0.0)
        if b == 0:
            z = z + jnp.where(go_left, at(EDGE - 1, padded, (a + 1) * 4 + 3), 0.0)
        else:
            z = z + jnp.where(go_right, at(EDGE + 1, padded, (a + 1) * 4), 0.0)
        z = jnp.where(valid, z, 0.0)
        z_ref[q] = z
        total = total + jnp.sum(z, axis=0, keepdims=True)
        squares = squares + jnp.sum(z * z, axis=0, keepdims=True)
    both = exchange_sums(
        rows, jnp.concatenate([total, squares, jnp.zeros((6, LANE), F32)], axis=0), sums, sum_s, sum_r
    )
    mean = both[0:1] / pixels
    inverse = lax.rsqrt(both[1:2] / pixels - mean * mean + EPSILON)
    stat_ref[...] = jnp.concatenate([mean, inverse, jnp.zeros((6, LANE), F32)], axis=0)
    for q in range(4):
        y = gb_ref[0:1] * ((z_ref[q] - mean) * inverse) + gb_ref[1:2]
        next_ref[q] = jnp.where(valid, y * jax.nn.sigmoid(y), 0.0).astype(BF16)
    core_copy.wait_send()
    for copy in x_copies + forwards + halos:
        copy.wait_send()
    out_copy.wait()


def backward_kernel(
    rows, count, padded, pixels,
    g_ref, z_ref, stat_ref, gb_ref, mask_ref, full_ref, w_ref,
    grad_ref, wgrad_ref, gbgrad_ref,
    gy, gext, above, below, patch, part, keep, core_out, core_in, x_out, x_in,
    to_next, to_prev, from_prev, from_next, sums,
    core_s, core_r, x_s, x_r, halo_s, halo_r, sum_s, sum_r,
):
    mine = lax.axis_index("grp")
    here = lax.axis_index("rows")
    half, core = mine // 2, lax.rem(mine, 2)
    partner, across = grp_peers()
    greet([partner, across] + row_peers(rows))
    mean, inverse = stat_ref[0:1], stat_ref[1:2]
    gain, shift = gb_ref[0:1], gb_ref[1:2]
    valid = mask_of(mask_ref, M_VALID, EDGE, padded)

    shift_sum = jnp.zeros((1, LANE), F32)
    gain_sum = jnp.zeros((1, LANE), F32)
    for q in range(4):
        normed = (z_ref[q] - mean) * inverse
        y = gain * normed + shift
        s = jax.nn.sigmoid(y)
        grad = g_ref[q] * s * (1.0 + y * (1.0 - s))
        grad = jnp.where(valid, grad, 0.0)
        gy[q] = grad
        shift_sum = shift_sum + jnp.sum(grad, axis=0, keepdims=True)
        gain_sum = gain_sum + jnp.sum(grad * normed, axis=0, keepdims=True)
    both = exchange_sums(
        rows, jnp.concatenate([shift_sum, gain_sum, jnp.zeros((6, LANE), F32)], axis=0), sums, sum_s, sum_r
    )
    gbgrad_ref[...] = both
    gext[EDGE + padded :, :] = jnp.zeros((EDGE, 4 * LANE), F32)
    for q in range(4):
        normed = (z_ref[q] - mean) * inverse
        gz = inverse * gain * (gy[q] - both[0:1] / pixels - normed * both[1:2] / pixels)
        gz = jnp.where(valid, gz, 0.0).astype(BF16).astype(F32)
        gext[EDGE : EDGE + padded, q * LANE : (q + 1) * LANE] = gz
    to_next[...] = gext[count : count + EDGE, :].astype(BF16)
    to_prev[...] = gext[EDGE : 2 * EDGE, :].astype(BF16)
    after = (lax.rem(here + 1, rows), mine)
    before = (lax.rem(here + rows - 1, rows), mine)
    halos = [
        remote(to_next, from_prev, halo_s.at[0], halo_r.at[0], after),
        remote(to_prev, from_next, halo_s.at[1], halo_r.at[1], before),
    ]
    for copy in halos:
        copy.start()
    for copy in halos:
        copy.wait()
    gext[:EDGE, :] = from_prev[...].astype(F32)
    gext[EDGE + count : 2 * EDGE + count, :] = from_next[...].astype(F32)

    low, size = EDGE - 8, padded + 16
    for kept, which, sign, lanes in (
        (above, M_UP, -1, slice(2 * LANE, 4 * LANE)),
        (below, M_DOWN, 1, slice(0, 2 * LANE)),
    ):
        rowwise = by_width(
            mask_ref, low, size, lambda w: gext[low + sign * w : low + sign * w + size, lanes]
        )
        kept[...] = jnp.where(mask_of(mask_ref, which, low, size), rowwise, 0.0)
    go_left = mask_of(mask_ref, M_LEFT, EDGE, padded)
    go_right = mask_of(mask_ref, M_RIGHT, EDGE, padded)
    for step, (kept, top, lane) in enumerate(
        ((above, 8, 0), (gext, EDGE, 0), (gext, EDGE, 2 * LANE), (below, 8, 0))
    ):
        even, odd = slice(lane, lane + LANE), slice(lane + LANE, lane + 2 * LANE)
        blocks = [
            jnp.where(go_left, kept[top - 1 : top - 1 + padded, odd], 0.0),
            kept[top : top + padded, even],
            kept[top : top + padded, odd],
            jnp.where(go_right, kept[top + 1 : top + 1 + padded, even], 0.0),
        ]
        for column, block in enumerate(blocks):
            spot = step * 4 + column
            patch[:, spot * LANE : (spot + 1) * LANE] = block.astype(BF16)

    def taps(q, step):
        a, b = q // 2, q % 2
        first = (a + step) * 4 + b
        return patch[:, first * LANE : (first + 3) * LANE]

    def input_grad(q, base):
        total = None
        for step in range(3):
            right = w_ref[pl.ds(base, 2 * LANE), step * 3 * LANE : (step + 1) * 3 * LANE]
            product = lax.dot_general(
                taps(q, step), right, (((1,), (1,)), ((), ())), preferred_element_type=F32
            )
            total = product if total is None else total + product
        part[...] = total

    own_lanes = pl.ds(pl.multiple_of(core * LANE, LANE), LANE)
    other_lanes = pl.ds(pl.multiple_of((1 - core) * LANE, LANE), LANE)
    own_base = pl.multiple_of(half * 2 * LANE, 2 * LANE)
    far_base = pl.multiple_of((1 - half) * 2 * LANE, 2 * LANE)
    core_copies, x_copies = [], []

    def send_across(q):
        core_copies[q].wait_recv()
        x_out[q] = (keep[q] + core_in[q].astype(F32)).astype(BF16)
        copy = remote(x_out.at[q], x_in.at[q], x_s.at[q], x_r.at[q], across)
        copy.start()
        x_copies.append(copy)

    for turn, base in enumerate((far_base, own_base)):
        for q in range(4):
            spot = turn * 4 + q
            input_grad(q, base)
            core_out[spot] = part[:, other_lanes].astype(BF16)
            keep[spot] = part[:, own_lanes]
            copy = remote(
                core_out.at[spot], core_in.at[spot], core_s.at[spot], core_r.at[spot], partner
            )
            copy.start()
            core_copies.append(copy)
            if turn == 0 and q > 0:
                send_across(q - 1)
        if turn == 0:
            send_across(3)

    for step in range(3):
        total = None
        for q in range(4):
            product = lax.dot_general(
                full_ref[q], taps(q, step), (((0,), (0,)), ((), ())), preferred_element_type=F32
            )
            total = product if total is None else total + product
        wgrad_ref[:, step * 3 * LANE : (step + 1) * 3 * LANE] = total.astype(BF16)

    for q in range(4):
        core_copies[4 + q].wait_recv()
        x_copies[q].wait_recv()
        grad_ref[q] = keep[4 + q] + core_in[4 + q].astype(F32) + x_in[q].astype(F32)
    for copy in core_copies + x_copies:
        copy.wait_send()


VM = pl.BlockSpec(memory_space=pltpu.VMEM)
HBM = pl.BlockSpec(memory_space=pl.ANY)
LIMIT = 56 * 1024 * 1024


def forward_layer(rows, count, padded, pixels, planes, weight, gain_shift, masks):
    channels = weight.shape[0]
    ext = padded + 2 * EDGE
    n_parts = len(row_parts(padded, count))
    dma = pltpu.SemaphoreType.DMA
    return pl.pallas_call(
        functools.partial(forward_kernel, rows, count, padded, pixels),
        name="layer_forward",
        out_shape=(
            jax.ShapeDtypeStruct((4, padded, LANE), BF16),
            jax.ShapeDtypeStruct((4, padded, LANE), F32),
            jax.ShapeDtypeStruct((8, LANE), F32),
            jax.ShapeDtypeStruct((4, padded, channels), BF16),
        ),
        in_specs=[VM] * 4,
        out_specs=(VM, VM, VM, HBM),
        scratch_shapes=[
            pltpu.VMEM((4, padded, channels), BF16),
            pltpu.VMEM((ext, 16 * LANE), F32),
            pltpu.VMEM((ext, 2 * LANE), F32),
            pltpu.VMEM((ext, 2 * LANE), F32),
        ]
        + [pltpu.VMEM((EDGE, 6 * LANE), F32)] * 4
        + [pltpu.VMEM((rows, 8, LANE), F32)]
        + [dma, dma]
        + [dma((n_parts,))] * 4
        + [dma((2,))] * 2
        + [dma((rows - 1,))] * 2
        + [dma],
        compiler_params=pltpu.CompilerParams(
            collective_id=0, has_side_effects=True, vmem_limit_bytes=LIMIT
        ),
        cost_estimate=pl.CostEstimate(
            flops=2 * 36 * padded * channels * LANE, bytes_accessed=8 * 2**20, transcendentals=0
        ),
    )(planes, weight, gain_shift, masks)


def backward_layer(rows, count, padded, pixels, grad, z, stat, gain_shift, masks, full, weight):
    channels = weight.shape[0]
    ext = padded + 2 * EDGE
    dma = pltpu.SemaphoreType.DMA
    return pl.pallas_call(
        functools.partial(backward_kernel, rows, count, padded, pixels),
        name="layer_backward",
        out_shape=(
            jax.ShapeDtypeStruct((4, padded, LANE), F32),
            jax.ShapeDtypeStruct((channels, 9 * LANE), BF16),
            jax.ShapeDtypeStruct((8, LANE), F32),
        ),
        in_specs=[VM] * 7,
        out_specs=(VM, VM, VM),
        scratch_shapes=[
            pltpu.VMEM((4, padded, LANE), F32),
            pltpu.VMEM((ext, 4 * LANE), F32),
            pltpu.VMEM((padded + 16, 2 * LANE), F32),
            pltpu.VMEM((padded + 16, 2 * LANE), F32),
            pltpu.VMEM((padded, 16 * LANE), BF16),
            pltpu.VMEM((padded, 2 * LANE), F32),
            pltpu.VMEM((8, padded, LANE), F32),
            pltpu.VMEM((8, padded, LANE), BF16),
            pltpu.VMEM((8, padded, LANE), BF16),
            pltpu.VMEM((4, padded, LANE), BF16),
            pltpu.VMEM((4, padded, LANE), BF16),
        ]
        + [pltpu.VMEM((EDGE, 4 * LANE), BF16)] * 4
        + [pltpu.VMEM((rows, 8, LANE), F32)]
        + [dma((8,))] * 2
        + [dma((4,))] * 2
        + [dma((2,))] * 2
        + [dma((rows - 1,))] * 2,
        compiler_params=pltpu.CompilerParams(
            collective_id=1, has_side_effects=True, vmem_limit_bytes=LIMIT
        ),
        cost_estimate=pl.CostEstimate(
            flops=4 * 36 * padded * channels * LANE, bytes_accessed=8 * 2**20, transcendentals=0
        ),
    )(grad, z, stat, gain_shift, masks, full, weight)


def shards(
    features, image_group, switches, enc_weight, dec_weight,
    enc_gain, enc_bias, dec_gain, dec_bias, d_decoded,
):
    rows = lax.axis_size("rows")
    count = features.shape[0] // 4
    padded = ceil_to(count, 16)
    pixels = float(features.shape[0] * rows)
    masks = window_masks(image_group, lax.axis_index("rows") * count, count, padded)

    def whole_weight(weight):
        flat = jnp.transpose(weight[::-1], (1, 0, 2)).reshape(weight.shape[1], -1)
        return lax.all_gather(flat, "rows", axis=0, tiled=True)

    def pair(gain, shift):
        return jnp.pad(jnp.stack([gain, shift]), ((0, 6), (0, 0)))

    weights = [whole_weight(w[l]) for w in (enc_weight, dec_weight) for l in range(3)]
    pairs = [pair(g[l], s[l]) for g, s in ((enc_gain, enc_bias), (dec_gain, dec_bias)) for l in range(3)]
    hits = switches[None, :] == jnp.arange(4, dtype=jnp.int32)[:, None]
    hits = jnp.pad(hits.astype(F32), ((0, 0), (0, padded - count)))[:, :, None]

    saved = []
    planes = to_planes(features, count, padded)
    pooled = blocks = None
    for layer in range(6):
        planes, z, stat, full = forward_layer(
            rows, count, padded, pixels, planes, weights[layer], pairs[layer], masks
        )
        saved.append((z, stat, full))
        if layer == 2:
            y = pairs[2][0] * ((z - stat[0]) * stat[1]) + pairs[2][1]
            blocks = jax.nn.silu(y)
            pooled = jnp.log(jnp.mean(jnp.exp(blocks), axis=0))
            planes = (pooled[None] * hits).astype(BF16)
    decoded = to_stream(planes, count)

    grad = to_planes(d_decoded, count, padded).astype(F32)
    weight_grads, pair_grads = [None] * 6, [None] * 6
    for layer in range(5, -1, -1):
        z, stat, full = saved[layer]
        grad, weight_grad, pair_grads[layer] = backward_layer(
            rows, count, padded, pixels, grad, z, stat, pairs[layer], masks, full, weights[layer]
        )
        mine = lax.psum_scatter(weight_grad, "rows", scatter_dimension=0, tiled=True).astype(F32)
        mine = jnp.transpose(mine.reshape(mine.shape[0], 9, -1)[:, ::-1], (1, 0, 2))
        weight_grads[layer] = mine
        if layer == 3:
            grad_pooled = jnp.sum(grad * hits, axis=0)
            grad = grad_pooled[None] * jnp.exp(blocks - pooled[None]) * 0.25
    return (
        decoded,
        to_stream(grad.astype(BF16), count),
        jnp.stack(weight_grads[:3]),
        jnp.stack(weight_grads[3:]),
        jnp.stack([p[1] for p in pair_grads[:3]]),
        jnp.stack([p[0] for p in pair_grads[:3]]),
        jnp.stack([p[1] for p in pair_grads[3:]]),
        jnp.stack([p[0] for p in pair_grads[3:]]),
    )


def solution(mesh):
    wide = P("rows", "grp")
    kernels = P(None, None, "rows", "grp")
    vector = P(None, "grp")
    return jax.shard_map(
        shards,
        mesh=mesh,
        in_specs=(wide, P(), P("rows"), kernels, kernels, vector, vector, vector, vector, wide),
        out_specs=(wide, wide, kernels, kernels, vector, vector, vector, vector),
        check_vma=False,
    )
```

```python
import functools

import jax
import jax.numpy as jnp
from jax import lax
from jax.experimental import pallas as pl
from jax.experimental.pallas import tpu as pltpu
from jax.sharding import PartitionSpec as P

SIZES = ((15, 20), (18, 24), (30, 40))
WIDTHS = tuple(w for _, w in SIZES)
EDGE = 48
EPSILON = 1e-05
MESH = pl.DeviceIdType.MESH
F32 = jnp.float32
BF16 = jnp.bfloat16
LANE = 128
(M_W0, M_W1, M_UP, M_DOWN, M_LEFT, M_RIGHT, M_VALID) = range(7)


def ceil_to(value, step):
    return -(-value // step) * step


def window_masks(image_group, first_window, count, padded):
    chosen = (image_group[:, None] == jnp.arange(3, dtype=jnp.int32)[None, :]).astype(jnp.int32)
    heights = jnp.sum(chosen * jnp.array([h for h, _ in SIZES], jnp.int32)[None, :], axis=1)
    widths = jnp.sum(chosen * jnp.array(WIDTHS, jnp.int32)[None, :], axis=1)
    areas = heights * widths
    ends = jnp.cumsum(areas)
    starts = ends - areas
    local = jnp.arange(padded + 2 * EDGE, dtype=jnp.int32) - EDGE
    windows = local + first_window
    member = ((windows[:, None] >= starts[None, :]) & (windows[:, None] < ends[None, :])).astype(jnp.int32)
    base = jnp.sum(member * starts[None, :], axis=1)
    height = jnp.sum(member * heights[None, :], axis=1)
    width = jnp.sum(member * widths[None, :], axis=1)
    inside = width > 0
    position = windows - base
    safe = jnp.maximum(width, 1)
    row = position // safe
    column = position - row * safe
    masks = [
        width == WIDTHS[0],
        width == WIDTHS[1],
        inside & (row > 0),
        inside & (row < height - 1),
        inside & (column > 0),
        inside & (column < width - 1),
        (local >= 0) & (local < count),
    ]
    table = jnp.stack([m.astype(F32) for m in masks], axis=1)
    return jnp.pad(table, ((0, 0), (0, LANE - len(masks))))


def to_planes(stream, count, padded):
    planes = jnp.transpose(stream.reshape(count, 4, stream.shape[1]), (1, 0, 2))
    return jnp.pad(planes, ((0, 0), (0, padded - count), (0, 0)))


def to_stream(planes, count):
    return jnp.transpose(planes[:, :count], (1, 0, 2)).reshape(4 * count, planes.shape[2])


def mask_of(mask_ref, which, low, count):
    return mask_ref[low : low + count, which : which + 1] > 0.5


def by_width(mask_ref, low, count, shifted):
    return jnp.where(
        mask_of(mask_ref, M_W0, low, count),
        shifted(WIDTHS[0]),
        jnp.where(mask_of(mask_ref, M_W1, low, count), shifted(WIDTHS[1]), shifted(WIDTHS[2])),
    )


def row_peers(rows):
    here = lax.axis_index("rows")
    there = lax.axis_index("grp")
    return [(lax.rem(here + k, rows), there) for k in range(1, rows)]


def grp_peers():
    here = lax.axis_index("rows")
    mine = lax.axis_index("grp")
    half, core = mine // 2, lax.rem(mine, 2)
    return (here, half * 2 + 1 - core), (here, (1 - half) * 2 + core)


def greet(peers):
    barrier = pltpu.get_barrier_semaphore()
    for peer in peers:
        pl.semaphore_signal(barrier, inc=1, device_id=peer, device_id_type=MESH)
    pl.semaphore_wait(barrier, len(peers))


def remote(src, dst, send, recv, peer):
    return pltpu.make_async_remote_copy(
        src_ref=src, dst_ref=dst, send_sem=send, recv_sem=recv, device_id=peer, device_id_type=MESH
    )


def exchange_sums(rows, own, buf, send, recv):
    buf[0] = own
    copies = []
    for k, peer in enumerate(row_peers(rows)):
        copy = remote(buf.at[0], buf.at[k + 1], send.at[k], recv.at[k], peer)
        copy.start()
        copies.append(copy)
    for copy in copies:
        copy.wait()
    total = buf[0]
    for k in range(1, rows):
        total = total + buf[k]
    return total


def row_parts(padded, count):
    tail = (count - EDGE) // 16 * 16
    parts = [(0, EDGE), (tail, padded - tail)]
    start, steps = EDGE, 3
    for k in range(steps):
        size = min(ceil_to(-(-(tail - start) // (steps - k)), 16), tail - start)
        parts.append((start, size))
        start += size
    return parts


def lanes_of(block):
    return pl.ds(pl.multiple_of(block * LANE, LANE), LANE)


class Gather:
    def __init__(self, rows, shard, buf, send, recv, pass_send, pass_recv):
        self.shard, self.buf = shard, buf
        self.far = rows // 2
        here, there = lax.axis_index("rows"), lax.axis_index("grp")
        self.high, self.low = here // 2, lax.rem(here, 2)
        self.there = there
        self.send, self.recv, self.pass_send, self.pass_recv = send, recv, pass_send, pass_recv

    def rows_of(self, step, low):
        block = lax.rem(self.high + step, self.far) * 2 + low
        return pl.ds(pl.multiple_of(block * self.shard, 16), self.shard)

    def spread(self, layer, step):
        own = self.buf.at[layer, self.rows_of(0, self.low), :]
        peer = (lax.rem(self.high + step, self.far) * 2 + self.low, self.there)
        k = step - 1
        return remote(own, own, self.send.at[layer, k], self.recv.at[layer, k], peer)

    def across(self, layer, step):
        piece = self.buf.at[layer, self.rows_of(self.far - step, self.low), :]
        peer = (self.high * 2 + 1 - self.low, self.there)
        return remote(piece, piece, self.pass_send.at[layer, step], self.pass_recv.at[layer, step], peer)

    def start(self, layer, own):
        self.buf[layer, self.rows_of(0, self.low), :] = own
        for step in range(1, self.far):
            self.spread(layer, step).start()
        self.across(layer, 0).start()

    def forward(self, layer, step):
        self.spread(layer, step).wait_recv()
        self.across(layer, step).start()

    def wait(self, layer):
        for step in range(self.far):
            self.across(layer, step).wait_recv()

    def drain(self, layer):
        for step in range(1, self.far):
            self.spread(layer, step).wait_send()
        for step in range(self.far):
            self.across(layer, step).wait_send()


class Scatter:
    def __init__(self, rows, shard, grads, first, second, third, out, send, recv, far_send, far_recv):
        self.shard, self.grads, self.first, self.second, self.third = shard, grads, first, second, third
        self.out, self.far = out, rows // 2
        here, self.there = lax.axis_index("rows"), lax.axis_index("grp")
        self.high, self.low = here // 2, lax.rem(here, 2)
        self.send, self.recv, self.far_send, self.far_recv = send, recv, far_send, far_recv

    def rows_of(self, step, low):
        block = lax.rem(self.high + step, self.far) * 2 + low
        return pl.ds(pl.multiple_of(block * self.shard, 16), self.shard)

    def across(self, slot, step):
        peer = (self.high * 2 + 1 - self.low, self.there)
        return remote(
            self.grads.at[slot, self.rows_of(step, 1 - self.low), :], self.first.at[slot, step],
            self.send.at[slot, step], self.recv.at[slot, step], peer,
        )

    def spread(self, slot, step):
        peer = (lax.rem(self.high + step, self.far) * 2 + self.low, self.there)
        k = step - 1
        return remote(
            self.second.at[slot, k], self.third.at[slot, k],
            self.far_send.at[slot, k], self.far_recv.at[slot, k], peer,
        )

    def order(self):
        return list(range(1, self.far)) + [0]

    def start(self, slot):
        for step in self.order():
            self.across(slot, step).start()

    def forward(self, slot, step):
        self.across(slot, step).wait_recv()
        total = self.grads[slot, self.rows_of(step, self.low), :].astype(F32) + self.first[slot, step].astype(F32)
        if step == 0:
            self.out[slot] = total
        else:
            self.second[slot, step - 1] = total.astype(BF16)
            self.spread(slot, step).start()

    def finish(self, slot):
        total = self.out[slot]
        for step in range(1, self.far):
            self.spread(slot, step).wait_recv()
            total = total + self.third[slot, step - 1].astype(F32)
        self.out[slot] = total

    def drain(self, slot):
        for step in range(self.far):
            self.across(slot, step).wait_send()
        for step in range(1, self.far):
            self.spread(slot, step).wait_send()


def each(count, body):
    lax.fori_loop(0, count, lambda i, carry: (body(i), carry)[1], 0)


def forward_kernel(
    inside, layers, rows, count, padded, pixels,
    v_ref, w_ref, gb_ref, mask_ref,
    next_ref, stat_ref, z_out, full_out, w_out,
    vbuf, wbuf, zbuf, yext, over, under, to_next, to_prev, from_prev, from_next, sums,
    core_s, core_r, x_s, x_r, fwd_s, fwd_r, halo_s, halo_r, sum_s, sum_r, out_sem,
    w_s, w_r, wp_s, wp_r,
):
    mine, here = lax.axis_index("grp"), lax.axis_index("rows")
    half = mine // 2
    partner, across = grp_peers()
    parts = row_parts(padded, count)
    own_lanes, far_lanes = lanes_of(mine), lanes_of(across[1])
    own_base = pl.multiple_of(half * 2 * LANE, 2 * LANE)
    far_base = pl.multiple_of((1 - half) * 2 * LANE, 2 * LANE)
    gather = Gather(rows, w_ref.shape[1], wbuf, w_s, w_r, wp_s, wp_r)

    def slab(layer, k, lanes):
        low, size = parts[k]
        return vbuf.at[layer, :, pl.ds(low, size), lanes]

    def to_core(layer, k):
        piece = slab(layer, k, own_lanes)
        return remote(piece, piece, core_s.at[layer, k], core_r.at[layer, k], partner)

    def to_far(layer, k):
        piece = slab(layer, k, own_lanes)
        return remote(piece, piece, x_s.at[layer, k], x_r.at[layer, k], across)

    def pass_on(layer, k):
        piece = slab(layer, k, far_lanes)
        return remote(piece, piece, fwd_s.at[layer, k], fwd_r.at[layer, k], partner)

    def load(layer):
        return pltpu.make_async_copy(w_ref.at[layer], wbuf.at[layer], w_s.at[layer, 0])

    def saves(layer):
        pairs = [(vbuf.at[layer], full_out.at[layer]), (zbuf.at[layer], z_out.at[layer])]
        if inside:
            pairs.append((wbuf.at[layer], w_out.at[layer]))
        return [pltpu.make_async_copy(src, dst, out_sem.at[layer, k]) for k, (src, dst) in enumerate(pairs)]

    after = (lax.rem(here + 1, rows), mine)
    before = (lax.rem(here + rows - 1, rows), mine)
    down = remote(to_next, from_prev, halo_s.at[0], halo_r.at[0], after)
    up = remote(to_prev, from_next, halo_s.at[1], halo_r.at[1], before)

    def add_products(layer, low, size, base, touched):
        for q in range(4):
            a, b = q // 2, q % 2
            left = vbuf[layer, q, low : low + size, pl.ds(base, 2 * LANE)]
            for step in range(3):
                right = wbuf[layer, pl.ds(base, 2 * LANE), step * 3 * LANE : (step + 1) * 3 * LANE]
                product = jnp.dot(left, right, preferred_element_type=F32)
                for column in range(3):
                    spot = (a + step) * 4 + b + column
                    block = product[:, column * LANE : (column + 1) * LANE]
                    where = (slice(EDGE + low, EDGE + low + size), slice(spot * LANE, (spot + 1) * LANE))
                    if spot in touched:
                        yext[where] += block
                    else:
                        yext[where] = block
                        touched.add(spot)

    def at(low, size, spot):
        return yext[low : low + size, spot * LANE : (spot + 1) * LANE]

    greet([partner, across] + row_peers(rows))
    vbuf[0, :, :, own_lanes] = v_ref[...]
    for k in range(len(parts)):
        to_far(0, k).start()
        to_core(0, k).start()
    if inside:
        gather.start(0, w_ref[0])
    else:
        load(0).start()
    yext[:EDGE, :] = jnp.zeros((EDGE, yext.shape[1]), F32)
    yext[EDGE + padded :, :] = jnp.zeros((EDGE, yext.shape[1]), F32)
    if inside:
        for step in range(1, rows // 2):
            gather.forward(0, step)

    def layer_step(layer):
        more = layer + 1 < layers
        if inside:
            gather.wait(layer)
            saves(layer)[2].start()

            @pl.when(more)
            def _():
                gather.start(layer + 1, w_ref[layer + 1])
        else:
            load(layer).wait()

            @pl.when(more)
            def _():
                load(layer + 1).start()

        for k in range(len(parts)):
            to_core(layer, k).wait_recv()
        add_products(layer, 0, padded, own_base, set())

        def far_products(k):
            pass_on(layer, k).wait_recv()
            low, size = parts[k]
            add_products(layer, low, size, far_base, set(range(16)))
            if k != 1:
                return
            to_next[:, : 4 * LANE] = yext[count : count + EDGE, 12 * LANE :]
            to_next[:, 4 * LANE : 5 * LANE] = at(count, EDGE, 7)
            to_next[:, 5 * LANE :] = at(count, EDGE, 11)
            to_prev[:, : 4 * LANE] = yext[EDGE : 2 * EDGE, : 4 * LANE]
            to_prev[:, 4 * LANE : 5 * LANE] = at(EDGE, EDGE, 4)
            to_prev[:, 5 * LANE :] = at(EDGE, EDGE, 8)

            @pl.when(here + 1 < rows)
            def _():
                down.start()

            @pl.when(here > 0)
            def _():
                up.start()

        for k in range(len(parts)):
            to_far(layer, k).wait_recv()
            pass_on(layer, k).start()
            if k > 0:
                far_products(k - 1)
            step = k - (len(parts) - (rows // 2))
            if inside and step >= 1:

                @pl.when(more)
                def _():
                    gather.forward(layer + 1, step)
        far_products(len(parts) - 1)
        saves(layer)[0].start()

        @pl.when(here > 0)
        def _():
            down.wait_recv()
            up.wait_send()
            yext[:EDGE, 12 * LANE :] = from_prev[:, : 4 * LANE]
            yext[:EDGE, 7 * LANE : 8 * LANE] = from_prev[:, 4 * LANE : 5 * LANE]
            yext[:EDGE, 11 * LANE : 12 * LANE] = from_prev[:, 5 * LANE :]

        @pl.when(here + 1 < rows)
        def _():
            up.wait_recv()
            down.wait_send()
            beyond = slice(EDGE + count, 2 * EDGE + count)
            yext[beyond, : 4 * LANE] = from_next[:, : 4 * LANE]
            yext[beyond, 4 * LANE : 5 * LANE] = from_next[:, 4 * LANE : 5 * LANE]
            yext[beyond, 8 * LANE : 9 * LANE] = from_next[:, 5 * LANE :]

        low, size = 8, padded + 2 * EDGE - 16
        go_left = mask_of(mask_ref, M_LEFT, low, size)
        go_right = mask_of(mask_ref, M_RIGHT, low, size)
        for kept, first in ((over, 12), (under, 0)):
            kept[low : low + size, :LANE] = at(low, size, first + 1) + jnp.where(
                go_left, at(low - 1, size, first + 3), 0.0
            )
            kept[low : low + size, LANE:] = at(low, size, first + 2) + jnp.where(
                go_right, at(low + 1, size, first), 0.0
            )
        go_left = mask_of(mask_ref, M_LEFT, EDGE, padded)
        go_right = mask_of(mask_ref, M_RIGHT, EDGE, padded)
        valid = mask_of(mask_ref, M_VALID, EDGE, padded)
        total = jnp.zeros((1, LANE), F32)
        squares = jnp.zeros((1, LANE), F32)
        for q in range(4):
            a, b = q // 2, q % 2
            lanes = slice(b * LANE, (b + 1) * LANE)
            kept, sign = (over, -1) if a == 0 else (under, 1)
            rowwise = by_width(
                mask_ref, EDGE, padded,
                lambda w: kept[EDGE + sign * w : EDGE + sign * w + padded, lanes],
            )
            z = at(EDGE, padded, (a + 1) * 4 + b + 1)
            z = z + jnp.where(mask_of(mask_ref, (M_UP, M_DOWN)[a], EDGE, padded), rowwise, 0.0)
            if b == 0:
                z = z + jnp.where(go_left, at(EDGE - 1, padded, (a + 1) * 4 + 3), 0.0)
            else:
                z = z + jnp.where(go_right, at(EDGE + 1, padded, (a + 1) * 4), 0.0)
            z = jnp.where(valid, z, 0.0)
            zbuf[layer, q] = z
            total = total + jnp.sum(z, axis=0, keepdims=True)
            squares = squares + jnp.sum(z * z, axis=0, keepdims=True)
        saves(layer)[1].start()
        both = exchange_sums(
            rows, jnp.concatenate([total, squares, jnp.zeros((6, LANE), F32)], axis=0),
            sums.at[layer], sum_s.at[layer], sum_r.at[layer],
        )
        mean = both[0:1] / pixels
        inverse = lax.rsqrt(both[1:2] / pixels - mean * mean + EPSILON)
        stat_ref[layer] = jnp.concatenate([mean, inverse, jnp.zeros((6, LANE), F32)], axis=0)

        def activation(k, q):
            low, size = parts[k]
            y = gb_ref[layer, 0:1] * ((zbuf[layer, q, low : low + size] - mean) * inverse) + gb_ref[layer, 1:2]
            keep = mask_of(mask_ref, M_VALID, EDGE + low, size)
            return jnp.where(keep, y * jax.nn.sigmoid(y), 0.0).astype(BF16)

        @pl.when(more)
        def _():
            for k, (low, size) in enumerate(parts):
                for q in range(4):
                    vbuf[layer + 1, q, low : low + size, own_lanes] = activation(k, q)
                to_far(layer + 1, k).start()
                to_core(layer + 1, k).start()

        @pl.when(layer + 1 == layers)
        def _():
            for k, (low, size) in enumerate(parts):
                for q in range(4):
                    next_ref[q, low : low + size] = activation(k, q)

    each(layers, layer_step)

    def drain(layer):
        for k in range(len(parts)):
            to_far(layer, k).wait_send()
            to_core(layer, k).wait_send()
            pass_on(layer, k).wait_send()
        if inside:
            gather.drain(layer)
        for copy in saves(layer):
            copy.wait()

    each(layers, drain)


def backward_kernel(
    inside, pending, flush, layers, rows, count, padded, pixels, *refs
):
    refs = list(refs)
    g_ref, stat_ref, gb_ref, mask_ref, z_in, full_in, w_in = refs[:7]
    del refs[:7]
    dk_in = refs.pop(0) if pending else None
    grad_ref, gbgrad_ref = refs.pop(0), refs.pop(0)
    wgrad_ref = refs.pop(0) if inside else None
    dk_out = None if flush else refs.pop(0)
    (
        zbuf, fbuf, wbuf, dk, gy, gext, above, below, patch, part, keep, core_out, core_in, x_out, x_in,
        to_next, to_prev, from_prev, from_next, sums,
        core_s, core_r, x_s, x_r, halo_s, halo_r, sum_s, sum_r, load_sem, out_sem,
    ) = refs[:30]
    mine, here = lax.axis_index("grp"), lax.axis_index("rows")
    half, core = mine // 2, lax.rem(mine, 2)
    partner, across = grp_peers()
    own_lanes, other_lanes = lanes_of(core), lanes_of(1 - core)
    own_base = pl.multiple_of(half * 2 * LANE, 2 * LANE)
    far_base = pl.multiple_of((1 - half) * 2 * LANE, 2 * LANE)
    scatter = None
    if inside:
        first, second, third, s1, r1, s2, r2 = refs[30:]
        scatter = Scatter(rows, dk.shape[1] // rows, dk, first, second, third, wgrad_ref, s1, r1, s2, r2)

    def loads(layer):
        pairs = [(z_in, zbuf), (w_in, wbuf), (full_in, fbuf)]
        return [
            pltpu.make_async_copy(src.at[layer], dst.at[layer], load_sem.at[layer, k])
            for k, (src, dst) in enumerate(pairs)
        ]

    def dk_load():
        return pltpu.make_async_copy(dk_in, dk.at[0], out_sem)

    for layer in range(layers - 1, -1, -1):
        for copy in loads(layer):
            copy.start()
    if pending:
        dk_load().start()
    after = (lax.rem(here + 1, rows), mine)
    before = (lax.rem(here + rows - 1, rows), mine)
    down = remote(to_next, from_prev, halo_s.at[0], halo_r.at[0], after)
    up = remote(to_prev, from_next, halo_s.at[1], halo_r.at[1], before)
    grad_ref[...] = g_ref[...]
    gext[:EDGE, :] = jnp.zeros((EDGE, 4 * LANE), F32)
    gext[EDGE + padded :, :] = jnp.zeros((EDGE, 4 * LANE), F32)
    greet([partner, across] + row_peers(rows))
    if pending:
        dk_load().wait()

    def taps(q, step):
        first = (q // 2 + step) * 4 + q % 2
        return patch[:, first * LANE : (first + 3) * LANE]

    def layer_step(turn):
        layer = layers - 1 - turn
        side = lax.rem(turn, 2)
        last = turn + 1 == layers
        scattering = (turn >= 0) if pending else (turn > 0)
        mean, inverse = stat_ref[layer, 0:1], stat_ref[layer, 1:2]
        gain, shift = gb_ref[layer, 0:1], gb_ref[layer, 1:2]
        valid = mask_of(mask_ref, M_VALID, EDGE, padded)
        loads(layer)[0].wait()
        shift_sum = jnp.zeros((1, LANE), F32)
        gain_sum = jnp.zeros((1, LANE), F32)
        for q in range(4):
            normed = (zbuf[layer, q] - mean) * inverse
            y = gain * normed + shift
            s = jax.nn.sigmoid(y)
            grad = jnp.where(valid, grad_ref[q] * s * (1.0 + y * (1.0 - s)), 0.0)
            gy[q] = grad
            shift_sum = shift_sum + jnp.sum(grad, axis=0, keepdims=True)
            gain_sum = gain_sum + jnp.sum(grad * normed, axis=0, keepdims=True)
        both = exchange_sums(
            rows, jnp.concatenate([shift_sum, gain_sum, jnp.zeros((6, LANE), F32)], axis=0),
            sums.at[turn], sum_s.at[turn], sum_r.at[turn],
        )
        gbgrad_ref[layer] = both
        for q in range(4):
            normed = (zbuf[layer, q] - mean) * inverse
            gz = inverse * gain * (gy[q] - both[0:1] / pixels - normed * both[1:2] / pixels)
            gz = jnp.where(valid, gz, 0.0).astype(BF16).astype(F32)
            gext[EDGE : EDGE + padded, q * LANE : (q + 1) * LANE] = gz
        to_next[...] = gext[count : count + EDGE, :].astype(BF16)
        to_prev[...] = gext[EDGE : 2 * EDGE, :].astype(BF16)

        @pl.when(here + 1 < rows)
        def _():
            down.start()

        @pl.when(here > 0)
        def _():
            up.start()

        if inside:

            @pl.when(scattering)
            def _():
                scatter.start(turn)

        @pl.when(here > 0)
        def _():
            down.wait_recv()
            up.wait_send()
            gext[:EDGE, :] = from_prev[...].astype(F32)

        @pl.when(here + 1 < rows)
        def _():
            up.wait_recv()
            down.wait_send()
            gext[EDGE + count : 2 * EDGE + count, :] = from_next[...].astype(F32)

        low, size = EDGE - 8, padded + 16
        for kept, which, sign, lanes in (
            (above, M_UP, -1, slice(2 * LANE, 4 * LANE)),
            (below, M_DOWN, 1, slice(0, 2 * LANE)),
        ):
            rowwise = by_width(
                mask_ref, low, size, lambda w: gext[low + sign * w : low + sign * w + size, lanes]
            )
            kept[...] = jnp.where(mask_of(mask_ref, which, low, size), rowwise, 0.0)
        go_left = mask_of(mask_ref, M_LEFT, EDGE, padded)
        go_right = mask_of(mask_ref, M_RIGHT, EDGE, padded)
        for step, (kept, top, lane) in enumerate(
            ((above, 8, 0), (gext, EDGE, 0), (gext, EDGE, 2 * LANE), (below, 8, 0))
        ):
            even, odd = slice(lane, lane + LANE), slice(lane + LANE, lane + 2 * LANE)
            blocks = [
                jnp.where(go_left, kept[top - 1 : top - 1 + padded, odd], 0.0),
                kept[top : top + padded, even],
                kept[top : top + padded, odd],
                jnp.where(go_right, kept[top + 1 : top + 1 + padded, even], 0.0),
            ]
            for column, block in enumerate(blocks):
                spot = step * 4 + column
                patch[:, spot * LANE : (spot + 1) * LANE] = block.astype(BF16)

        def kernel_grad(step):
            total = None
            for q in range(4):
                product = lax.dot_general(
                    fbuf[layer, q], taps(q, step), (((0,), (0,)), ((), ())), preferred_element_type=F32
                )
                total = product if total is None else total + product
            dk[turn + 1, :, step * 3 * LANE : (step + 1) * 3 * LANE] = total.astype(BF16)

        loads(layer)[1].wait()
        loads(layer)[2].wait()
        if flush:

            @pl.when(last)
            def _():
                for step in range(3):
                    kernel_grad(step)
                if inside:
                    scatter.start(layers)

        def input_grad(q, base):
            total = None
            for step in range(3):
                right = wbuf[layer, pl.ds(base, 2 * LANE), step * 3 * LANE : (step + 1) * 3 * LANE]
                product = lax.dot_general(
                    taps(q, step), right, (((1,), (1,)), ((), ())), preferred_element_type=F32
                )
                total = product if total is None else total + product
            part[...] = total

        def to_core(spot):
            return remote(
                core_out.at[side, spot], core_in.at[side, spot],
                core_s.at[side, spot], core_r.at[side, spot], partner,
            )

        def to_far(q):
            return remote(x_out.at[side, q], x_in.at[side, q], x_s.at[side, q], x_r.at[side, q], across)

        def send_across(q):
            to_core(q).wait_recv()
            x_out[side, q] = (keep[q] + core_in[side, q].astype(F32)).astype(BF16)
            to_far(q).start()

        for which, base in enumerate((far_base, own_base)):
            for q in range(4):
                spot = which * 4 + q
                input_grad(q, base)
                core_out[side, spot] = part[:, other_lanes].astype(BF16)
                keep[spot] = part[:, own_lanes]
                to_core(spot).start()
                if which == 0 and q > 0:
                    send_across(q - 1)
            if which == 0:
                send_across(3)

        @pl.when(jnp.logical_not(last) if flush else turn >= 0)
        def _():
            for step in range(3):
                kernel_grad(step)

        if inside:

            @pl.when(scattering)
            def _():
                for step in scatter.order():
                    scatter.forward(turn, step)
        for q in range(4):
            to_core(4 + q).wait_recv()
            to_far(q).wait_recv()
            grad_ref[q] = keep[4 + q] + core_in[side, 4 + q].astype(F32) + x_in[side, q].astype(F32)
        for spot in range(8):
            to_core(spot).wait_send()
        for q in range(4):
            to_far(q).wait_send()
        if inside:

            @pl.when(scattering)
            def _():
                scatter.finish(turn)
                scatter.drain(turn)

    each(layers, layer_step)
    if inside and flush:
        for step in scatter.order():
            scatter.forward(layers, step)
        scatter.finish(layers)
        scatter.drain(layers)
    if not flush:
        copy = pltpu.make_async_copy(dk.at[layers] if inside else dk, dk_out, out_sem)
        copy.start()
        copy.wait()


VM = pl.BlockSpec(memory_space=pltpu.VMEM)
HBM = pl.BlockSpec(memory_space=pl.ANY)
LIMIT = 56 * 1024 * 1024
DMA = pltpu.SemaphoreType.DMA


def forward_block(inside, rows, count, padded, pixels, planes, weight, gain_shift, masks):
    layers, channels, taps = weight.shape[0], 4 * LANE, weight.shape[2]
    ext = padded + 2 * EDGE
    n_parts = len(row_parts(padded, count))
    far = rows // 2
    out = pl.pallas_call(
        functools.partial(forward_kernel, inside, layers, rows, count, padded, pixels),
        name="forward_block",
        out_shape=(
            jax.ShapeDtypeStruct((4, padded, LANE), BF16),
            jax.ShapeDtypeStruct((layers, 8, LANE), F32),
            jax.ShapeDtypeStruct((layers, 4, padded, LANE), F32),
            jax.ShapeDtypeStruct((layers, 4, padded, channels), BF16),
            jax.ShapeDtypeStruct((layers, channels, taps) if inside else (1, 16, LANE), BF16),
        ),
        in_specs=[VM, VM if inside else HBM, VM, VM],
        out_specs=(VM, VM, HBM, HBM, HBM),
        scratch_shapes=[
            pltpu.VMEM((layers, 4, padded, channels), BF16),
            pltpu.VMEM((layers, channels, taps), BF16),
            pltpu.VMEM((layers, 4, padded, LANE), F32),
            pltpu.VMEM((ext, 16 * LANE), F32),
            pltpu.VMEM((ext, 2 * LANE), F32),
            pltpu.VMEM((ext, 2 * LANE), F32),
        ]
        + [pltpu.VMEM((EDGE, 6 * LANE), F32)] * 4
        + [pltpu.VMEM((layers, rows, 8, LANE), F32)]
        + [DMA((layers, n_parts))] * 6
        + [DMA((2,))] * 2
        + [DMA((layers, rows - 1))] * 2
        + [DMA((layers, 3))]
        + [DMA((layers, far - 1))] * 2
        + [DMA((layers, far))] * 2,
        compiler_params=pltpu.CompilerParams(
            collective_id=0, has_side_effects=True, vmem_limit_bytes=LIMIT
        ),
    )(planes, weight, gain_shift, masks)
    return out[:4] + ((out[4] if inside else weight),)


def backward_block(
    inside, flush, rows, count, padded, pixels, grad, z, stat, gain_shift, masks, full, weight, dk
):
    layers, channels, taps = weight.shape
    ext = padded + 2 * EDGE
    pending = dk is not None
    shard = channels // rows
    far = rows // 2
    outs = [
        (jax.ShapeDtypeStruct((4, padded, LANE), F32), VM),
        (jax.ShapeDtypeStruct((layers, 8, LANE), F32), VM),
    ]
    if inside:
        outs.append((jax.ShapeDtypeStruct((layers + 1, shard, taps), F32), VM))
    if not flush:
        outs.append(
            (jax.ShapeDtypeStruct((channels, taps) if inside else (layers + 1, channels, taps), BF16), HBM)
        )
    scratch = [
        pltpu.VMEM((layers, 4, padded, LANE), F32),
        pltpu.VMEM((layers, 4, padded, channels), BF16),
        pltpu.VMEM((layers, channels, taps), BF16),
        pltpu.VMEM((layers + 1, channels, taps), BF16),
        pltpu.VMEM((4, padded, LANE), F32),
        pltpu.VMEM((ext, 4 * LANE), F32),
        pltpu.VMEM((padded + 16, 2 * LANE), F32),
        pltpu.VMEM((padded + 16, 2 * LANE), F32),
        pltpu.VMEM((padded, 16 * LANE), BF16),
        pltpu.VMEM((padded, 2 * LANE), F32),
        pltpu.VMEM((8, padded, LANE), F32),
        pltpu.VMEM((2, 8, padded, LANE), BF16),
        pltpu.VMEM((2, 8, padded, LANE), BF16),
        pltpu.VMEM((2, 4, padded, LANE), BF16),
        pltpu.VMEM((2, 4, padded, LANE), BF16),
    ]
    scratch += [pltpu.VMEM((EDGE, 4 * LANE), BF16)] * 4
    scratch += [pltpu.VMEM((layers, rows, 8, LANE), F32)]
    scratch += [DMA((2, 8))] * 2 + [DMA((2, 4))] * 2 + [DMA((2,))] * 2 + [DMA((layers, rows - 1))] * 2
    scratch += [DMA((layers, 3)), DMA]
    if inside:
        scratch += [
            pltpu.VMEM((layers + 1, far, shard, taps), BF16),
            pltpu.VMEM((layers + 1, far - 1, shard, taps), BF16),
            pltpu.VMEM((layers + 1, far - 1, shard, taps), BF16),
        ]
        scratch += [DMA((layers + 1, far))] * 2 + [DMA((layers + 1, far - 1))] * 2
    args = [grad, stat, gain_shift, masks, z, full, weight] + ([dk] if pending else [])
    return pl.pallas_call(
        functools.partial(backward_kernel, inside, pending, flush, layers, rows, count, padded, pixels),
        name="backward_block",
        out_shape=tuple(o for o, _ in outs),
        in_specs=[VM] * 4 + [HBM] * (len(args) - 4),
        out_specs=tuple(s for _, s in outs),
        scratch_shapes=scratch,
        compiler_params=pltpu.CompilerParams(
            collective_id=2 if flush else 1, has_side_effects=True, vmem_limit_bytes=LIMIT
        ),
    )(*args)


def shards(
    features, image_group, switches, enc_weight, dec_weight,
    enc_gain, enc_bias, dec_gain, dec_bias, d_decoded,
):
    rows = lax.axis_size("rows")
    count = features.shape[0] // 4
    padded = ceil_to(count, 16)
    pixels = float(features.shape[0] * rows)
    shard = enc_weight.shape[2]
    inside = shard % 16 == 0
    sizes = (rows, count, padded, pixels)
    masks = window_masks(image_group, lax.axis_index("rows") * count, count, padded)

    def flat_weight(weight):
        flat = jnp.transpose(weight[:, ::-1], (0, 2, 1, 3)).reshape(weight.shape[0], shard, -1)
        return flat if inside else lax.all_gather(flat, "rows", axis=1, tiled=True)

    def pair(gain, shift):
        return jnp.pad(jnp.stack([gain, shift], axis=1), ((0, 0), (0, 6), (0, 0)))

    enc_pair, dec_pair = pair(enc_gain, enc_bias), pair(dec_gain, dec_bias)
    hits = switches[None, :] == jnp.arange(4, dtype=jnp.int32)[:, None]
    hits = jnp.pad(hits.astype(F32), ((0, 0), (0, padded - count)))[:, :, None]

    _, enc_stat, enc_z, enc_full, enc_w = forward_block(
        inside, *sizes, to_planes(features, count, padded), flat_weight(enc_weight), enc_pair, masks
    )
    y = enc_pair[2, 0] * ((enc_z[2] - enc_stat[2, 0]) * enc_stat[2, 1]) + enc_pair[2, 1]
    blocks = jax.nn.silu(y)
    pooled = jnp.log(jnp.mean(jnp.exp(blocks), axis=0))
    planes = (pooled[None] * hits).astype(BF16)
    planes, dec_stat, dec_z, dec_full, dec_w = forward_block(
        inside, *sizes, planes, flat_weight(dec_weight), dec_pair, masks
    )
    decoded = to_stream(planes, count)

    grad = to_planes(d_decoded, count, padded).astype(F32)
    dec_out = backward_block(
        inside, False, *sizes, grad, dec_z, dec_stat, dec_pair, masks, dec_full, dec_w, None
    )
    grad_pooled = jnp.sum(dec_out[0] * hits, axis=0)
    grad = grad_pooled[None] * jnp.exp(blocks - pooled[None]) * 0.25
    enc_out = backward_block(
        inside, inside, *sizes, grad, enc_z, enc_stat, enc_pair, masks, enc_full, enc_w,
        dec_out[-1] if inside else None,
    )
    if inside:
        dec_parts = jnp.stack([enc_out[2][0], dec_out[2][2], dec_out[2][1]])
        enc_parts = jnp.stack([enc_out[2][3], enc_out[2][2], enc_out[2][1]])
    else:
        dec_parts, enc_parts = (
            lax.psum_scatter(out[-1][:0:-1], "rows", scatter_dimension=1, tiled=True).astype(F32)
            for out in (dec_out, enc_out)
        )

    def whole_taps(parts):
        return jnp.transpose(parts.reshape(3, shard, 9, -1)[:, :, ::-1], (0, 2, 1, 3))

    return (
        decoded,
        to_stream(enc_out[0].astype(BF16), count),
        whole_taps(enc_parts),
        whole_taps(dec_parts),
        enc_out[1][:, 1],
        enc_out[1][:, 0],
        dec_out[1][:, 1],
        dec_out[1][:, 0],
    )


def solution(mesh):
    wide = P("rows", "grp")
    kernels = P(None, None, "rows", "grp")
    vector = P(None, "grp")
    return jax.shard_map(
        shards,
        mesh=mesh,
        in_specs=(wide, P(), P("rows"), kernels, kernels, vector, vector, vector, vector, wide),
        out_specs=(wide, wide, kernels, kernels, vector, vector, vector, vector),
        check_vma=False,
    )
```

```python
import functools

import jax
import jax.numpy as jnp
from jax import lax
from jax.experimental import pallas as pl
from jax.experimental.pallas import tpu as pltpu
from jax.sharding import PartitionSpec as P

SIZES = ((15, 20), (18, 24), (30, 40))
WIDTHS = tuple(w for _, w in SIZES)
EDGE = 48
EPSILON = 1e-05
MESH = pl.DeviceIdType.MESH
F32 = jnp.float32
BF16 = jnp.bfloat16
LANE = 128
(M_W0, M_W1, M_UP, M_DOWN, M_LEFT, M_RIGHT, M_VALID, M_HIT) = range(8)
POOL = 2


def ceil_to(value, step):
    return -(-value // step) * step


def window_masks(image_group, switches, first_window, count, padded):
    chosen = (image_group[:, None] == jnp.arange(3, dtype=jnp.int32)[None, :]).astype(jnp.int32)
    heights = jnp.sum(chosen * jnp.array([h for h, _ in SIZES], jnp.int32)[None, :], axis=1)
    widths = jnp.sum(chosen * jnp.array(WIDTHS, jnp.int32)[None, :], axis=1)
    areas = heights * widths
    ends = jnp.cumsum(areas)
    starts = ends - areas
    local = jnp.arange(padded + 2 * EDGE, dtype=jnp.int32) - EDGE
    windows = local + first_window
    member = ((windows[:, None] >= starts[None, :]) & (windows[:, None] < ends[None, :])).astype(jnp.int32)
    base = jnp.sum(member * starts[None, :], axis=1)
    height = jnp.sum(member * heights[None, :], axis=1)
    width = jnp.sum(member * widths[None, :], axis=1)
    inside = width > 0
    position = windows - base
    safe = jnp.maximum(width, 1)
    row = position // safe
    column = position - row * safe
    masks = [
        width == WIDTHS[0],
        width == WIDTHS[1],
        inside & (row > 0),
        inside & (row < height - 1),
        inside & (column > 0),
        inside & (column < width - 1),
        (local >= 0) & (local < count),
    ]
    kept = jnp.pad(switches, (EDGE, padded - count + EDGE), constant_values=-1)
    masks += [kept == q for q in range(4)]
    table = jnp.stack([m.astype(F32) for m in masks], axis=1)
    return jnp.pad(table, ((0, 0), (0, LANE - len(masks))))


def to_planes(stream, count, padded):
    planes = jnp.transpose(stream.reshape(count, 4, stream.shape[1]), (1, 0, 2))
    return jnp.pad(planes, ((0, 0), (0, padded - count), (0, 0)))


def to_stream(planes, count):
    return jnp.transpose(planes[:, :count], (1, 0, 2)).reshape(4 * count, planes.shape[2])


def mask_of(mask_ref, which, low, count):
    return mask_ref[low : low + count, which : which + 1] > 0.5


def by_width(mask_ref, low, count, shifted):
    return jnp.where(
        mask_of(mask_ref, M_W0, low, count),
        shifted(WIDTHS[0]),
        jnp.where(mask_of(mask_ref, M_W1, low, count), shifted(WIDTHS[1]), shifted(WIDTHS[2])),
    )


def smooth_max(blocks):
    total = sum(jnp.exp(block) for block in blocks)
    return jnp.log(total * 0.25)


def row_peers(rows):
    here = lax.axis_index("rows")
    there = lax.axis_index("grp")
    order = sorted(range(1, rows), key=lambda k: -min(k, rows - k))
    return [(lax.rem(here + k, rows), there) for k in order]


def grp_peers():
    here = lax.axis_index("rows")
    mine = lax.axis_index("grp")
    half, core = mine // 2, lax.rem(mine, 2)
    return (here, half * 2 + 1 - core), (here, (1 - half) * 2 + core)


def greet(peers):
    barrier = pltpu.get_barrier_semaphore()
    for peer in peers:
        pl.semaphore_signal(barrier, inc=1, device_id=peer, device_id_type=MESH)
    pl.semaphore_wait(barrier, len(peers))


def remote(src, dst, send, recv, peer):
    return pltpu.make_async_remote_copy(
        src_ref=src, dst_ref=dst, send_sem=send, recv_sem=recv, device_id=peer, device_id_type=MESH
    )


def exchange_sums(rows, own, buf, send, recv):
    buf[0] = own
    copies = []
    for k, peer in enumerate(row_peers(rows)):
        copy = remote(buf.at[0], buf.at[k + 1], send.at[k], recv.at[k], peer)
        copy.start()
        copies.append(copy)
    for copy in copies:
        copy.wait()
    total = buf[0]
    for k in range(1, rows):
        total = total + buf[k]
    return total


def row_parts(padded, count):
    tail = (count - EDGE) // 16 * 16
    parts = [(0, EDGE), (tail, padded - tail)]
    start, steps = EDGE, 3
    for k in range(steps):
        size = min(ceil_to(-(-(tail - start) // (steps - k)), 16), tail - start)
        parts.append((start, size))
        start += size
    return parts


def lanes_of(block):
    return pl.ds(pl.multiple_of(block * LANE, LANE), LANE)


class Gather:
    def __init__(self, rows, shard, buf, send, recv, pass_send, pass_recv):
        self.shard, self.buf = shard, buf
        self.far = rows // 2
        here, there = lax.axis_index("rows"), lax.axis_index("grp")
        self.high, self.low = here // 2, lax.rem(here, 2)
        self.there = there
        self.send, self.recv, self.pass_send, self.pass_recv = send, recv, pass_send, pass_recv

    def rows_of(self, step, low):
        block = lax.rem(self.high + step, self.far) * 2 + low
        return pl.ds(pl.multiple_of(block * self.shard, 16), self.shard)

    def spread(self, layer, step):
        own = self.buf.at[layer, self.rows_of(0, self.low), :]
        peer = (lax.rem(self.high + step, self.far) * 2 + self.low, self.there)
        k = step - 1
        return remote(own, own, self.send.at[layer, k], self.recv.at[layer, k], peer)

    def across(self, layer, step):
        piece = self.buf.at[layer, self.rows_of(self.far - step, self.low), :]
        peer = (self.high * 2 + 1 - self.low, self.there)
        return remote(piece, piece, self.pass_send.at[layer, step], self.pass_recv.at[layer, step], peer)

    def start(self, layer, own):
        self.buf[layer, self.rows_of(0, self.low), :] = own
        for step in range(1, self.far):
            self.spread(layer, step).start()
        self.across(layer, 0).start()

    def forward(self, layer, step):
        self.spread(layer, step).wait_recv()
        self.across(layer, step).start()

    def wait(self, layer):
        for step in range(self.far):
            self.across(layer, step).wait_recv()

    def drain(self, layer):
        for step in range(1, self.far):
            self.spread(layer, step).wait_send()
        for step in range(self.far):
            self.across(layer, step).wait_send()


class Scatter:
    def __init__(self, rows, shard, grads, first, second, third, out, send, recv, far_send, far_recv):
        self.shard, self.grads, self.first, self.second, self.third = shard, grads, first, second, third
        self.out, self.far = out, rows // 2
        here, self.there = lax.axis_index("rows"), lax.axis_index("grp")
        self.high, self.low = here // 2, lax.rem(here, 2)
        self.send, self.recv, self.far_send, self.far_recv = send, recv, far_send, far_recv

    def rows_of(self, step, low):
        block = lax.rem(self.high + step, self.far) * 2 + low
        return pl.ds(pl.multiple_of(block * self.shard, 16), self.shard)

    def across(self, turn, step):
        slot = lax.rem(turn, 2)
        peer = (self.high * 2 + 1 - self.low, self.there)
        return remote(
            self.grads.at[slot, self.rows_of(step, 1 - self.low), :], self.first.at[slot, step],
            self.send.at[slot, step], self.recv.at[slot, step], peer,
        )

    def spread(self, turn, step):
        slot = lax.rem(turn, 2)
        peer = (lax.rem(self.high + step, self.far) * 2 + self.low, self.there)
        k = step - 1
        return remote(
            self.second.at[slot, k], self.third.at[slot, k],
            self.far_send.at[slot, k], self.far_recv.at[slot, k], peer,
        )

    def order(self):
        return list(range(1, self.far)) + [0]

    def start(self, turn):
        for step in self.order():
            self.across(turn, step).start()

    def forward(self, turn, step, layer):
        slot = lax.rem(turn, 2)
        self.across(turn, step).wait_recv()
        own = self.grads[slot, self.rows_of(step, self.low), :]
        total = own.astype(F32) + self.first[slot, step].astype(F32)
        if step == 0:
            self.out[layer] = total
        else:
            self.second[slot, step - 1] = total.astype(BF16)
            self.spread(turn, step).start()

    def finish(self, turn, layer):
        slot = lax.rem(turn, 2)
        total = self.out[layer]
        for step in range(1, self.far):
            self.spread(turn, step).wait_recv()
            total = total + self.third[slot, step - 1].astype(F32)
        self.out[layer] = total

    def drain(self, turn):
        for step in range(self.far):
            self.across(turn, step).wait_send()
        for step in range(1, self.far):
            self.spread(turn, step).wait_send()


def each(count, body):
    lax.fori_loop(0, count, lambda i, carry: (body(i), carry)[1], 0)


def forward_kernel(
    inside, layers, rows, count, padded, pixels,
    v_ref, w_ref, gb_ref, mask_ref,
    next_ref, stat_ref, z_out, full_out, w_out,
    vbuf, wbuf, zbuf, yext, over, under, to_next, to_prev, from_prev, from_next, sums,
    core_s, core_r, x_s, x_r, fwd_s, fwd_r, halo_s, halo_r, sum_s, sum_r, out_sem,
    w_s, w_r, wp_s, wp_r,
):
    mine, here = lax.axis_index("grp"), lax.axis_index("rows")
    half = mine // 2
    partner, across = grp_peers()
    parts = row_parts(padded, count)
    own_lanes, far_lanes = lanes_of(mine), lanes_of(across[1])
    own_base = pl.multiple_of(half * 2 * LANE, 2 * LANE)
    far_base = pl.multiple_of((1 - half) * 2 * LANE, 2 * LANE)
    gather = Gather(rows, w_ref.shape[1], wbuf, w_s, w_r, wp_s, wp_r)

    def slab(layer, k, lanes):
        low, size = parts[k]
        return vbuf.at[layer, :, pl.ds(low, size), lanes]

    def to_core(layer, k):
        piece = slab(layer, k, own_lanes)
        return remote(piece, piece, core_s.at[layer, k], core_r.at[layer, k], partner)

    def to_far(layer, k):
        piece = slab(layer, k, own_lanes)
        return remote(piece, piece, x_s.at[layer, k], x_r.at[layer, k], across)

    def pass_on(layer, k):
        piece = slab(layer, k, far_lanes)
        return remote(piece, piece, fwd_s.at[layer, k], fwd_r.at[layer, k], partner)

    def load(layer):
        return pltpu.make_async_copy(w_ref.at[layer], wbuf.at[layer], w_s.at[layer, 0])

    def save(layer, which):
        pairs = [(vbuf, full_out), (zbuf, z_out), (wbuf, w_out)]
        src, dst = pairs[which]
        return pltpu.make_async_copy(src.at[layer], dst.at[layer], out_sem.at[layer, which])

    after = (lax.rem(here + 1, rows), mine)
    before = (lax.rem(here + rows - 1, rows), mine)
    down = remote(to_next, from_prev, halo_s.at[0], halo_r.at[0], after)
    up = remote(to_prev, from_next, halo_s.at[1], halo_r.at[1], before)

    def add_products(layer, low, size, base, touched):
        for q in range(4):
            a, b = q // 2, q % 2
            left = vbuf[layer, q, low : low + size, pl.ds(base, 2 * LANE)]
            for step in range(3):
                right = wbuf[layer, pl.ds(base, 2 * LANE), step * 3 * LANE : (step + 1) * 3 * LANE]
                product = jnp.dot(left, right, preferred_element_type=F32)
                for column in range(3):
                    spot = (a + step) * 4 + b + column
                    block = product[:, column * LANE : (column + 1) * LANE]
                    where = (slice(EDGE + low, EDGE + low + size), slice(spot * LANE, (spot + 1) * LANE))
                    if spot in touched:
                        yext[where] += block
                    else:
                        yext[where] = block
                        touched.add(spot)

    def at(low, size, spot):
        return yext[low : low + size, spot * LANE : (spot + 1) * LANE]

    greet([partner, across] + row_peers(rows))
    vbuf[0, :, :, own_lanes] = v_ref[...]
    for k in range(len(parts)):
        to_far(0, k).start()
        to_core(0, k).start()
    if inside:
        gather.start(0, w_ref[0])
    else:
        load(0).start()
    yext[:EDGE, :] = jnp.zeros((EDGE, yext.shape[1]), F32)
    yext[EDGE + padded :, :] = jnp.zeros((EDGE, yext.shape[1]), F32)
    if inside:
        for step in range(1, rows // 2):
            gather.forward(0, step)

    def layer_step(layer):
        more = layer + 1 < layers
        if inside:
            gather.wait(layer)
            save(layer, 2).start()

            @pl.when(more)
            def _():
                gather.start(layer + 1, w_ref[layer + 1])
        else:
            load(layer).wait()

            @pl.when(more)
            def _():
                load(layer + 1).start()

        for k in range(len(parts)):
            to_core(layer, k).wait_recv()
        add_products(layer, 0, padded, own_base, set())

        def gather_forward(first, end):
            @pl.when(more)
            def _():
                for step in range(first, end):
                    gather.forward(layer + 1, step)

        def far_products(k):
            pass_on(layer, k).wait_recv()
            low, size = parts[k]
            add_products(layer, low, size, far_base, set(range(16)))
            if k != 1:
                return
            for lane, spot in enumerate((12, 13, 14, 15, 7, 11)):
                to_next[:, lane * LANE : (lane + 1) * LANE] = at(count, EDGE, spot).astype(BF16)
            for lane, spot in enumerate((0, 1, 2, 3, 4, 8)):
                to_prev[:, lane * LANE : (lane + 1) * LANE] = at(EDGE, EDGE, spot).astype(BF16)

            @pl.when(here + 1 < rows)
            def _():
                down.start()

            @pl.when(here > 0)
            def _():
                up.start()

        for k in range(len(parts)):
            to_far(layer, k).wait_recv()
            pass_on(layer, k).start()
            if k > 0:
                far_products(k - 1)
            if inside and k == 2:
                gather_forward(1, 2)
        far_products(len(parts) - 1)
        save(layer, 0).start()
        if inside:
            gather_forward(2, 3)

        @pl.when(here > 0)
        def _():
            down.wait_recv()
            up.wait_send()
            for lane, spot in enumerate((12, 13, 14, 15, 7, 11)):
                received = from_prev[:, lane * LANE : (lane + 1) * LANE].astype(F32)
                yext[:EDGE, spot * LANE : (spot + 1) * LANE] = received

        @pl.when(here + 1 < rows)
        def _():
            up.wait_recv()
            down.wait_send()
            for lane, spot in enumerate((0, 1, 2, 3, 4, 8)):
                received = from_next[:, lane * LANE : (lane + 1) * LANE].astype(F32)
                yext[EDGE + count : 2 * EDGE + count, spot * LANE : (spot + 1) * LANE] = received

        low, size = 8, padded + 2 * EDGE - 16
        go_left = mask_of(mask_ref, M_LEFT, low, size)
        go_right = mask_of(mask_ref, M_RIGHT, low, size)
        for kept, first in ((over, 12), (under, 0)):
            kept[low : low + size, :LANE] = at(low, size, first + 1) + jnp.where(
                go_left, at(low - 1, size, first + 3), 0.0
            )
            kept[low : low + size, LANE:] = at(low, size, first + 2) + jnp.where(
                go_right, at(low + 1, size, first), 0.0
            )
        go_left = mask_of(mask_ref, M_LEFT, EDGE, padded)
        go_right = mask_of(mask_ref, M_RIGHT, EDGE, padded)
        valid = mask_of(mask_ref, M_VALID, EDGE, padded)
        total = jnp.zeros((1, LANE), F32)
        squares = jnp.zeros((1, LANE), F32)
        for q in range(4):
            a, b = q // 2, q % 2
            lanes = slice(b * LANE, (b + 1) * LANE)
            kept, sign = (over, -1) if a == 0 else (under, 1)
            rowwise = by_width(
                mask_ref, EDGE, padded,
                lambda w: kept[EDGE + sign * w : EDGE + sign * w + padded, lanes],
            )
            z = at(EDGE, padded, (a + 1) * 4 + b + 1)
            z = z + jnp.where(mask_of(mask_ref, (M_UP, M_DOWN)[a], EDGE, padded), rowwise, 0.0)
            if b == 0:
                z = z + jnp.where(go_left, at(EDGE - 1, padded, (a + 1) * 4 + 3), 0.0)
            else:
                z = z + jnp.where(go_right, at(EDGE + 1, padded, (a + 1) * 4), 0.0)
            z = jnp.where(valid, z, 0.0)
            zbuf[layer, q] = z
            total = total + jnp.sum(z, axis=0, keepdims=True)
            squares = squares + jnp.sum(z * z, axis=0, keepdims=True)
        save(layer, 1).start()
        both = exchange_sums(
            rows, jnp.concatenate([total, squares, jnp.zeros((6, LANE), F32)], axis=0),
            sums.at[layer], sum_s.at[layer], sum_r.at[layer],
        )
        if inside:
            gather_forward(3, rows // 2)
        mean = both[0:1] / pixels
        inverse = lax.rsqrt(both[1:2] / pixels - mean * mean + EPSILON)
        stat_ref[layer] = jnp.concatenate([mean, inverse, jnp.zeros((6, LANE), F32)], axis=0)

        def activation(k, q):
            low, size = parts[k]
            y = gb_ref[layer, 0:1] * ((zbuf[layer, q, low : low + size] - mean) * inverse) + gb_ref[layer, 1:2]
            return y * jax.nn.sigmoid(y)

        def kept(k, which):
            low, size = parts[k]
            return mask_of(mask_ref, which, EDGE + low, size)

        def pass_to_next(of_part):
            for k, (low, size) in enumerate(parts):
                blocks = of_part(k)
                for q in range(4):
                    vbuf[layer + 1, q, low : low + size, own_lanes] = blocks[q].astype(BF16)
                to_far(layer + 1, k).start()
                to_core(layer + 1, k).start()

        def plain(k):
            return [jnp.where(kept(k, M_VALID), activation(k, q), 0.0) for q in range(4)]

        def unpooled(k):
            pooled = smooth_max([activation(k, q) for q in range(4)])
            return [jnp.where(kept(k, M_HIT + q), pooled, 0.0) for q in range(4)]

        @pl.when(jnp.logical_and(more, layer != POOL))
        def _():
            pass_to_next(plain)

        @pl.when(layer == POOL)
        def _():
            pass_to_next(unpooled)

        @pl.when(layer + 1 == layers)
        def _():
            for k, (low, size) in enumerate(parts):
                for q, block in enumerate(plain(k)):
                    next_ref[q, low : low + size] = block.astype(BF16)

    each(layers, layer_step)

    def drain(layer):
        for k in range(len(parts)):
            to_far(layer, k).wait_send()
            to_core(layer, k).wait_send()
            pass_on(layer, k).wait_send()
        if inside:
            gather.drain(layer)
        for which in range(3 if inside else 2):
            save(layer, which).wait()

    each(layers, drain)


def backward_kernel(inside, layers, rows, count, padded, pixels, *refs):
    refs = list(refs)
    g_ref, stat_ref, gb_ref, mask_ref, z_in, full_in, w_in = refs[:7]
    grad_ref, gbgrad_ref, wgrad_ref = refs[7:10]
    (
        zbuf, fbuf, wbuf, dk, gy, gext, above, below, patch, part, keep, core_out, core_in, x_out, x_in,
        to_next, to_prev, from_prev, from_next, sums,
        core_s, core_r, x_s, x_r, halo_s, halo_r, sum_s, sum_r, load_sem, out_sem,
    ) = refs[10:40]
    mine, here = lax.axis_index("grp"), lax.axis_index("rows")
    half, core = mine // 2, lax.rem(mine, 2)
    partner, across = grp_peers()
    own_lanes, other_lanes = lanes_of(core), lanes_of(1 - core)
    own_base = pl.multiple_of(half * 2 * LANE, 2 * LANE)
    far_base = pl.multiple_of((1 - half) * 2 * LANE, 2 * LANE)
    if inside:
        first, second, third, s1, r1, s2, r2 = refs[40:]
        scatter = Scatter(rows, dk.shape[1] // rows, dk, first, second, third, wgrad_ref, s1, r1, s2, r2)

    def load(turn, which):
        src, dst = ((z_in, zbuf), (w_in, wbuf), (full_in, fbuf))[which]
        side = lax.rem(turn, 2)
        return pltpu.make_async_copy(src.at[layers - 1 - turn], dst.at[side], load_sem.at[side, which])

    def save(turn):
        side = lax.rem(turn, 2)
        return pltpu.make_async_copy(dk.at[side], wgrad_ref.at[layers - 1 - turn], out_sem.at[side])

    for turn in range(2):
        for which in range(3):
            load(turn, which).start()
    after = (lax.rem(here + 1, rows), mine)
    before = (lax.rem(here + rows - 1, rows), mine)
    grad_ref[...] = g_ref[...]
    gext[:EDGE, :] = jnp.zeros((EDGE, 4 * LANE), F32)
    gext[EDGE + padded :, :] = jnp.zeros((EDGE, 4 * LANE), F32)
    greet([partner, across] + row_peers(rows))

    def taps(q, step):
        first = (q // 2 + step) * 4 + q % 2
        return patch[:, first * LANE : (first + 3) * LANE]

    def layer_step(turn):
        layer = layers - 1 - turn
        side = lax.rem(turn, 2)
        last = turn + 1 == layers
        mean, inverse = stat_ref[layer, 0:1], stat_ref[layer, 1:2]
        gain, shift = gb_ref[layer, 0:1], gb_ref[layer, 1:2]
        valid = mask_of(mask_ref, M_VALID, EDGE, padded)
        load(turn, 0).wait()
        down = remote(to_next, from_prev.at[side], halo_s.at[0], halo_r.at[side, 0], after)
        up = remote(to_prev, from_next.at[side], halo_s.at[1], halo_r.at[side, 1], before)

        def shifted(q):
            normed = (zbuf[side, q] - mean) * inverse
            return normed, gain * normed + shift

        @pl.when(layer == POOL)
        def _():
            pooled_grad = jnp.zeros((padded, LANE), F32)
            for q in range(4):
                pooled_grad = jnp.where(mask_of(mask_ref, M_HIT + q, EDGE, padded), grad_ref[q], pooled_grad)
            blocks = []
            for q in range(4):
                _, y = shifted(q)
                gy[q] = y * jax.nn.sigmoid(y)
            pooled = smooth_max([gy[q] for q in range(4)])
            for q in range(4):
                grad_ref[q] = pooled_grad * (jnp.exp(gy[q] - pooled) * 0.25)

        shift_sum = jnp.zeros((1, LANE), F32)
        gain_sum = jnp.zeros((1, LANE), F32)
        for q in range(4):
            normed, y = shifted(q)
            s = jax.nn.sigmoid(y)
            grad = jnp.where(valid, grad_ref[q] * s * (1.0 + y * (1.0 - s)), 0.0)
            gy[q] = grad
            shift_sum = shift_sum + jnp.sum(grad, axis=0, keepdims=True)
            gain_sum = gain_sum + jnp.sum(grad * normed, axis=0, keepdims=True)

        def spread(buf, low, planes):
            for lane, q in enumerate(planes):
                piece = slice(low, low + EDGE)
                normed = (zbuf[side, q, piece] - mean) * inverse
                buf[:, 2 * lane * LANE : (2 * lane + 1) * LANE] = gy[q, piece].astype(BF16)
                buf[:, (2 * lane + 1) * LANE : (2 * lane + 2) * LANE] = normed.astype(BF16)

        spread(to_next, count - EDGE, (2, 3, 1))
        spread(to_prev, 0, (0, 1, 2))

        @pl.when(here + 1 < rows)
        def _():
            down.start()

        @pl.when(here > 0)
        def _():
            up.start()

        if inside:

            @pl.when(turn > 1)
            def _():
                scatter.finish(turn - 2, layer + 2)
                scatter.drain(turn - 2)

        both = exchange_sums(
            rows, jnp.concatenate([shift_sum, gain_sum, jnp.zeros((6, LANE), F32)], axis=0),
            sums.at[side], sum_s.at[side], sum_r.at[side],
        )
        gbgrad_ref[layer] = both
        if inside:

            @pl.when(turn > 0)
            def _():
                scatter.start(turn - 1)

        def conv_grad(grad, normed):
            out = inverse * gain * (grad - both[0:1] / pixels - normed * both[1:2] / pixels)
            return out.astype(BF16).astype(F32)

        for q in range(4):
            normed, _ = shifted(q)
            gext[EDGE : EDGE + padded, q * LANE : (q + 1) * LANE] = jnp.where(
                valid, conv_grad(gy[q], normed), 0.0
            )

        def receive(buf, low, planes):
            for lane, q in enumerate(planes):
                grad = buf[side, :, 2 * lane * LANE : (2 * lane + 1) * LANE].astype(F32)
                normed = buf[side, :, (2 * lane + 1) * LANE : (2 * lane + 2) * LANE].astype(F32)
                gext[low : low + EDGE, q * LANE : (q + 1) * LANE] = conv_grad(grad, normed)

        @pl.when(here > 0)
        def _():
            down.wait_recv()
            up.wait_send()
            receive(from_prev, 0, (2, 3, 1))

        @pl.when(here + 1 < rows)
        def _():
            up.wait_recv()
            down.wait_send()
            receive(from_next, EDGE + count, (0, 1, 2))

        low, size = EDGE - 8, padded + 16
        for kept, which, sign, lanes in (
            (above, M_UP, -1, slice(2 * LANE, 4 * LANE)),
            (below, M_DOWN, 1, slice(0, 2 * LANE)),
        ):
            rowwise = by_width(
                mask_ref, low, size, lambda w: gext[low + sign * w : low + sign * w + size, lanes]
            )
            kept[...] = jnp.where(mask_of(mask_ref, which, low, size), rowwise, 0.0)
        go_left = mask_of(mask_ref, M_LEFT, EDGE, padded)
        go_right = mask_of(mask_ref, M_RIGHT, EDGE, padded)
        for step, (kept, top, lane) in enumerate(
            ((above, 8, 0), (gext, EDGE, 0), (gext, EDGE, 2 * LANE), (below, 8, 0))
        ):
            even, odd = slice(lane, lane + LANE), slice(lane + LANE, lane + 2 * LANE)
            blocks = [
                jnp.where(go_left, kept[top - 1 : top - 1 + padded, odd], 0.0),
                kept[top : top + padded, even],
                kept[top : top + padded, odd],
                jnp.where(go_right, kept[top + 1 : top + 1 + padded, even], 0.0),
            ]
            for column, block in enumerate(blocks):
                spot = step * 4 + column
                patch[:, spot * LANE : (spot + 1) * LANE] = block.astype(BF16)

        def kernel_grad():
            for step in range(3):
                total = None
                for q in range(4):
                    product = lax.dot_general(
                        fbuf[side, q], taps(q, step), (((0,), (0,)), ((), ())), preferred_element_type=F32
                    )
                    total = product if total is None else total + product
                dk[side, :, step * 3 * LANE : (step + 1) * 3 * LANE] = total.astype(BF16)
            if not inside:
                save(turn).start()

        load(turn, 1).wait()
        load(turn, 2).wait()
        if not inside:

            @pl.when(turn > 1)
            def _():
                save(turn - 2).wait()

        @pl.when(last)
        def _():
            kernel_grad()
            if inside:
                scatter.start(turn)

        def input_grad(q, base):
            total = None
            for step in range(3):
                right = wbuf[side, pl.ds(base, 2 * LANE), step * 3 * LANE : (step + 1) * 3 * LANE]
                product = lax.dot_general(
                    taps(q, step), right, (((1,), (1,)), ((), ())), preferred_element_type=F32
                )
                total = product if total is None else total + product
            part[...] = total

        def to_core(spot):
            return remote(
                core_out.at[side, spot], core_in.at[side, spot],
                core_s.at[side, spot], core_r.at[side, spot], partner,
            )

        def to_far(q):
            return remote(x_out.at[side, q], x_in.at[side, q], x_s.at[side, q], x_r.at[side, q], across)

        def send_across(q):
            to_core(q).wait_recv()
            x_out[side, q] = (keep[q] + core_in[side, q].astype(F32)).astype(BF16)
            to_far(q).start()

        for spot in range(8):
            input_grad(spot % 4, far_base if spot < 4 else own_base)
            core_out[side, spot] = part[:, other_lanes].astype(BF16)
            keep[spot] = part[:, own_lanes]
            to_core(spot).start()
            if 2 <= spot < 6:
                send_across(spot - 2)

        @pl.when(jnp.logical_not(last))
        def _():
            kernel_grad()

        @pl.when(turn + 2 < layers)
        def _():
            for which in range(3):
                load(turn + 2, which).start()

        if inside:

            @pl.when(turn > 0)
            def _():
                for step in scatter.order():
                    scatter.forward(turn - 1, step, layer + 1)
        for q in range(4):
            to_core(4 + q).wait_recv()
            to_far(q).wait_recv()
            grad_ref[q] = keep[4 + q] + core_in[side, 4 + q].astype(F32) + x_in[side, q].astype(F32)
        for spot in range(8):
            to_core(spot).wait_send()
        for q in range(4):
            to_far(q).wait_send()

    each(layers, layer_step)
    if inside:
        for step in scatter.order():
            scatter.forward(layers - 1, step, 0)
        for turn in (layers - 2, layers - 1):
            scatter.finish(turn, layers - 1 - turn)
            scatter.drain(turn)
    else:
        for turn in (layers - 2, layers - 1):
            save(turn).wait()


VM = pl.BlockSpec(memory_space=pltpu.VMEM)
HBM = pl.BlockSpec(memory_space=pl.ANY)
LIMIT = 56 * 1024 * 1024
DMA = pltpu.SemaphoreType.DMA


def forward_block(inside, rows, count, padded, pixels, planes, weight, gain_shift, masks):
    layers, channels, taps = weight.shape[0], 4 * LANE, weight.shape[2]
    ext = padded + 2 * EDGE
    n_parts = len(row_parts(padded, count))
    far = rows // 2
    out = pl.pallas_call(
        functools.partial(forward_kernel, inside, layers, rows, count, padded, pixels),
        name="forward_block",
        out_shape=(
            jax.ShapeDtypeStruct((4, padded, LANE), BF16),
            jax.ShapeDtypeStruct((layers, 8, LANE), F32),
            jax.ShapeDtypeStruct((layers, 4, padded, LANE), F32),
            jax.ShapeDtypeStruct((layers, 4, padded, channels), BF16),
            jax.ShapeDtypeStruct((layers, channels, taps) if inside else (1, 16, LANE), BF16),
        ),
        in_specs=[VM, VM if inside else HBM, VM, VM],
        out_specs=(VM, VM, HBM, HBM, HBM),
        scratch_shapes=[
            pltpu.VMEM((layers, 4, padded, channels), BF16),
            pltpu.VMEM((layers, channels, taps), BF16),
            pltpu.VMEM((layers, 4, padded, LANE), F32),
            pltpu.VMEM((ext, 16 * LANE), F32),
            pltpu.VMEM((ext, 2 * LANE), F32),
            pltpu.VMEM((ext, 2 * LANE), F32),
        ]
        + [pltpu.VMEM((EDGE, 6 * LANE), BF16)] * 4
        + [pltpu.VMEM((layers, rows, 8, LANE), F32)]
        + [DMA((layers, n_parts))] * 6
        + [DMA((2,))] * 2
        + [DMA((layers, rows - 1))] * 2
        + [DMA((layers, 3))]
        + [DMA((layers, far - 1))] * 2
        + [DMA((layers, far))] * 2,
        compiler_params=pltpu.CompilerParams(
            collective_id=0, has_side_effects=True, vmem_limit_bytes=LIMIT
        ),
    )(planes, weight, gain_shift, masks)
    return out[:4] + ((out[4] if inside else weight),)


def backward_block(inside, rows, count, padded, pixels, grad, z, stat, gain_shift, masks, full, weight):
    layers, channels, taps = weight.shape
    ext = padded + 2 * EDGE
    shard = channels // rows
    far = rows // 2
    scratch = [
        pltpu.VMEM((2, 4, padded, LANE), F32),
        pltpu.VMEM((2, 4, padded, channels), BF16),
        pltpu.VMEM((2, channels, taps), BF16),
        pltpu.VMEM((2, channels, taps), BF16),
        pltpu.VMEM((4, padded, LANE), F32),
        pltpu.VMEM((ext, 4 * LANE), F32),
        pltpu.VMEM((padded + 16, 2 * LANE), F32),
        pltpu.VMEM((padded + 16, 2 * LANE), F32),
        pltpu.VMEM((padded, 16 * LANE), BF16),
        pltpu.VMEM((padded, 2 * LANE), F32),
        pltpu.VMEM((8, padded, LANE), F32),
        pltpu.VMEM((2, 8, padded, LANE), BF16),
        pltpu.VMEM((2, 8, padded, LANE), BF16),
        pltpu.VMEM((2, 4, padded, LANE), BF16),
        pltpu.VMEM((2, 4, padded, LANE), BF16),
    ]
    scratch += [pltpu.VMEM((EDGE, 6 * LANE), BF16)] * 2 + [pltpu.VMEM((2, EDGE, 6 * LANE), BF16)] * 2
    scratch += [pltpu.VMEM((2, rows, 8, LANE), F32)]
    scratch += [DMA((2, 8))] * 2 + [DMA((2, 4))] * 2 + [DMA((2,)), DMA((2, 2))] + [DMA((2, rows - 1))] * 2
    scratch += [DMA((2, 3)), DMA((2,))]
    if inside:
        scratch += [
            pltpu.VMEM((2, far, shard, taps), BF16),
            pltpu.VMEM((2, far - 1, shard, taps), BF16),
            pltpu.VMEM((2, far - 1, shard, taps), BF16),
        ]
        scratch += [DMA((2, far))] * 2 + [DMA((2, far - 1))] * 2
    return pl.pallas_call(
        functools.partial(backward_kernel, inside, layers, rows, count, padded, pixels),
        name="backward_block",
        out_shape=(
            jax.ShapeDtypeStruct((4, padded, LANE), F32),
            jax.ShapeDtypeStruct((layers, 8, LANE), F32),
            jax.ShapeDtypeStruct((layers, shard, taps), F32)
            if inside
            else jax.ShapeDtypeStruct((layers, channels, taps), BF16),
        ),
        in_specs=[VM] * 4 + [HBM] * 3,
        out_specs=(VM, VM, VM if inside else HBM),
        scratch_shapes=scratch,
        compiler_params=pltpu.CompilerParams(
            collective_id=1, has_side_effects=True, vmem_limit_bytes=LIMIT
        ),
    )(grad, stat, gain_shift, masks, z, full, weight)


def shards(
    features, image_group, switches, enc_weight, dec_weight,
    enc_gain, enc_bias, dec_gain, dec_bias, d_decoded,
):
    rows = lax.axis_size("rows")
    count = features.shape[0] // 4
    padded = ceil_to(count, 16)
    pixels = float(features.shape[0] * rows)
    shard = enc_weight.shape[2]
    inside = shard % 16 == 0
    sizes = (rows, count, padded, pixels)
    masks = window_masks(image_group, switches, lax.axis_index("rows") * count, count, padded)

    both = jnp.concatenate([enc_weight, dec_weight])
    flat = jnp.transpose(both[:, ::-1], (0, 2, 1, 3)).reshape(both.shape[0], shard, -1)
    if not inside:
        flat = lax.all_gather(flat, "rows", axis=1, tiled=True)
    pairs = jnp.stack([jnp.concatenate([enc_gain, dec_gain]), jnp.concatenate([enc_bias, dec_bias])], axis=1)
    pairs = jnp.pad(pairs, ((0, 0), (0, 6), (0, 0)))

    planes, stat, z, full, weight = forward_block(
        inside, *sizes, to_planes(features, count, padded), flat, pairs, masks
    )
    grad = to_planes(d_decoded, count, padded).astype(F32)
    grad, pair_grads, weight_grads = backward_block(
        inside, *sizes, grad, z, stat, pairs, masks, full, weight
    )
    if not inside:
        weight_grads = lax.psum_scatter(weight_grads, "rows", scatter_dimension=1, tiled=True).astype(F32)
    layers = weight_grads.shape[0]
    weight_grads = jnp.transpose(weight_grads.reshape(layers, shard, 9, -1)[:, :, ::-1], (0, 2, 1, 3))
    return (
        to_stream(planes, count),
        to_stream(grad.astype(BF16), count),
        weight_grads[:3],
        weight_grads[3:],
        pair_grads[:3, 1],
        pair_grads[:3, 0],
        pair_grads[3:, 1],
        pair_grads[3:, 0],
    )


def solution(mesh):
    wide = P("rows", "grp")
    kernels = P(None, None, "rows", "grp")
    vector = P(None, "grp")
    return jax.shard_map(
        shards,
        mesh=mesh,
        in_specs=(wide, P(), P("rows"), kernels, kernels, vector, vector, vector, vector, wide),
        out_specs=(wide, wide, kernels, kernels, vector, vector, vector, vector),
        check_vma=False,
    )
```

```python
import functools

import jax
import jax.numpy as jnp
from jax import lax
from jax.experimental import pallas as pl
from jax.experimental.pallas import tpu as pltpu
from jax.sharding import PartitionSpec as P

SIZES = ((15, 20), (18, 24), (30, 40))
WIDTHS = tuple(w for _, w in SIZES)
EDGE = 48
EPSILON = 1e-05
MESH = pl.DeviceIdType.MESH
F32 = jnp.float32
BF16 = jnp.bfloat16
LANE = 128
(M_W0, M_W1, M_UP, M_DOWN, M_LEFT, M_RIGHT, M_VALID, M_HIT) = range(8)
POOL = 2


def ceil_to(value, step):
    return -(-value // step) * step


def fill_masks(group_ref, first_window, count, padded, switch_ref, mask_ref):
    shape = (padded + 2 * EDGE, 1)
    local = lax.broadcasted_iota(jnp.int32, shape, 0) - EDGE
    windows = local + first_window

    start = jnp.int32(0)
    base = height = width = jnp.zeros(shape, jnp.int32)
    for image in range(group_ref.shape[0]):
        group = group_ref[image]
        tall, wide = (
            jnp.where(group == 0, SIZES[0][k], jnp.where(group == 1, SIZES[1][k], SIZES[2][k])) for k in range(2)
        )
        end = start + tall * wide
        member = (windows >= start) & (windows < end)
        base, height, width = (
            jnp.where(member, new, old) for new, old in ((start, base), (tall, height), (wide, width))
        )
        start = end
    inside = width > 0
    position = windows - base
    row = jnp.zeros(shape, jnp.int32)
    for tall, wide in SIZES:
        quotient = jnp.floor((position.astype(F32) + 0.5) * (1.0 / wide)).astype(jnp.int32)
        row = jnp.where(width == wide, quotient, row)
    column = position - row * width
    masks = [
        width == WIDTHS[0],
        width == WIDTHS[1],
        inside & (row > 0),
        inside & (row < height - 1),
        inside & (column > 0),
        inside & (column < width - 1),
        (local >= 0) & (local < count),
    ]
    lane = lax.broadcasted_iota(jnp.int32, (shape[0], LANE), 1)
    table = (lane - M_HIT == switch_ref[...]).astype(F32)
    for k, mask in enumerate(masks):
        table = jnp.where((lane == k) & mask, 1.0, table)
    mask_ref[...] = table


def split_planes(stream_ref, wide_ref, count):
    wide_ref[: 4 * count] = stream_ref[...].astype(F32)
    wide_ref[4 * count :] = jnp.zeros((wide_ref.shape[0] - 4 * count, LANE), F32)


def plane(wide_ref, q):
    return wide_ref[pl.ds(q, wide_ref.shape[0] // 4, stride=4), :]


def set_plane(wide_ref, q, low, block):
    wide_ref[pl.ds(4 * low + q, block.shape[0], stride=4), :] = block


def mask_of(mask_ref, which, low, count):
    return mask_ref[low : low + count, which : which + 1] > 0.5


def by_width(mask_ref, low, count, shifted):
    return jnp.where(
        mask_of(mask_ref, M_W0, low, count),
        shifted(WIDTHS[0]),
        jnp.where(mask_of(mask_ref, M_W1, low, count), shifted(WIDTHS[1]), shifted(WIDTHS[2])),
    )


def smooth_max(blocks):
    total = sum(jnp.exp(block) for block in blocks)
    return jnp.log(total * 0.25)


def row_peers(rows):
    here = lax.axis_index("rows")
    there = lax.axis_index("grp")
    order = sorted(range(1, rows), key=lambda k: -min(k, rows - k))
    return [(lax.rem(here + k, rows), there) for k in order]


def grp_peers():
    here = lax.axis_index("rows")
    mine = lax.axis_index("grp")
    half, core = mine // 2, lax.rem(mine, 2)
    return (here, half * 2 + 1 - core), (here, (1 - half) * 2 + core)


def greet(peers):
    barrier = pltpu.get_barrier_semaphore()
    for peer in peers:
        pl.semaphore_signal(barrier, inc=1, device_id=peer, device_id_type=MESH)
    pl.semaphore_wait(barrier, len(peers))


def remote(src, dst, send, recv, peer):
    return pltpu.make_async_remote_copy(
        src_ref=src, dst_ref=dst, send_sem=send, recv_sem=recv, device_id=peer, device_id_type=MESH
    )


def sums_copies(rows, buf, send, recv):
    return [
        remote(buf.at[0], buf.at[k + 1], send.at[k], recv.at[k], peer) for k, peer in enumerate(row_peers(rows))
    ]


def send_sums(rows, own, buf, send, recv):
    buf[0] = own
    for copy in sums_copies(rows, buf, send, recv):
        copy.start()


def add_sums(rows, buf, send, recv):
    for copy in sums_copies(rows, buf, send, recv):
        copy.wait()
    total = buf[0]
    for k in range(1, rows):
        total = total + buf[k]
    return total


def row_parts(padded, count):
    tail = (count - EDGE) // 16 * 16
    parts = [(0, EDGE), (tail, padded - tail)]
    start, steps = EDGE, 3
    for k in range(steps):
        size = min(ceil_to(-(-(tail - start) // (steps - k)), 16), tail - start)
        parts.append((start, size))
        start += size
    return parts


def lanes_of(block):
    return pl.ds(pl.multiple_of(block * LANE, LANE), LANE)


class Gather:
    def __init__(self, rows, shard, buf, send, recv, pass_send, pass_recv):
        self.shard, self.buf = shard, buf
        self.far = rows // 2
        here, there = lax.axis_index("rows"), lax.axis_index("grp")
        self.high, self.low = here // 2, lax.rem(here, 2)
        self.there = there
        self.send, self.recv, self.pass_send, self.pass_recv = send, recv, pass_send, pass_recv

    def rows_of(self, step, low):
        block = lax.rem(self.high + step, self.far) * 2 + low
        return pl.ds(pl.multiple_of(block * self.shard, 16), self.shard)

    def block(self, layer, step, piece):
        lanes = slice(None) if piece is None else slice(piece * 3 * LANE, (piece + 1) * 3 * LANE)
        slot = layer if piece is None else piece
        return self.buf.at[layer, self.rows_of(step, self.low), lanes], slot

    def spread(self, layer, step, piece=None):
        own, slot = self.block(layer, 0, piece)
        peer = (lax.rem(self.high + step, self.far) * 2 + self.low, self.there)
        k = step - 1
        return remote(own, own, self.send.at[slot, k], self.recv.at[slot, k], peer)

    def across(self, layer, step, piece=None):
        part, slot = self.block(layer, self.far - step, piece)
        peer = (self.high * 2 + 1 - self.low, self.there)
        return remote(part, part, self.pass_send.at[slot, step], self.pass_recv.at[slot, step], peer)

    def start(self, layer, piece=None):
        for step in range(1, self.far):
            self.spread(layer, step, piece).start()
        self.across(layer, 0, piece).start()

    def forward(self, layer, step, piece=None):
        self.spread(layer, step, piece).wait_recv()
        self.across(layer, step, piece).start()

    def wait(self, layer, piece=None):
        for step in range(self.far):
            self.across(layer, step, piece).wait_recv()

    def drain(self, layer, piece=None):
        for step in range(1, self.far):
            self.spread(layer, step, piece).wait_send()
        for step in range(self.far):
            self.across(layer, step, piece).wait_send()


class Scatter:
    def __init__(self, rows, shard, grads, first, second, third, total, outs, send, recv, far_send, far_recv):
        self.shard, self.grads, self.first, self.second, self.third = shard, grads, first, second, third
        self.total, self.outs, self.far = total, outs, rows // 2
        here, self.there = lax.axis_index("rows"), lax.axis_index("grp")
        self.high, self.low = here // 2, lax.rem(here, 2)
        self.send, self.recv, self.far_send, self.far_recv = send, recv, far_send, far_recv

    def rows_of(self, step, low):
        block = lax.rem(self.high + step, self.far) * 2 + low
        return pl.ds(pl.multiple_of(block * self.shard, 16), self.shard)

    def across(self, turn, step):
        slot = lax.rem(turn, 3)
        peer = (self.high * 2 + 1 - self.low, self.there)
        return remote(
            self.grads.at[slot, self.rows_of(step, 1 - self.low), :], self.first.at[slot, step],
            self.send.at[slot, step], self.recv.at[slot, step], peer,
        )

    def spread(self, turn, step):
        slot = lax.rem(turn, 3)
        peer = (lax.rem(self.high + step, self.far) * 2 + self.low, self.there)
        k = step - 1
        return remote(
            self.second.at[slot, k], self.third.at[slot, k],
            self.far_send.at[slot, k], self.far_recv.at[slot, k], peer,
        )

    def order(self):
        return list(range(1, self.far)) + [0]

    def start(self, turn):
        for step in self.order():
            self.across(turn, step).start()

    def forward(self, turn, step):
        slot = lax.rem(turn, 3)
        self.across(turn, step).wait_recv()
        own = self.grads[slot, self.rows_of(step, self.low), :]
        total = own.astype(F32) + self.first[slot, step].astype(F32)
        if step == 0:
            self.total[slot] = total
        else:
            self.second[slot, step - 1] = total.astype(BF16)
            self.spread(turn, step).start()

    def finish(self, turn, layer):
        slot = lax.rem(turn, 3)
        total = self.total[slot]
        for step in range(1, self.far):
            self.spread(turn, step).wait_recv()
            total = total + self.third[slot, step - 1].astype(F32)
        depth = self.outs[0].shape[0]

        def put(out, index):
            for block in range(9):
                out[index, 8 - block] = total[:, block * LANE : (block + 1) * LANE]

        @pl.when(layer < depth)
        def _():
            put(self.outs[0], layer)

        @pl.when(layer >= depth)
        def _():
            put(self.outs[1], layer - depth)

    def drain(self, turn):
        for step in range(self.far):
            self.across(turn, step).wait_send()
        for step in range(1, self.far):
            self.spread(turn, step).wait_send()


def each(count, body):
    lax.fori_loop(0, count, lambda i, carry: (body(i), carry)[1], 0)


def forward_kernel(
    inside, layers, rows, count, padded, pixels, group_ref, switch_ref, v_ref, gb_ref, *refs
):
    w_refs, refs = refs[: 1 + inside], refs[1 + inside :]
    (
        next_ref, stat_ref, mask_ref, z_out, full_out, w_out,
        vbuf, wbuf, zbuf, yext, over, under, wide, to_next, to_prev, from_prev, from_next, sums,
        core_s, core_r, x_s, x_r, fwd_s, fwd_r, halo_s, halo_r, sum_s, sum_r, out_sem,
        w_s, w_r, wp_s, wp_r, first_s, first_r, first_ps, first_pr,
    ) = refs
    mine, here = lax.axis_index("grp"), lax.axis_index("rows")
    half = mine // 2
    partner, across = grp_peers()
    parts = row_parts(padded, count)
    own_lanes, far_lanes = lanes_of(mine), lanes_of(across[1])
    own_base = pl.multiple_of(half * 2 * LANE, 2 * LANE)
    far_base = pl.multiple_of((1 - half) * 2 * LANE, 2 * LANE)
    shard = wbuf.shape[1] // rows
    gather = Gather(rows, shard, wbuf, w_s, w_r, wp_s, wp_r)
    first_gather = Gather(rows, shard, wbuf, first_s, first_r, first_ps, first_pr)

    def slab(layer, k, lanes):
        low, size = parts[k]
        return vbuf.at[layer, :, pl.ds(low, size), lanes]

    def to_core(layer, k):
        piece = slab(layer, k, own_lanes)
        return remote(piece, piece, core_s.at[layer, k], core_r.at[layer, k], partner)

    def to_far(layer, k):
        piece = slab(layer, k, own_lanes)
        return remote(piece, piece, x_s.at[layer, k], x_r.at[layer, k], across)

    def pass_on(layer, k):
        piece = slab(layer, k, far_lanes)
        return remote(piece, piece, fwd_s.at[layer, k], fwd_r.at[layer, k], partner)

    def load(layer):
        return pltpu.make_async_copy(w_refs[0].at[layer], wbuf.at[layer], w_s.at[layer, 0])

    def save(layer, which):
        pairs = [(vbuf, full_out), (zbuf, z_out), (wbuf, w_out)]
        src, dst = pairs[which]
        return pltpu.make_async_copy(src.at[layer], dst.at[layer], out_sem.at[layer, which])

    after = (lax.rem(here + 1, rows), mine)
    before = (lax.rem(here + rows - 1, rows), mine)
    down = remote(to_next, from_prev, halo_s.at[0], halo_r.at[0], after)
    up = remote(to_prev, from_next, halo_s.at[1], halo_r.at[1], before)

    def add_products(layer, low, size, base, touched):
        for q in range(4):
            a, b = q // 2, q % 2
            left = vbuf[layer, q, low : low + size, pl.ds(base, 2 * LANE)]
            for step in range(3):
                right = wbuf[layer, pl.ds(base, 2 * LANE), step * 3 * LANE : (step + 1) * 3 * LANE]
                product = jnp.dot(left, right, preferred_element_type=F32)
                for column in range(3):
                    spot = (a + step) * 4 + b + column
                    block = product[:, column * LANE : (column + 1) * LANE]
                    where = (slice(EDGE + low, EDGE + low + size), slice(spot * LANE, (spot + 1) * LANE))
                    if spot in touched:
                        yext[where] += block
                    else:
                        yext[where] = block
                        touched.add(spot)

    def at(low, size, spot):
        return yext[low : low + size, spot * LANE : (spot + 1) * LANE]

    greet([partner, across] + row_peers(rows))
    if inside:
        own_rows = gather.rows_of(0, gather.low)
        for layer in range(layers):
            source = w_refs[layer // (layers // 2)]
            for block in range(9):
                lanes = slice(block * LANE, (block + 1) * LANE)
                wbuf[layer, own_rows, lanes] = source[layer % (layers // 2), 8 - block]
            if layer == 0:
                for piece in range(3):
                    first_gather.start(0, piece)
    else:
        load(0).start()
    split_planes(v_ref, wide, count)
    for q in range(4):
        vbuf[0, q, :, own_lanes] = plane(wide, q).astype(BF16)
    for k in range(len(parts)):
        to_far(0, k).start()
        to_core(0, k).start()
    yext[:EDGE, :] = jnp.zeros((EDGE, yext.shape[1]), F32)
    yext[EDGE + padded :, :] = jnp.zeros((EDGE, yext.shape[1]), F32)
    fill_masks(group_ref, here * count, count, padded, switch_ref, mask_ref)
    if inside:
        for piece in range(3):
            for step in range(1, rows // 2):
                first_gather.forward(0, step, piece)
        for piece in range(3):
            first_gather.wait(0, piece)

    def layer_step(layer):
        more = layer + 1 < layers
        if inside:
            @pl.when(layer > 0)
            def _():
                gather.wait(layer)

            save(layer, 2).start()

            @pl.when(more)
            def _():
                gather.start(layer + 1)
        else:
            load(layer).wait()

            @pl.when(more)
            def _():
                load(layer + 1).start()

        for k in range(len(parts)):
            to_core(layer, k).wait_recv()
        add_products(layer, 0, padded, own_base, set())

        def gather_forward(first, end):
            @pl.when(more)
            def _():
                for step in range(first, end):
                    gather.forward(layer + 1, step)

        def far_products(k):
            pass_on(layer, k).wait_recv()
            low, size = parts[k]
            add_products(layer, low, size, far_base, set(range(16)))
            if k != 1:
                return
            for lane, spot in enumerate((12, 13, 14, 15, 7, 11)):
                to_next[:, lane * LANE : (lane + 1) * LANE] = at(count, EDGE, spot).astype(BF16)
            for lane, spot in enumerate((0, 1, 2, 3, 4, 8)):
                to_prev[:, lane * LANE : (lane + 1) * LANE] = at(EDGE, EDGE, spot).astype(BF16)

            @pl.when(here + 1 < rows)
            def _():
                down.start()

            @pl.when(here > 0)
            def _():
                up.start()

        for k in range(len(parts)):
            to_far(layer, k).wait_recv()
            pass_on(layer, k).start()
            if k > 0:
                far_products(k - 1)
            if inside and k == 2:
                gather_forward(1, 2)
        far_products(len(parts) - 1)
        save(layer, 0).start()
        if inside:
            gather_forward(2, rows // 2)

        @pl.when(here > 0)
        def _():
            down.wait_recv()
            up.wait_send()
            for lane, spot in enumerate((12, 13, 14, 15, 7, 11)):
                received = from_prev[:, lane * LANE : (lane + 1) * LANE].astype(F32)
                yext[:EDGE, spot * LANE : (spot + 1) * LANE] = received

        @pl.when(here + 1 < rows)
        def _():
            up.wait_recv()
            down.wait_send()
            for lane, spot in enumerate((0, 1, 2, 3, 4, 8)):
                received = from_next[:, lane * LANE : (lane + 1) * LANE].astype(F32)
                yext[EDGE + count : 2 * EDGE + count, spot * LANE : (spot + 1) * LANE] = received

        low, size = 8, padded + 2 * EDGE - 16
        go_left = mask_of(mask_ref, M_LEFT, low, size)
        go_right = mask_of(mask_ref, M_RIGHT, low, size)
        for kept, first in ((over, 12), (under, 0)):
            kept[low : low + size, :LANE] = at(low, size, first + 1) + jnp.where(
                go_left, at(low - 1, size, first + 3), 0.0
            )
            kept[low : low + size, LANE:] = at(low, size, first + 2) + jnp.where(
                go_right, at(low + 1, size, first), 0.0
            )
        go_left = mask_of(mask_ref, M_LEFT, EDGE, padded)
        go_right = mask_of(mask_ref, M_RIGHT, EDGE, padded)
        valid = mask_of(mask_ref, M_VALID, EDGE, padded)
        total = jnp.zeros((1, LANE), F32)
        squares = jnp.zeros((1, LANE), F32)
        for q in range(4):
            a, b = q // 2, q % 2
            lanes = slice(b * LANE, (b + 1) * LANE)
            kept, sign = (over, -1) if a == 0 else (under, 1)
            rowwise = by_width(
                mask_ref, EDGE, padded,
                lambda w: kept[EDGE + sign * w : EDGE + sign * w + padded, lanes],
            )
            z = at(EDGE, padded, (a + 1) * 4 + b + 1)
            z = z + jnp.where(mask_of(mask_ref, (M_UP, M_DOWN)[a], EDGE, padded), rowwise, 0.0)
            if b == 0:
                z = z + jnp.where(go_left, at(EDGE - 1, padded, (a + 1) * 4 + 3), 0.0)
            else:
                z = z + jnp.where(go_right, at(EDGE + 1, padded, (a + 1) * 4), 0.0)
            z = jnp.where(valid, z, 0.0)
            zbuf[layer, q] = z
            total = total + jnp.sum(z, axis=0, keepdims=True)
            squares = squares + jnp.sum(z * z, axis=0, keepdims=True)
        save(layer, 1).start()
        own = jnp.concatenate([total, squares, jnp.zeros((6, LANE), F32)], axis=0)
        channel = (sums.at[layer], sum_s.at[layer], sum_r.at[layer])
        send_sums(rows, own, *channel)
        both = add_sums(rows, *channel)
        mean = both[0:1] / pixels
        inverse = lax.rsqrt(both[1:2] / pixels - mean * mean + EPSILON)
        stat_ref[layer] = jnp.concatenate([mean, inverse, jnp.zeros((6, LANE), F32)], axis=0)

        def activation(k, q):
            low, size = parts[k]
            y = gb_ref[layer, 0:1] * ((zbuf[layer, q, low : low + size] - mean) * inverse) + gb_ref[layer, 1:2]
            return y * jax.nn.sigmoid(y)

        def kept(k, which):
            low, size = parts[k]
            return mask_of(mask_ref, which, EDGE + low, size)

        def pass_to_next(of_part):
            for k, (low, size) in enumerate(parts):
                blocks = of_part(k)
                for q in range(4):
                    vbuf[layer + 1, q, low : low + size, own_lanes] = blocks[q].astype(BF16)
                to_far(layer + 1, k).start()
                to_core(layer + 1, k).start()

        def plain(k):
            return [jnp.where(kept(k, M_VALID), activation(k, q), 0.0) for q in range(4)]

        def unpooled(k):
            pooled = smooth_max([activation(k, q) for q in range(4)])
            return [jnp.where(kept(k, M_HIT + q), pooled, 0.0) for q in range(4)]

        @pl.when(jnp.logical_and(more, layer != POOL))
        def _():
            pass_to_next(plain)

        @pl.when(layer == POOL)
        def _():
            pass_to_next(unpooled)

        @pl.when(layer + 1 == layers)
        def _():
            for k, (low, size) in enumerate(parts):
                for q, block in enumerate(plain(k)):
                    set_plane(wide, q, low, block)
            next_ref[...] = wide[: 4 * count].astype(BF16)

    each(layers, layer_step)

    def drain(layer):
        for k in range(len(parts)):
            to_far(layer, k).wait_send()
            to_core(layer, k).wait_send()
            pass_on(layer, k).wait_send()
        if inside:

            @pl.when(layer > 0)
            def _():
                gather.drain(layer)

        for which in range(3 if inside else 2):
            save(layer, which).wait()

    each(layers, drain)
    if inside:
        for piece in range(3):
            first_gather.drain(0, piece)


def backward_kernel(inside, layers, rows, count, padded, pixels, *refs):
    refs = list(refs)
    g_ref, stat_ref, gb_ref, mask_ref, z_in, full_in, w_in = refs[:7]
    del refs[:7]
    out_ref, gbgrad_ref = refs[:2]
    wgrad_refs = refs[2 : 3 + inside]
    del refs[: 3 + inside]
    (
        grad_ref, wide, zbuf, fbuf, wbuf, dk, gy, gext, above, below, patch, part, keep, core_out, core_in, x_out, x_in,
        to_next, to_prev, from_prev, from_next, sums,
        core_s, core_r, x_s, x_r, halo_s, halo_r, sum_s, sum_r, load_sem, out_sem,
    ) = refs[:32]
    mine, here = lax.axis_index("grp"), lax.axis_index("rows")
    half, core = mine // 2, lax.rem(mine, 2)
    partner, across = grp_peers()
    own_lanes, other_lanes = lanes_of(core), lanes_of(1 - core)
    own_base = pl.multiple_of(half * 2 * LANE, 2 * LANE)
    far_base = pl.multiple_of((1 - half) * 2 * LANE, 2 * LANE)
    if inside:
        first, second, third, total_ref, s1, r1, s2, r2 = refs[32:]
        shard = dk.shape[1] // rows
        scatter = Scatter(rows, shard, dk, first, second, third, total_ref, wgrad_refs, s1, r1, s2, r2)

    def load(turn, which):
        src, dst = ((z_in, zbuf), (w_in, wbuf), (full_in, fbuf))[which]
        side = lax.rem(turn, 2)
        return pltpu.make_async_copy(src.at[layers - 1 - turn], dst.at[side], load_sem.at[side, which])

    def save(turn):
        slot = lax.rem(turn, 3)
        return pltpu.make_async_copy(dk.at[slot], wgrad_refs[0].at[layers - 1 - turn], out_sem.at[slot])

    for turn in range(2):
        for which in range(3):
            load(turn, which).start()
    after = (lax.rem(here + 1, rows), mine)
    before = (lax.rem(here + rows - 1, rows), mine)
    split_planes(g_ref, wide, count)
    for q in range(4):
        grad_ref[q] = plane(wide, q)
    gext[:EDGE, :] = jnp.zeros((EDGE, 4 * LANE), F32)
    gext[EDGE + padded :, :] = jnp.zeros((EDGE, 4 * LANE), F32)
    greet([partner, across] + row_peers(rows))

    def taps(q, step):
        first = (q // 2 + step) * 4 + q % 2
        return patch[:, first * LANE : (first + 3) * LANE]

    def layer_step(turn):
        layer = layers - 1 - turn
        side, slot = lax.rem(turn, 2), lax.rem(turn, 3)
        last = turn + 1 == layers
        mean, inverse = stat_ref[layer, 0:1], stat_ref[layer, 1:2]
        gain, shift = gb_ref[layer, 0:1], gb_ref[layer, 1:2]
        valid = mask_of(mask_ref, M_VALID, EDGE, padded)
        load(turn, 0).wait()
        down = remote(to_next, from_prev.at[side], halo_s.at[0], halo_r.at[side, 0], after)
        up = remote(to_prev, from_next.at[side], halo_s.at[1], halo_r.at[side, 1], before)

        def shifted(q):
            normed = (zbuf[side, q] - mean) * inverse
            return normed, gain * normed + shift

        @pl.when(layer == POOL)
        def _():
            pooled_grad = jnp.zeros((padded, LANE), F32)
            for q in range(4):
                pooled_grad = jnp.where(mask_of(mask_ref, M_HIT + q, EDGE, padded), grad_ref[q], pooled_grad)
            blocks = []
            for q in range(4):
                _, y = shifted(q)
                gy[q] = y * jax.nn.sigmoid(y)
            pooled = smooth_max([gy[q] for q in range(4)])
            for q in range(4):
                grad_ref[q] = pooled_grad * (jnp.exp(gy[q] - pooled) * 0.25)

        shift_sum = jnp.zeros((1, LANE), F32)
        gain_sum = jnp.zeros((1, LANE), F32)
        for q in range(4):
            normed, y = shifted(q)
            s = jax.nn.sigmoid(y)
            grad = jnp.where(valid, grad_ref[q] * s * (1.0 + y * (1.0 - s)), 0.0)
            gy[q] = grad
            shift_sum = shift_sum + jnp.sum(grad, axis=0, keepdims=True)
            gain_sum = gain_sum + jnp.sum(grad * normed, axis=0, keepdims=True)

        def spread(buf, low, planes):
            for lane, q in enumerate(planes):
                piece = slice(low, low + EDGE)
                normed = (zbuf[side, q, piece] - mean) * inverse
                buf[:, 2 * lane * LANE : (2 * lane + 1) * LANE] = gy[q, piece].astype(BF16)
                buf[:, (2 * lane + 1) * LANE : (2 * lane + 2) * LANE] = normed.astype(BF16)

        spread(to_next, count - EDGE, (2, 3, 1))
        spread(to_prev, 0, (0, 1, 2))

        @pl.when(here + 1 < rows)
        def _():
            down.start()

        @pl.when(here > 0)
        def _():
            up.start()

        own = jnp.concatenate([shift_sum, gain_sum, jnp.zeros((6, LANE), F32)], axis=0)
        channel = (sums.at[side], sum_s.at[side], sum_r.at[side])
        send_sums(rows, own, *channel)
        if inside:

            @pl.when(turn > 0)
            def _():
                scatter.start(turn - 1)

        both = add_sums(rows, *channel)
        gbgrad_ref[layer] = both

        def conv_grad(grad, normed):
            out = inverse * gain * (grad - both[0:1] / pixels - normed * both[1:2] / pixels)
            return out.astype(BF16).astype(F32)

        for q in range(4):
            normed, _ = shifted(q)
            gext[EDGE : EDGE + padded, q * LANE : (q + 1) * LANE] = jnp.where(
                valid, conv_grad(gy[q], normed), 0.0
            )

        def receive(buf, low, planes):
            for lane, q in enumerate(planes):
                grad = buf[side, :, 2 * lane * LANE : (2 * lane + 1) * LANE].astype(F32)
                normed = buf[side, :, (2 * lane + 1) * LANE : (2 * lane + 2) * LANE].astype(F32)
                gext[low : low + EDGE, q * LANE : (q + 1) * LANE] = conv_grad(grad, normed)

        @pl.when(here > 0)
        def _():
            down.wait_recv()
            up.wait_send()
            receive(from_prev, 0, (2, 3, 1))

        @pl.when(here + 1 < rows)
        def _():
            up.wait_recv()
            down.wait_send()
            receive(from_next, EDGE + count, (0, 1, 2))

        low, size = EDGE - 8, padded + 16
        for kept, which, sign, lanes in (
            (above, M_UP, -1, slice(2 * LANE, 4 * LANE)),
            (below, M_DOWN, 1, slice(0, 2 * LANE)),
        ):
            rowwise = by_width(
                mask_ref, low, size, lambda w: gext[low + sign * w : low + sign * w + size, lanes]
            )
            kept[...] = jnp.where(mask_of(mask_ref, which, low, size), rowwise, 0.0)
        go_left = mask_of(mask_ref, M_LEFT, EDGE, padded)
        go_right = mask_of(mask_ref, M_RIGHT, EDGE, padded)
        for step, (kept, top, lane) in enumerate(
            ((above, 8, 0), (gext, EDGE, 0), (gext, EDGE, 2 * LANE), (below, 8, 0))
        ):
            even, odd = slice(lane, lane + LANE), slice(lane + LANE, lane + 2 * LANE)
            blocks = [
                jnp.where(go_left, kept[top - 1 : top - 1 + padded, odd], 0.0),
                kept[top : top + padded, even],
                kept[top : top + padded, odd],
                jnp.where(go_right, kept[top + 1 : top + 1 + padded, even], 0.0),
            ]
            for column, block in enumerate(blocks):
                spot = step * 4 + column
                patch[:, spot * LANE : (spot + 1) * LANE] = block.astype(BF16)

        def kernel_grad():
            for step in range(3):
                total = None
                for q in range(4):
                    product = lax.dot_general(
                        fbuf[side, q], taps(q, step), (((0,), (0,)), ((), ())), preferred_element_type=F32
                    )
                    total = product if total is None else total + product
                dk[slot, :, step * 3 * LANE : (step + 1) * 3 * LANE] = total.astype(BF16)
            if not inside:
                save(turn).start()

        def scatter_forward(step):
            @pl.when(turn > 0)
            def _():
                scatter.forward(turn - 1, step)

        if inside:

            @pl.when(turn > 1)
            def _():
                scatter.finish(turn - 2, layer + 2)
                scatter.drain(turn - 2)

            scatter_forward(1)
        load(turn, 1).wait()
        load(turn, 2).wait()
        if not inside:

            @pl.when(turn > 2)
            def _():
                save(turn - 3).wait()

        @pl.when(last)
        def _():
            kernel_grad()
            if inside:
                scatter.start(turn)

        def input_grad(q, base):
            total = None
            for step in range(3):
                right = wbuf[side, pl.ds(base, 2 * LANE), step * 3 * LANE : (step + 1) * 3 * LANE]
                product = lax.dot_general(
                    taps(q, step), right, (((1,), (1,)), ((), ())), preferred_element_type=F32
                )
                total = product if total is None else total + product
            part[...] = total

        def to_core(spot):
            return remote(
                core_out.at[side, spot], core_in.at[side, spot],
                core_s.at[side, spot], core_r.at[side, spot], partner,
            )

        def to_far(q):
            return remote(x_out.at[side, q], x_in.at[side, q], x_s.at[side, q], x_r.at[side, q], across)

        def send_across(q):
            to_core(q).wait_recv()
            x_out[side, q] = (keep[q] + core_in[side, q].astype(F32)).astype(BF16)
            to_far(q).start()

        for spot in range(8):
            input_grad(spot % 4, far_base if spot < 4 else own_base)
            core_out[side, spot] = part[:, other_lanes].astype(BF16)
            keep[spot] = part[:, own_lanes]
            to_core(spot).start()
            if 2 <= spot < 6:
                send_across(spot - 2)
            if inside and spot == 5:
                scatter_forward(2)

        @pl.when(jnp.logical_not(last))
        def _():
            kernel_grad()

        @pl.when(turn + 2 < layers)
        def _():
            for which in range(3):
                load(turn + 2, which).start()

        if inside:
            for step in range(3, rows // 2):
                scatter_forward(step)
            scatter_forward(0)
        for q in range(4):
            to_core(4 + q).wait_recv()
            to_far(q).wait_recv()
            grad_ref[q] = keep[4 + q] + core_in[side, 4 + q].astype(F32) + x_in[side, q].astype(F32)
        for spot in range(8):
            to_core(spot).wait_send()
        for q in range(4):
            to_far(q).wait_send()

    each(layers, layer_step)
    for q in range(4):
        set_plane(wide, q, 0, grad_ref[q])
    out_ref[...] = wide[: 4 * count].astype(BF16)
    if inside:
        for step in scatter.order():
            scatter.forward(layers - 1, step)
        for turn in (layers - 2, layers - 1):
            scatter.finish(turn, layers - 1 - turn)
            scatter.drain(turn)
    else:
        for turn in range(layers - 3, layers):
            save(turn).wait()


VM = pl.BlockSpec(memory_space=pltpu.VMEM)
HBM = pl.BlockSpec(memory_space=pl.ANY)
LIMIT = 56 * 1024 * 1024
DMA = pltpu.SemaphoreType.DMA


def forward_block(inside, rows, count, padded, pixels, image_group, switches, features, pairs, weights):
    layers, channels, taps = pairs.shape[0], 4 * LANE, 9 * LANE
    ext = padded + 2 * EDGE
    n_parts = len(row_parts(padded, count))
    far = rows // 2
    shape = jax.ShapeDtypeStruct
    out = pl.pallas_call(
        functools.partial(forward_kernel, inside, layers, rows, count, padded, pixels),
        name="forward_block",
        out_shape=(
            shape((4 * count, LANE), BF16),
            shape((layers, 8, LANE), F32),
            shape((ext, LANE), F32),
            shape((layers, 4, padded, LANE), F32),
            shape((layers, 4, padded, channels), BF16),
            shape((layers, channels, taps) if inside else (1, 16, LANE), BF16),
        ),
        in_specs=[pl.BlockSpec(memory_space=pltpu.SMEM), VM, VM, VM] + [VM if inside else HBM] * len(weights),
        out_specs=(VM, VM, VM, HBM, HBM, HBM),
        scratch_shapes=[
            pltpu.VMEM((layers, 4, padded, channels), BF16),
            pltpu.VMEM((layers, channels, taps), BF16),
            pltpu.VMEM((layers, 4, padded, LANE), F32),
            pltpu.VMEM((ext, 16 * LANE), F32),
            pltpu.VMEM((ext, 2 * LANE), F32),
            pltpu.VMEM((ext, 2 * LANE), F32),
            pltpu.VMEM((4 * padded, LANE), F32),
        ]
        + [pltpu.VMEM((EDGE, 6 * LANE), BF16)] * 4
        + [pltpu.VMEM((layers, rows, 8, LANE), F32)]
        + [DMA((layers, n_parts))] * 6
        + [DMA((2,))] * 2
        + [DMA((layers, rows - 1))] * 2
        + [DMA((layers, 3))]
        + [DMA((layers, far - 1))] * 2
        + [DMA((layers, far))] * 2
        + [DMA((3, far - 1))] * 2
        + [DMA((3, far))] * 2,
        compiler_params=pltpu.CompilerParams(
            collective_id=0, has_side_effects=True, vmem_limit_bytes=LIMIT
        ),
    )(image_group, switches, features, pairs, *weights)
    return out[:5] + ((out[5] if inside else weights[0]),)


def backward_block(inside, rows, count, padded, pixels, grad, z, stat, pairs, masks, full, weight):
    layers, channels, taps = weight.shape
    ext = padded + 2 * EDGE
    shard = channels // rows
    far = rows // 2
    shape = jax.ShapeDtypeStruct
    scratch = [
        pltpu.VMEM((4, padded, LANE), F32),
        pltpu.VMEM((4 * padded, LANE), F32),
        pltpu.VMEM((2, 4, padded, LANE), F32),
        pltpu.VMEM((2, 4, padded, channels), BF16),
        pltpu.VMEM((2, channels, taps), BF16),
        pltpu.VMEM((3, channels, taps), BF16),
        pltpu.VMEM((4, padded, LANE), F32),
        pltpu.VMEM((ext, 4 * LANE), F32),
        pltpu.VMEM((padded + 16, 2 * LANE), F32),
        pltpu.VMEM((padded + 16, 2 * LANE), F32),
        pltpu.VMEM((padded, 16 * LANE), BF16),
        pltpu.VMEM((padded, 2 * LANE), F32),
        pltpu.VMEM((8, padded, LANE), F32),
        pltpu.VMEM((2, 8, padded, LANE), BF16),
        pltpu.VMEM((2, 8, padded, LANE), BF16),
        pltpu.VMEM((2, 4, padded, LANE), BF16),
        pltpu.VMEM((2, 4, padded, LANE), BF16),
    ]
    scratch += [pltpu.VMEM((EDGE, 6 * LANE), BF16)] * 2 + [pltpu.VMEM((2, EDGE, 6 * LANE), BF16)] * 2
    scratch += [pltpu.VMEM((2, rows, 8, LANE), F32)]
    scratch += [DMA((2, 8))] * 2 + [DMA((2, 4))] * 2 + [DMA((2,)), DMA((2, 2))] + [DMA((2, rows - 1))] * 2
    scratch += [DMA((2, 3)), DMA((3,))]
    wgrads = [shape((layers, channels, taps), BF16)]
    if inside:
        wgrads = [shape((layers // 2, 9, shard, LANE), F32)] * 2
        scratch += [
            pltpu.VMEM((3, far, shard, taps), BF16),
            pltpu.VMEM((3, far - 1, shard, taps), BF16),
            pltpu.VMEM((3, far - 1, shard, taps), BF16),
            pltpu.VMEM((3, shard, taps), F32),
        ]
        scratch += [DMA((3, far))] * 2 + [DMA((3, far - 1))] * 2
    return pl.pallas_call(
        functools.partial(backward_kernel, inside, layers, rows, count, padded, pixels),
        name="backward_block",
        out_shape=[shape((4 * count, LANE), BF16), shape((layers, 8, LANE), F32)] + wgrads,
        in_specs=[VM] * 4 + [HBM] * 3,
        out_specs=[VM, VM] + [VM if inside else HBM] * len(wgrads),
        scratch_shapes=scratch,
        compiler_params=pltpu.CompilerParams(
            collective_id=1, has_side_effects=True, vmem_limit_bytes=LIMIT
        ),
    )(grad, stat, pairs, masks, z, full, weight)


def shards(
    features, image_group, switches, enc_weight, dec_weight,
    enc_gain, enc_bias, dec_gain, dec_bias, d_decoded,
):
    rows = lax.axis_size("rows")
    count = features.shape[0] // 4
    padded = ceil_to(count, 16)
    pixels = float(features.shape[0] * rows)
    depth, shard = enc_weight.shape[0], enc_weight.shape[2]
    inside = shard % 16 == 0
    sizes = (rows, count, padded, pixels)
    weights = [enc_weight, dec_weight]
    if not inside:
        both = jnp.concatenate(weights)
        flat = jnp.transpose(both[:, ::-1], (0, 2, 1, 3)).reshape(both.shape[0], shard, -1)
        weights = [lax.all_gather(flat, "rows", axis=1, tiled=True)]
    pairs = jnp.stack([jnp.concatenate([enc_gain, dec_gain]), jnp.concatenate([enc_bias, dec_bias])], axis=1)
    pairs = jnp.pad(pairs, ((0, 0), (0, 6), (0, 0)))

    hits = jnp.pad(switches, (EDGE, padded - count + EDGE), constant_values=-LANE)[:, None]
    decoded, stat, masks, z, full, weight = forward_block(
        inside, *sizes, image_group, hits, features, pairs, weights
    )
    grad, pair_grads, *wgrads = backward_block(
        inside, *sizes, d_decoded, z, stat, pairs, masks, full, weight
    )
    if not inside:
        wgrad = lax.psum_scatter(wgrads[0], "rows", scatter_dimension=1, tiled=True).astype(F32)
        wgrad = jnp.transpose(wgrad.reshape(2 * depth, shard, 9, -1)[:, :, ::-1], (0, 2, 1, 3))
        wgrads = [wgrad[:depth], wgrad[depth:]]
    return (
        decoded,
        grad,
        *wgrads,
        pair_grads[:depth, 1],
        pair_grads[:depth, 0],
        pair_grads[depth:, 1],
        pair_grads[depth:, 0],
    )


def solution(mesh):
    wide = P("rows", "grp")
    kernels = P(None, None, "rows", "grp")
    vector = P(None, "grp")
    return jax.shard_map(
        shards,
        mesh=mesh,
        in_specs=(wide, P(), P("rows"), kernels, kernels, vector, vector, vector, vector, wide),
        out_specs=(wide, wide, kernels, kernels, vector, vector, vector, vector),
        check_vma=False,
    )
```

```python
import functools

import jax
import jax.numpy as jnp
from jax import lax
from jax.experimental import pallas as pl
from jax.experimental.pallas import tpu as pltpu
from jax.sharding import PartitionSpec as P

SIZES = ((15, 20), (18, 24), (30, 40))
WIDTHS = tuple(w for _, w in SIZES)
EDGE = 48
EPSILON = 1e-05
MESH = pl.DeviceIdType.MESH
F32 = jnp.float32
BF16 = jnp.bfloat16
LANE = 128
(M_W0, M_W1, M_UP, M_DOWN, M_LEFT, M_RIGHT, M_VALID, M_HIT) = range(8)
POOL = 2


def ceil_to(value, step):
    return -(-value // step) * step


def fill_masks(group_ref, first_window, count, padded, switch_ref, mask_ref):
    shape = (padded + 2 * EDGE, 1)
    local = lax.broadcasted_iota(jnp.int32, shape, 0) - EDGE
    windows = local + first_window

    start = jnp.int32(0)
    base = height = width = jnp.zeros(shape, jnp.int32)
    for image in range(group_ref.shape[0]):
        group = group_ref[image]
        tall, wide = (
            jnp.where(group == 0, SIZES[0][k], jnp.where(group == 1, SIZES[1][k], SIZES[2][k])) for k in range(2)
        )
        end = start + tall * wide
        member = (windows >= start) & (windows < end)
        base, height, width = (
            jnp.where(member, new, old) for new, old in ((start, base), (tall, height), (wide, width))
        )
        start = end
    inside = width > 0
    position = windows - base
    row = jnp.zeros(shape, jnp.int32)
    for tall, wide in SIZES:
        quotient = jnp.floor((position.astype(F32) + 0.5) * (1.0 / wide)).astype(jnp.int32)
        row = jnp.where(width == wide, quotient, row)
    column = position - row * width
    masks = [
        width == WIDTHS[0],
        width == WIDTHS[1],
        inside & (row > 0),
        inside & (row < height - 1),
        inside & (column > 0),
        inside & (column < width - 1),
        (local >= 0) & (local < count),
    ]
    lane = lax.broadcasted_iota(jnp.int32, (shape[0], LANE), 1)
    table = (lane - M_HIT == switch_ref[...]).astype(F32)
    for k, mask in enumerate(masks):
        table = jnp.where((lane == k) & mask, 1.0, table)
    mask_ref[...] = table


def split_planes(stream_ref, wide_ref, count):
    wide_ref[: 4 * count] = stream_ref[...].astype(F32)
    wide_ref[4 * count :] = jnp.zeros((wide_ref.shape[0] - 4 * count, LANE), F32)


def plane(wide_ref, q):
    return wide_ref[pl.ds(q, wide_ref.shape[0] // 4, stride=4), :]


def set_plane(wide_ref, q, low, block):
    wide_ref[pl.ds(4 * low + q, block.shape[0], stride=4), :] = block


def mask_of(mask_ref, which, low, count):
    return mask_ref[low : low + count, which : which + 1] > 0.5


def by_width(mask_ref, low, count, shifted):
    return jnp.where(
        mask_of(mask_ref, M_W0, low, count),
        shifted(WIDTHS[0]),
        jnp.where(mask_of(mask_ref, M_W1, low, count), shifted(WIDTHS[1]), shifted(WIDTHS[2])),
    )


def smooth_max(blocks):
    total = sum(jnp.exp(block) for block in blocks)
    return jnp.log(total * 0.25)


def row_peers(rows):
    here = lax.axis_index("rows")
    there = lax.axis_index("grp")
    order = sorted(range(1, rows), key=lambda k: -min(k, rows - k))
    return [(lax.rem(here + k, rows), there) for k in order]


def grp_peers():
    here = lax.axis_index("rows")
    mine = lax.axis_index("grp")
    half, core = mine // 2, lax.rem(mine, 2)
    return (here, half * 2 + 1 - core), (here, (1 - half) * 2 + core)


def greet(peers):
    barrier = pltpu.get_barrier_semaphore()
    for peer in peers:
        pl.semaphore_signal(barrier, inc=1, device_id=peer, device_id_type=MESH)
    pl.semaphore_wait(barrier, len(peers))


def remote(src, dst, send, recv, peer):
    return pltpu.make_async_remote_copy(
        src_ref=src, dst_ref=dst, send_sem=send, recv_sem=recv, device_id=peer, device_id_type=MESH
    )


def sums_copies(rows, buf, send, recv):
    return [
        remote(buf.at[0], buf.at[k + 1], send.at[k], recv.at[k], peer) for k, peer in enumerate(row_peers(rows))
    ]


def send_sums(rows, own, buf, send, recv):
    buf[0] = own
    for copy in sums_copies(rows, buf, send, recv):
        copy.start()


def add_sums(rows, buf, send, recv):
    for copy in sums_copies(rows, buf, send, recv):
        copy.wait()
    total = buf[0]
    for k in range(1, rows):
        total = total + buf[k]
    return total


def row_parts(padded, count):
    tail = (count - EDGE) // 16 * 16
    inner, start, steps = [], EDGE, 3
    for k in range(steps):
        size = min(ceil_to(-(-(tail - start) // (steps - k)), 16), tail - start)
        inner.append((start, size))
        start += size
    return [(0, EDGE), (tail, padded - tail), inner[0], inner[2], inner[1]]


REACH = max(WIDTHS) + 1


def far_pieces(parts):
    low, size = parts[4]
    first, last = (low - REACH) // 8 * 8, ceil_to(low + size + REACH, 8)
    return [
        (2, parts[2][0], first - parts[2][0]),
        (3, last, parts[3][0] + parts[3][1] - last),
        (0, *parts[0]),
        (1, *parts[1]),
        (2, first, parts[2][0] + parts[2][1] - first),
        (3, parts[3][0], last - parts[3][0]),
        (4, low, size),
    ]


def lanes_of(block):
    return pl.ds(pl.multiple_of(block * LANE, LANE), LANE)


class Gather:
    def __init__(self, rows, shard, buf, send, recv, pass_send, pass_recv):
        self.shard, self.buf = shard, buf
        self.far = rows // 2
        here, there = lax.axis_index("rows"), lax.axis_index("grp")
        self.high, self.low = here // 2, lax.rem(here, 2)
        self.there = there
        self.send, self.recv, self.pass_send, self.pass_recv = send, recv, pass_send, pass_recv

    def rows_of(self, step, low):
        block = lax.rem(self.high + step, self.far) * 2 + low
        return pl.ds(pl.multiple_of(block * self.shard, 16), self.shard)

    def block(self, layer, step, piece):
        lanes = slice(None) if piece is None else slice(piece * 3 * LANE, (piece + 1) * 3 * LANE)
        slot = layer if piece is None else piece
        return self.buf.at[layer, self.rows_of(step, self.low), lanes], slot

    def spread(self, layer, step, piece=None):
        own, slot = self.block(layer, 0, piece)
        peer = (lax.rem(self.high + step, self.far) * 2 + self.low, self.there)
        k = step - 1
        return remote(own, own, self.send.at[slot, k], self.recv.at[slot, k], peer)

    def across(self, layer, step, piece=None):
        part, slot = self.block(layer, self.far - step, piece)
        peer = (self.high * 2 + 1 - self.low, self.there)
        return remote(part, part, self.pass_send.at[slot, step], self.pass_recv.at[slot, step], peer)

    def start(self, layer, piece=None):
        for step in range(1, self.far):
            self.spread(layer, step, piece).start()
        self.across(layer, 0, piece).start()

    def forward(self, layer, step, piece=None):
        self.spread(layer, step, piece).wait_recv()
        self.across(layer, step, piece).start()

    def wait(self, layer, piece=None):
        for step in range(self.far):
            self.across(layer, step, piece).wait_recv()

    def drain(self, layer, piece=None):
        for step in range(1, self.far):
            self.spread(layer, step, piece).wait_send()
        for step in range(self.far):
            self.across(layer, step, piece).wait_send()


class Scatter:
    def __init__(self, rows, shard, grads, first, second, third, total, outs, send, recv, far_send, far_recv):
        self.shard, self.grads, self.first, self.second, self.third = shard, grads, first, second, third
        self.total, self.outs, self.far = total, outs, rows // 2
        here, self.there = lax.axis_index("rows"), lax.axis_index("grp")
        self.high, self.low = here // 2, lax.rem(here, 2)
        self.send, self.recv, self.far_send, self.far_recv = send, recv, far_send, far_recv

    def rows_of(self, step, low):
        block = lax.rem(self.high + step, self.far) * 2 + low
        return pl.ds(pl.multiple_of(block * self.shard, 16), self.shard)

    def across(self, turn, step):
        slot = lax.rem(turn, 3)
        peer = (self.high * 2 + 1 - self.low, self.there)
        return remote(
            self.grads.at[slot, self.rows_of(step, 1 - self.low), :], self.first.at[slot, step],
            self.send.at[slot, step], self.recv.at[slot, step], peer,
        )

    def spread(self, turn, step):
        slot = lax.rem(turn, 3)
        peer = (lax.rem(self.high + step, self.far) * 2 + self.low, self.there)
        k = step - 1
        return remote(
            self.second.at[slot, k], self.third.at[slot, k],
            self.far_send.at[slot, k], self.far_recv.at[slot, k], peer,
        )

    def order(self):
        return list(range(1, self.far)) + [0]

    def start(self, turn):
        for step in self.order():
            self.across(turn, step).start()

    def forward(self, turn, step):
        slot = lax.rem(turn, 3)
        self.across(turn, step).wait_recv()
        own = self.grads[slot, self.rows_of(step, self.low), :]
        total = own.astype(F32) + self.first[slot, step].astype(F32)
        if step == 0:
            self.total[slot] = total
        else:
            self.second[slot, step - 1] = total.astype(BF16)
            self.spread(turn, step).start()

    def finish(self, turn, layer):
        slot = lax.rem(turn, 3)
        total = self.total[slot]
        for step in range(1, self.far):
            self.spread(turn, step).wait_recv()
            total = total + self.third[slot, step - 1].astype(F32)
        depth = self.outs[0].shape[0]

        def put(out, index):
            for block in range(9):
                out[index, 8 - block] = total[:, block * LANE : (block + 1) * LANE]

        @pl.when(layer < depth)
        def _():
            put(self.outs[0], layer)

        @pl.when(layer >= depth)
        def _():
            put(self.outs[1], layer - depth)

    def drain(self, turn):
        for step in range(self.far):
            self.across(turn, step).wait_send()
        for step in range(1, self.far):
            self.spread(turn, step).wait_send()


def each(count, body):
    lax.fori_loop(0, count, lambda i, carry: (body(i), carry)[1], 0)


def forward_kernel(
    inside, layers, rows, count, padded, pixels, group_ref, switch_ref, v_ref, gb_ref, *refs
):
    w_refs, refs = refs[: 1 + inside], refs[1 + inside :]
    (
        next_ref, stat_ref, mask_ref, z_out, full_out, w_out,
        vbuf, wbuf, zbuf, raw, coef, yext, over, under, wide, to_next, to_prev, from_prev, from_next, sums,
        core_s, core_r, x_s, x_r, fwd_s, fwd_r, halo_s, halo_r, sum_s, sum_r, out_sem,
        coef_s, coef_r, w_s, w_r, wp_s, wp_r, first_s, first_r, first_ps, first_pr,
    ) = refs
    mine, here = lax.axis_index("grp"), lax.axis_index("rows")
    half = mine // 2
    partner, across = grp_peers()
    diagonal = (here, across[1] + partner[1] - mine)
    parts = row_parts(padded, count)
    pieces = far_pieces(parts)
    own_lanes, far_lanes = lanes_of(mine), lanes_of(across[1])
    own_base = pl.multiple_of(half * 2 * LANE, 2 * LANE)
    far_base = pl.multiple_of((1 - half) * 2 * LANE, 2 * LANE)
    shard = wbuf.shape[1] // rows
    gather = Gather(rows, shard, wbuf, w_s, w_r, wp_s, wp_r)
    first_gather = Gather(rows, shard, wbuf, first_s, first_r, first_ps, first_pr)

    def slab(layer, k, lanes):
        low, size = parts[k]
        return raw.at[lax.rem(layer, 2), :, pl.ds(low, size), lanes]

    def to_core(layer):
        whole = raw.at[lax.rem(layer, 2), :, :, own_lanes]
        return remote(whole, whole, core_s.at[layer], core_r.at[layer], partner)

    def to_far(layer, k):
        _, low, size = pieces[k]
        piece = raw.at[lax.rem(layer, 2), :, pl.ds(low, size), own_lanes]
        return remote(piece, piece, x_s.at[layer, k], x_r.at[layer, k], across)

    def pass_on(layer, k):
        piece = slab(layer, k, far_lanes)
        return remote(piece, piece, fwd_s.at[layer, k], fwd_r.at[layer, k], partner)

    def coef_copy(layer, k):
        own = coef.at[lax.rem(layer, 2), mine]
        return remote(own, own, coef_s.at[layer, k], coef_r.at[layer, k], (partner, across, diagonal)[k])

    def load(layer):
        return pltpu.make_async_copy(w_refs[0].at[layer], wbuf.at[layer], w_s.at[layer, 0])

    def save(layer, which):
        pairs = [(vbuf, full_out), (zbuf, z_out), (wbuf, w_out)]
        src, dst = pairs[which]
        return pltpu.make_async_copy(src.at[layer], dst.at[layer], out_sem.at[layer, which])

    after = (lax.rem(here + 1, rows), mine)
    before = (lax.rem(here + rows - 1, rows), mine)
    down = remote(to_next, from_prev, halo_s.at[0], halo_r.at[0], after)
    up = remote(to_prev, from_next, halo_s.at[1], halo_r.at[1], before)

    def add_products(layer, low, size, base, touched):
        for q in range(4):
            a, b = q // 2, q % 2
            left = vbuf[layer, q, low : low + size, pl.ds(base, 2 * LANE)]
            for step in range(3):
                right = wbuf[layer, pl.ds(base, 2 * LANE), step * 3 * LANE : (step + 1) * 3 * LANE]
                product = jnp.dot(left, right, preferred_element_type=F32)
                for column in range(3):
                    spot = (a + step) * 4 + b + column
                    block = product[:, column * LANE : (column + 1) * LANE]
                    where = (slice(EDGE + low, EDGE + low + size), slice(spot * LANE, (spot + 1) * LANE))
                    if spot in touched:
                        yext[where] += block
                    else:
                        yext[where] = block
                        touched.add(spot)

    def fill(layer, k, chip):
        low, size = parts[k]
        side = lax.rem(layer, 2)
        rows_here = slice(low, low + size)
        lanes = pl.ds(pl.multiple_of(chip * 2 * LANE, 2 * LANE), 2 * LANE)

        def kept(which):
            return mask_of(mask_ref, which, EDGE + low, size)

        def activation(q):
            scale, offset = (
                jnp.concatenate([coef[side, chip * 2, n : n + 1], coef[side, chip * 2 + 1, n : n + 1]], axis=1)
                for n in range(2)
            )
            y = raw[side, q, rows_here, lanes].astype(F32) * scale + offset
            return y * jax.nn.sigmoid(y)

        @pl.when(layer == 0)
        def _():
            for q in range(4):
                vbuf[layer, q, rows_here, lanes] = raw[side, q, rows_here, lanes]

        @pl.when(jnp.logical_and(layer != 0, layer != POOL + 1))
        def _():
            for q in range(4):
                block = activation(q)
                if low + size > count:
                    block = jnp.where(kept(M_VALID), block, 0.0)
                vbuf[layer, q, rows_here, lanes] = block.astype(BF16)

        @pl.when(layer == POOL + 1)
        def _():
            pooled = smooth_max([activation(q) for q in range(4)])
            for q in range(4):
                vbuf[layer, q, rows_here, lanes] = jnp.where(kept(M_HIT + q), pooled, 0.0).astype(BF16)

    def at(low, size, spot):
        return yext[low : low + size, spot * LANE : (spot + 1) * LANE]

    greet([partner, across, diagonal] + row_peers(rows))
    if inside:
        own_rows = gather.rows_of(0, gather.low)
        for layer in range(layers):
            source = w_refs[layer // (layers // 2)]
            for block in range(9):
                lanes = slice(block * LANE, (block + 1) * LANE)
                wbuf[layer, own_rows, lanes] = source[layer % (layers // 2), 8 - block]
            if layer == 0:
                for piece in range(3):
                    first_gather.start(0, piece)
            elif layer <= 2:
                gather.start(layer)
    else:
        load(0).start()
    split_planes(v_ref, wide, count)
    for q in range(4):
        raw[0, q, :, own_lanes] = plane(wide, q).astype(BF16)
    to_core(0).start()
    for k in range(len(pieces)):
        to_far(0, k).start()
    yext[:EDGE, :] = jnp.zeros((EDGE, yext.shape[1]), F32)
    yext[EDGE + padded :, :] = jnp.zeros((EDGE, yext.shape[1]), F32)
    fill_masks(group_ref, here * count, count, padded, switch_ref, mask_ref)
    if inside:
        for piece in range(3):
            for step in range(1, rows // 2):
                first_gather.forward(0, step, piece)
        for piece in range(3):
            first_gather.wait(0, piece)

    def layer_step(layer):
        more = layer + 1 < layers
        def forward_gathers(condition, which, steps):
            @pl.when(condition)
            def _():
                for step in steps:
                    gather.forward(which, step)

        far = rows // 2
        if not inside:
            load(layer).wait()

            @pl.when(more)
            def _():
                load(layer + 1).start()

        to_core(layer).wait_recv()

        @pl.when(layer > 0)
        def _():
            coef_copy(layer, 0).wait_recv()

        def take(part):
            for k, piece in enumerate(pieces):
                if piece[0] == part:
                    to_far(layer, k).wait_recv()
            pass_on(layer, part).start()

        for k in range(len(parts)):
            fill(layer, k, half)
        take(0)
        take(1)
        if inside:

            @pl.when(layer > 0)
            def _():
                gather.wait(layer)

            save(layer, 2).start()
        add_products(layer, 0, padded, own_base, set())

        @pl.when(layer > 0)
        def _():
            for k in range(1, 3):
                coef_copy(layer, k).wait_recv()

        def far_products(k):
            pass_on(layer, k).wait_recv()
            low, size = parts[k]
            fill(layer, k, 1 - half)
            add_products(layer, low, size, far_base, set(range(16)))
            if k != 1:
                return
            for lane, spot in enumerate((12, 13, 14, 15, 7, 11)):
                to_next[:, lane * LANE : (lane + 1) * LANE] = at(count, EDGE, spot).astype(BF16)
            for lane, spot in enumerate((0, 1, 2, 3, 4, 8)):
                to_prev[:, lane * LANE : (lane + 1) * LANE] = at(EDGE, EDGE, spot).astype(BF16)

            @pl.when(here + 1 < rows)
            def _():
                down.start()

            @pl.when(here > 0)
            def _():
                up.start()

        def receive_halos():
            @pl.when(here > 0)
            def _():
                down.wait_recv()
                up.wait_send()
                for lane, spot in enumerate((12, 13, 14, 15, 7, 11)):
                    received = from_prev[:, lane * LANE : (lane + 1) * LANE].astype(F32)
                    yext[:EDGE, spot * LANE : (spot + 1) * LANE] = received

            @pl.when(here + 1 < rows)
            def _():
                up.wait_recv()
                down.wait_send()
                for lane, spot in enumerate((0, 1, 2, 3, 4, 8)):
                    received = from_next[:, lane * LANE : (lane + 1) * LANE].astype(F32)
                    yext[EDGE + count : 2 * EDGE + count, spot * LANE : (spot + 1) * LANE] = received

        def over_columns(kept, first, begin, end):
            low, size = EDGE + begin, end - begin
            go_left = mask_of(mask_ref, M_LEFT, low, size)
            go_right = mask_of(mask_ref, M_RIGHT, low, size)
            kept[low : low + size, :LANE] = at(low, size, first + 1) + jnp.where(
                go_left, at(low - 1, size, first + 3), 0.0
            )
            kept[low : low + size, LANE:] = at(low, size, first + 2) + jnp.where(
                go_right, at(low + 1, size, first), 0.0
            )

        def assemble(begin, end, sums_so_far):
            low, size = EDGE + begin, end - begin
            go_left = mask_of(mask_ref, M_LEFT, low, size)
            go_right = mask_of(mask_ref, M_RIGHT, low, size)
            total, squares = sums_so_far
            for q in range(4):
                a, b = q // 2, q % 2
                lanes = slice(b * LANE, (b + 1) * LANE)
                kept, sign = (over, -1) if a == 0 else (under, 1)
                rowwise = by_width(
                    mask_ref, low, size, lambda w: kept[low + sign * w : low + sign * w + size, lanes]
                )
                z = at(low, size, (a + 1) * 4 + b + 1)
                z = z + jnp.where(mask_of(mask_ref, (M_UP, M_DOWN)[a], low, size), rowwise, 0.0)
                if b == 0:
                    z = z + jnp.where(go_left, at(low - 1, size, (a + 1) * 4 + 3), 0.0)
                else:
                    z = z + jnp.where(go_right, at(low + 1, size, (a + 1) * 4), 0.0)
                if end > count:
                    z = jnp.where(mask_of(mask_ref, M_VALID, low, size), z, 0.0)
                zbuf[layer, q, begin:end] = z
                total = total + jnp.sum(z, axis=0, keepdims=True)
                squares = squares + jnp.sum(z * z, axis=0, keepdims=True)
            return total, squares

        def prepare(k):
            _, low, size = pieces[k]
            for q in range(4):
                piece = zbuf[layer, q, low : low + size] - local
                raw[lax.rem(layer + 1, 2), q, low : low + size, own_lanes] = piece.astype(BF16)

        if inside:
            forward_gathers(jnp.logical_and(layer < 2, more), layer + 1, range(1, 2))
            forward_gathers(jnp.logical_and(layer > 1, more), layer + 1, range(2, 3))
        take(2)
        far_products(0)
        far_products(1)
        take(3)
        far_products(2)
        far_products(3)
        take(4)
        if inside:
            forward_gathers(jnp.logical_and(layer < 2, more), layer + 1, range(2, far - 1))
            forward_gathers(jnp.logical_and(layer > 1, more), layer + 1, range(3, far))
        near, widest = min(WIDTHS), max(WIDTHS)
        (_, top, size), (_, bottom, last_size) = pieces[:2]
        first = (top, top + size)
        last = (bottom, bottom + last_size)
        over_ready = [(n - widest, ceil_to(m - near, 8)) for n, m in (first, last)]
        under_ready = [((n + near) // 8 * 8, m + widest) for n, m in (first, last)]
        for kept, spot, ready in ((over, 12, over_ready), (under, 0, under_ready)):
            for begin, end in ready:
                over_columns(kept, spot, begin, end)
        none = (jnp.zeros((1, LANE), F32),) * 2
        inner = assemble(*last, assemble(*first, none))
        local = inner[0] / (4.0 * (size + last_size))

        @pl.when(more)
        def _():
            for k in range(2):
                prepare(k)
                to_far(layer + 1, k).start()

        far_products(4)
        save(layer, 0).start()
        receive_halos()
        over_rest = [(8 - EDGE, over_ready[0][0]), (over_ready[0][1], over_ready[1][0]), (over_ready[1][1], padded)]
        under_rest = [(0, under_ready[0][0]), (under_ready[0][1], under_ready[1][0]), (under_ready[1][1], padded + EDGE - 8)]
        for kept, spot, rest in ((over, 12, over_rest), (under, 0, under_rest)):
            for begin, end in rest:
                over_columns(kept, spot, begin, end)
        total, squares = assemble(last[1], padded, assemble(first[1], last[0], assemble(0, first[0], inner)))
        save(layer, 1).start()
        own = jnp.concatenate([total, squares, jnp.zeros((6, LANE), F32)], axis=0)
        channel = (sums.at[layer], sum_s.at[layer], sum_r.at[layer])
        send_sums(rows, own, *channel)

        @pl.when(more)
        def _():
            for k in range(2, len(pieces)):
                prepare(k)
                if k < 4:
                    to_far(layer + 1, k).start()
            to_core(layer + 1).start()

        for k in range(len(pieces)):
            to_far(layer, k).wait_send()
        for k in range(len(parts)):
            pass_on(layer, k).wait_send()
        to_core(layer).wait_send()

        @pl.when(layer > 0)
        def _():
            for k in range(3):
                coef_copy(layer, k).wait_send()

        if inside:
            forward_gathers(jnp.logical_and(layer < 2, more), layer + 1, range(far - 1, far))
        both = add_sums(rows, *channel)
        mean = both[0:1] / pixels
        inverse = lax.rsqrt(both[1:2] / pixels - mean * mean + EPSILON)
        stat_ref[layer] = jnp.concatenate([mean, inverse, jnp.zeros((6, LANE), F32)], axis=0)
        scale = gb_ref[layer, 0:1] * inverse

        @pl.when(more)
        def _():
            offset = scale * (local - mean) + gb_ref[layer, 1:2]
            coef[lax.rem(layer + 1, 2), mine] = jnp.concatenate([scale, offset, jnp.zeros((6, LANE), F32)], axis=0)
            for k in range(3):
                coef_copy(layer + 1, k).start()
            for k in range(4, len(pieces)):
                to_far(layer + 1, k).start()

        if inside:

            @pl.when(layer + 3 < layers)
            def _():
                gather.start(layer + 3)

            forward_gathers(jnp.logical_and(layer > 0, layer + 2 < layers), layer + 2, range(1, 2))

        @pl.when(layer + 1 == layers)
        def _():
            for q in range(4):
                y = scale * (zbuf[layer, q] - mean) + gb_ref[layer, 1:2]
                set_plane(wide, q, 0, y * jax.nn.sigmoid(y))
            next_ref[...] = wide[: 4 * count].astype(BF16)

    each(layers, layer_step)

    def drain(layer):
        if inside:

            @pl.when(layer > 0)
            def _():
                gather.drain(layer)

        for which in range(3 if inside else 2):
            save(layer, which).wait()

    each(layers, drain)
    if inside:
        for piece in range(3):
            first_gather.drain(0, piece)


def backward_kernel(inside, layers, rows, count, padded, pixels, *refs):
    refs = list(refs)
    g_ref, stat_ref, gb_ref, mask_ref, z_in, full_in, w_in = refs[:7]
    del refs[:7]
    out_ref, gbgrad_ref = refs[:2]
    wgrad_refs = refs[2 : 3 + inside]
    del refs[: 3 + inside]
    (
        grad_ref, wide, zbuf, fbuf, wbuf, dk, gy, gext, above, below, patch, part, keep, core_out, core_in, x_out, x_in,
        to_next, to_prev, from_prev, from_next, sums,
        core_s, core_r, x_s, x_r, halo_s, halo_r, sum_s, sum_r, load_sem, out_sem,
    ) = refs[:32]
    mine, here = lax.axis_index("grp"), lax.axis_index("rows")
    half, core = mine // 2, lax.rem(mine, 2)
    partner, across = grp_peers()
    own_lanes, other_lanes = lanes_of(core), lanes_of(1 - core)
    own_base = pl.multiple_of(half * 2 * LANE, 2 * LANE)
    far_base = pl.multiple_of((1 - half) * 2 * LANE, 2 * LANE)
    if inside:
        first, second, third, total_ref, s1, r1, s2, r2 = refs[32:]
        shard = dk.shape[1] // rows
        scatter = Scatter(rows, shard, dk, first, second, third, total_ref, wgrad_refs, s1, r1, s2, r2)

    def load(turn, which):
        src, dst = ((z_in, zbuf), (w_in, wbuf), (full_in, fbuf))[which]
        side = lax.rem(turn, 2)
        return pltpu.make_async_copy(src.at[layers - 1 - turn], dst.at[side], load_sem.at[side, which])

    def save(turn):
        slot = lax.rem(turn, 3)
        return pltpu.make_async_copy(dk.at[slot], wgrad_refs[0].at[layers - 1 - turn], out_sem.at[slot])

    for turn in range(2):
        for which in range(3):
            load(turn, which).start()
    after = (lax.rem(here + 1, rows), mine)
    before = (lax.rem(here + rows - 1, rows), mine)
    split_planes(g_ref, wide, count)
    for q in range(4):
        grad_ref[q] = plane(wide, q)
    gext[:EDGE, :] = jnp.zeros((EDGE, 4 * LANE), F32)
    gext[EDGE + padded :, :] = jnp.zeros((EDGE, 4 * LANE), F32)
    greet([partner, across] + row_peers(rows))

    def taps(q, step):
        first = (q // 2 + step) * 4 + q % 2
        return patch[:, first * LANE : (first + 3) * LANE]

    def layer_step(turn):
        layer = layers - 1 - turn
        side, slot = lax.rem(turn, 2), lax.rem(turn, 3)
        last = turn + 1 == layers
        mean, inverse = stat_ref[layer, 0:1], stat_ref[layer, 1:2]
        gain, shift = gb_ref[layer, 0:1], gb_ref[layer, 1:2]
        valid = mask_of(mask_ref, M_VALID, EDGE, padded)
        load(turn, 0).wait()
        down = remote(to_next, from_prev.at[side], halo_s.at[0], halo_r.at[side, 0], after)
        up = remote(to_prev, from_next.at[side], halo_s.at[1], halo_r.at[side, 1], before)

        def shifted(q):
            normed = (zbuf[side, q] - mean) * inverse
            return normed, gain * normed + shift

        @pl.when(layer == POOL)
        def _():
            pooled_grad = jnp.zeros((padded, LANE), F32)
            for q in range(4):
                pooled_grad = jnp.where(mask_of(mask_ref, M_HIT + q, EDGE, padded), grad_ref[q], pooled_grad)
            blocks = []
            for q in range(4):
                _, y = shifted(q)
                gy[q] = y * jax.nn.sigmoid(y)
            pooled = smooth_max([gy[q] for q in range(4)])
            for q in range(4):
                grad_ref[q] = pooled_grad * (jnp.exp(gy[q] - pooled) * 0.25)

        shift_sum = jnp.zeros((1, LANE), F32)
        gain_sum = jnp.zeros((1, LANE), F32)
        for q in range(4):
            normed, y = shifted(q)
            s = jax.nn.sigmoid(y)
            grad = jnp.where(valid, grad_ref[q] * s * (1.0 + y * (1.0 - s)), 0.0)
            gy[q] = grad
            shift_sum = shift_sum + jnp.sum(grad, axis=0, keepdims=True)
            gain_sum = gain_sum + jnp.sum(grad * normed, axis=0, keepdims=True)

        def spread(buf, low, planes):
            for lane, q in enumerate(planes):
                piece = slice(low, low + EDGE)
                normed = (zbuf[side, q, piece] - mean) * inverse
                buf[:, 2 * lane * LANE : (2 * lane + 1) * LANE] = gy[q, piece].astype(BF16)
                buf[:, (2 * lane + 1) * LANE : (2 * lane + 2) * LANE] = normed.astype(BF16)

        spread(to_next, count - EDGE, (2, 3, 1))
        spread(to_prev, 0, (0, 1, 2))

        @pl.when(here + 1 < rows)
        def _():
            down.start()

        @pl.when(here > 0)
        def _():
            up.start()

        own = jnp.concatenate([shift_sum, gain_sum, jnp.zeros((6, LANE), F32)], axis=0)
        channel = (sums.at[side], sum_s.at[side], sum_r.at[side])
        send_sums(rows, own, *channel)
        if inside:

            @pl.when(turn > 0)
            def _():
                scatter.start(turn - 1)

        both = add_sums(rows, *channel)
        gbgrad_ref[layer] = both

        def conv_grad(grad, normed):
            out = inverse * gain * (grad - both[0:1] / pixels - normed * both[1:2] / pixels)
            return out.astype(BF16).astype(F32)

        for q in range(4):
            normed, _ = shifted(q)
            gext[EDGE : EDGE + padded, q * LANE : (q + 1) * LANE] = jnp.where(
                valid, conv_grad(gy[q], normed), 0.0
            )

        def receive(buf, low, planes):
            for lane, q in enumerate(planes):
                grad = buf[side, :, 2 * lane * LANE : (2 * lane + 1) * LANE].astype(F32)
                normed = buf[side, :, (2 * lane + 1) * LANE : (2 * lane + 2) * LANE].astype(F32)
                gext[low : low + EDGE, q * LANE : (q + 1) * LANE] = conv_grad(grad, normed)

        @pl.when(here > 0)
        def _():
            down.wait_recv()
            up.wait_send()
            receive(from_prev, 0, (2, 3, 1))

        @pl.when(here + 1 < rows)
        def _():
            up.wait_recv()
            down.wait_send()
            receive(from_next, EDGE + count, (0, 1, 2))

        low, size = EDGE - 8, padded + 16
        for kept, which, sign, lanes in (
            (above, M_UP, -1, slice(2 * LANE, 4 * LANE)),
            (below, M_DOWN, 1, slice(0, 2 * LANE)),
        ):
            rowwise = by_width(
                mask_ref, low, size, lambda w: gext[low + sign * w : low + sign * w + size, lanes]
            )
            kept[...] = jnp.where(mask_of(mask_ref, which, low, size), rowwise, 0.0)
        go_left = mask_of(mask_ref, M_LEFT, EDGE, padded)
        go_right = mask_of(mask_ref, M_RIGHT, EDGE, padded)
        for step, (kept, top, lane) in enumerate(
            ((above, 8, 0), (gext, EDGE, 0), (gext, EDGE, 2 * LANE), (below, 8, 0))
        ):
            even, odd = slice(lane, lane + LANE), slice(lane + LANE, lane + 2 * LANE)
            blocks = [
                jnp.where(go_left, kept[top - 1 : top - 1 + padded, odd], 0.0),
                kept[top : top + padded, even],
                kept[top : top + padded, odd],
                jnp.where(go_right, kept[top + 1 : top + 1 + padded, even], 0.0),
            ]
            for column, block in enumerate(blocks):
                spot = step * 4 + column
                patch[:, spot * LANE : (spot + 1) * LANE] = block.astype(BF16)

        def kernel_grad():
            for step in range(3):
                total = None
                for q in range(4):
                    product = lax.dot_general(
                        fbuf[side, q], taps(q, step), (((0,), (0,)), ((), ())), preferred_element_type=F32
                    )
                    total = product if total is None else total + product
                dk[slot, :, step * 3 * LANE : (step + 1) * 3 * LANE] = total.astype(BF16)
            if not inside:
                save(turn).start()

        def scatter_forward(step):
            @pl.when(turn > 0)
            def _():
                scatter.forward(turn - 1, step)

        if inside:

            @pl.when(turn > 1)
            def _():
                scatter.finish(turn - 2, layer + 2)
                scatter.drain(turn - 2)

            scatter_forward(1)
        load(turn, 1).wait()
        load(turn, 2).wait()
        if not inside:

            @pl.when(turn > 2)
            def _():
                save(turn - 3).wait()

        @pl.when(last)
        def _():
            kernel_grad()
            if inside:
                scatter.start(turn)

        def input_grad(q, base):
            total = None
            for step in range(3):
                right = wbuf[side, pl.ds(base, 2 * LANE), step * 3 * LANE : (step + 1) * 3 * LANE]
                product = lax.dot_general(
                    taps(q, step), right, (((1,), (1,)), ((), ())), preferred_element_type=F32
                )
                total = product if total is None else total + product
            part[...] = total

        def to_core(spot):
            return remote(
                core_out.at[side, spot], core_in.at[side, spot],
                core_s.at[side, spot], core_r.at[side, spot], partner,
            )

        def to_far(q):
            return remote(x_out.at[side, q], x_in.at[side, q], x_s.at[side, q], x_r.at[side, q], across)

        def send_across(q):
            to_core(q).wait_recv()
            x_out[side, q] = (keep[q] + core_in[side, q].astype(F32)).astype(BF16)
            to_far(q).start()

        for spot in range(8):
            input_grad(spot % 4, far_base if spot < 4 else own_base)
            core_out[side, spot] = part[:, other_lanes].astype(BF16)
            keep[spot] = part[:, own_lanes]
            to_core(spot).start()
            if 2 <= spot < 6:
                send_across(spot - 2)
            if inside and spot == 5:
                scatter_forward(2)

        @pl.when(jnp.logical_not(last))
        def _():
            kernel_grad()

        @pl.when(turn + 2 < layers)
        def _():
            for which in range(3):
                load(turn + 2, which).start()

        if inside:
            for step in range(3, rows // 2):
                scatter_forward(step)
            scatter_forward(0)
        for q in range(4):
            to_core(4 + q).wait_recv()
            to_far(q).wait_recv()
            grad_ref[q] = keep[4 + q] + core_in[side, 4 + q].astype(F32) + x_in[side, q].astype(F32)
        for spot in range(8):
            to_core(spot).wait_send()
        for q in range(4):
            to_far(q).wait_send()

    each(layers, layer_step)
    for q in range(4):
        set_plane(wide, q, 0, grad_ref[q])
    out_ref[...] = wide[: 4 * count].astype(BF16)
    if inside:
        for step in scatter.order():
            scatter.forward(layers - 1, step)
        for turn in (layers - 2, layers - 1):
            scatter.finish(turn, layers - 1 - turn)
            scatter.drain(turn)
    else:
        for turn in range(layers - 3, layers):
            save(turn).wait()


VM = pl.BlockSpec(memory_space=pltpu.VMEM)
HBM = pl.BlockSpec(memory_space=pl.ANY)
LIMIT = 56 * 1024 * 1024
DMA = pltpu.SemaphoreType.DMA


def forward_block(inside, rows, count, padded, pixels, image_group, switches, features, pairs, weights):
    layers, channels, taps = pairs.shape[0], 4 * LANE, 9 * LANE
    ext = padded + 2 * EDGE
    n_parts = len(row_parts(padded, count))
    far = rows // 2
    shape = jax.ShapeDtypeStruct
    out = pl.pallas_call(
        functools.partial(forward_kernel, inside, layers, rows, count, padded, pixels),
        name="forward_block",
        out_shape=(
            shape((4 * count, LANE), BF16),
            shape((layers, 8, LANE), F32),
            shape((ext, LANE), F32),
            shape((layers, 4, padded, LANE), F32),
            shape((layers, 4, padded, channels), BF16),
            shape((layers, channels, taps) if inside else (1, 16, LANE), BF16),
        ),
        in_specs=[pl.BlockSpec(memory_space=pltpu.SMEM), VM, VM, VM] + [VM if inside else HBM] * len(weights),
        out_specs=(VM, VM, VM, HBM, HBM, HBM),
        scratch_shapes=[
            pltpu.VMEM((layers, 4, padded, channels), BF16),
            pltpu.VMEM((layers, channels, taps), BF16),
            pltpu.VMEM((layers, 4, padded, LANE), F32),
            pltpu.VMEM((2, 4, padded, channels), BF16),
            pltpu.VMEM((2, 4, 8, LANE), F32),
            pltpu.VMEM((ext, 16 * LANE), F32),
            pltpu.VMEM((ext, 2 * LANE), F32),
            pltpu.VMEM((ext, 2 * LANE), F32),
            pltpu.VMEM((4 * padded, LANE), F32),
        ]
        + [pltpu.VMEM((EDGE, 6 * LANE), BF16)] * 4
        + [pltpu.VMEM((layers, rows, 8, LANE), F32)]
        + [DMA((layers,))] * 2
        + [DMA((layers, len(far_pieces(row_parts(padded, count)))))] * 2
        + [DMA((layers, n_parts))] * 2
        + [DMA((2,))] * 2
        + [DMA((layers, rows - 1))] * 2
        + [DMA((layers, 3))] * 3
        + [DMA((layers, far - 1))] * 2
        + [DMA((layers, far))] * 2
        + [DMA((3, far - 1))] * 2
        + [DMA((3, far))] * 2,
        compiler_params=pltpu.CompilerParams(
            collective_id=0, has_side_effects=True, vmem_limit_bytes=LIMIT
        ),
    )(image_group, switches, features, pairs, *weights)
    return out[:5] + ((out[5] if inside else weights[0]),)


def backward_block(inside, rows, count, padded, pixels, grad, z, stat, pairs, masks, full, weight):
    layers, channels, taps = weight.shape
    ext = padded + 2 * EDGE
    shard = channels // rows
    far = rows // 2
    shape = jax.ShapeDtypeStruct
    scratch = [
        pltpu.VMEM((4, padded, LANE), F32),
        pltpu.VMEM((4 * padded, LANE), F32),
        pltpu.VMEM((2, 4, padded, LANE), F32),
        pltpu.VMEM((2, 4, padded, channels), BF16),
        pltpu.VMEM((2, channels, taps), BF16),
        pltpu.VMEM((3, channels, taps), BF16),
        pltpu.VMEM((4, padded, LANE), F32),
        pltpu.VMEM((ext, 4 * LANE), F32),
        pltpu.VMEM((padded + 16, 2 * LANE), F32),
        pltpu.VMEM((padded + 16, 2 * LANE), F32),
        pltpu.VMEM((padded, 16 * LANE), BF16),
        pltpu.VMEM((padded, 2 * LANE), F32),
        pltpu.VMEM((8, padded, LANE), F32),
        pltpu.VMEM((2, 8, padded, LANE), BF16),
        pltpu.VMEM((2, 8, padded, LANE), BF16),
        pltpu.VMEM((2, 4, padded, LANE), BF16),
        pltpu.VMEM((2, 4, padded, LANE), BF16),
    ]
    scratch += [pltpu.VMEM((EDGE, 6 * LANE), BF16)] * 2 + [pltpu.VMEM((2, EDGE, 6 * LANE), BF16)] * 2
    scratch += [pltpu.VMEM((2, rows, 8, LANE), F32)]
    scratch += [DMA((2, 8))] * 2 + [DMA((2, 4))] * 2 + [DMA((2,)), DMA((2, 2))] + [DMA((2, rows - 1))] * 2
    scratch += [DMA((2, 3)), DMA((3,))]
    wgrads = [shape((layers, channels, taps), BF16)]
    if inside:
        wgrads = [shape((layers // 2, 9, shard, LANE), F32)] * 2
        scratch += [
            pltpu.VMEM((3, far, shard, taps), BF16),
            pltpu.VMEM((3, far - 1, shard, taps), BF16),
            pltpu.VMEM((3, far - 1, shard, taps), BF16),
            pltpu.VMEM((3, shard, taps), F32),
        ]
        scratch += [DMA((3, far))] * 2 + [DMA((3, far - 1))] * 2
    return pl.pallas_call(
        functools.partial(backward_kernel, inside, layers, rows, count, padded, pixels),
        name="backward_block",
        out_shape=[shape((4 * count, LANE), BF16), shape((layers, 8, LANE), F32)] + wgrads,
        in_specs=[VM] * 4 + [HBM] * 3,
        out_specs=[VM, VM] + [VM if inside else HBM] * len(wgrads),
        scratch_shapes=scratch,
        compiler_params=pltpu.CompilerParams(
            collective_id=1, has_side_effects=True, vmem_limit_bytes=LIMIT
        ),
    )(grad, stat, pairs, masks, z, full, weight)


def shards(
    features, image_group, switches, enc_weight, dec_weight,
    enc_gain, enc_bias, dec_gain, dec_bias, d_decoded,
):
    rows = lax.axis_size("rows")
    count = features.shape[0] // 4
    padded = ceil_to(count, 16)
    pixels = float(features.shape[0] * rows)
    depth, shard = enc_weight.shape[0], enc_weight.shape[2]
    inside = shard % 16 == 0
    sizes = (rows, count, padded, pixels)
    weights = [enc_weight, dec_weight]
    if not inside:
        both = jnp.concatenate(weights)
        flat = jnp.transpose(both[:, ::-1], (0, 2, 1, 3)).reshape(both.shape[0], shard, -1)
        weights = [lax.all_gather(flat, "rows", axis=1, tiled=True)]
    pairs = jnp.stack([jnp.concatenate([enc_gain, dec_gain]), jnp.concatenate([enc_bias, dec_bias])], axis=1)
    pairs = jnp.pad(pairs, ((0, 0), (0, 6), (0, 0)))

    hits = jnp.pad(switches, (EDGE, padded - count + EDGE), constant_values=-LANE)[:, None]
    decoded, stat, masks, z, full, weight = forward_block(
        inside, *sizes, image_group, hits, features, pairs, weights
    )
    grad, pair_grads, *wgrads = backward_block(
        inside, *sizes, d_decoded, z, stat, pairs, masks, full, weight
    )
    if not inside:
        wgrad = lax.psum_scatter(wgrads[0], "rows", scatter_dimension=1, tiled=True).astype(F32)
        wgrad = jnp.transpose(wgrad.reshape(2 * depth, shard, 9, -1)[:, :, ::-1], (0, 2, 1, 3))
        wgrads = [wgrad[:depth], wgrad[depth:]]
    return (
        decoded,
        grad,
        *wgrads,
        pair_grads[:depth, 1],
        pair_grads[:depth, 0],
        pair_grads[depth:, 1],
        pair_grads[depth:, 0],
    )


def solution(mesh):
    wide = P("rows", "grp")
    kernels = P(None, None, "rows", "grp")
    vector = P(None, "grp")
    return jax.shard_map(
        shards,
        mesh=mesh,
        in_specs=(wide, P(), P("rows"), kernels, kernels, vector, vector, vector, vector, wide),
        out_specs=(wide, wide, kernels, kernels, vector, vector, vector, vector),
        check_vma=False,
    )
```

```python
import functools

import jax
import jax.numpy as jnp
from jax import lax
from jax.experimental import pallas as pl
from jax.experimental.pallas import tpu as pltpu
from jax.sharding import PartitionSpec as P

SIZES = ((15, 20), (18, 24), (30, 40))
WIDTHS = tuple(w for _, w in SIZES)
EDGE = 48
EPSILON = 1e-05
MESH = pl.DeviceIdType.MESH
F32 = jnp.float32
BF16 = jnp.bfloat16
LANE = 128
(M_W0, M_W1, M_UP, M_DOWN, M_LEFT, M_RIGHT, M_VALID, M_HIT) = range(8)
POOL = 2


def ceil_to(value, step):
    return -(-value // step) * step


def fill_masks(group_ref, first_window, count, padded, switch_ref, mask_ref):
    shape = (padded + 2 * EDGE, 1)
    local = lax.broadcasted_iota(jnp.int32, shape, 0) - EDGE
    windows = local + first_window

    start = jnp.int32(0)
    base = height = width = jnp.zeros(shape, jnp.int32)
    for image in range(group_ref.shape[0]):
        group = group_ref[image]
        tall, wide = (
            jnp.where(group == 0, SIZES[0][k], jnp.where(group == 1, SIZES[1][k], SIZES[2][k])) for k in range(2)
        )
        end = start + tall * wide
        member = (windows >= start) & (windows < end)
        base, height, width = (
            jnp.where(member, new, old) for new, old in ((start, base), (tall, height), (wide, width))
        )
        start = end
    inside = width > 0
    position = windows - base
    row = jnp.zeros(shape, jnp.int32)
    for tall, wide in SIZES:
        quotient = jnp.floor((position.astype(F32) + 0.5) * (1.0 / wide)).astype(jnp.int32)
        row = jnp.where(width == wide, quotient, row)
    column = position - row * width
    masks = [
        width == WIDTHS[0],
        width == WIDTHS[1],
        inside & (row > 0),
        inside & (row < height - 1),
        inside & (column > 0),
        inside & (column < width - 1),
        (local >= 0) & (local < count),
    ]
    lane = lax.broadcasted_iota(jnp.int32, (shape[0], LANE), 1)
    table = (lane - M_HIT == switch_ref[...]).astype(F32)
    for k, mask in enumerate(masks):
        table = jnp.where((lane == k) & mask, 1.0, table)
    mask_ref[...] = table


def split_planes(stream_ref, wide_ref, count):
    wide_ref[: 4 * count] = stream_ref[...].astype(F32)
    wide_ref[4 * count :] = jnp.zeros((wide_ref.shape[0] - 4 * count, LANE), F32)


def plane(wide_ref, q):
    return wide_ref[pl.ds(q, wide_ref.shape[0] // 4, stride=4), :]


def set_plane(wide_ref, q, low, block):
    wide_ref[pl.ds(4 * low + q, block.shape[0], stride=4), :] = block


def mask_of(mask_ref, which, low, count):
    return mask_ref[low : low + count, which : which + 1] > 0.5


def by_width(mask_ref, low, count, shifted):
    return jnp.where(
        mask_of(mask_ref, M_W0, low, count),
        shifted(WIDTHS[0]),
        jnp.where(mask_of(mask_ref, M_W1, low, count), shifted(WIDTHS[1]), shifted(WIDTHS[2])),
    )


def smooth_max(blocks):
    total = sum(jnp.exp(block) for block in blocks)
    return jnp.log(total * 0.25)


def row_peers(rows):
    here = lax.axis_index("rows")
    there = lax.axis_index("grp")
    order = sorted(range(1, rows), key=lambda k: -min(k, rows - k))
    return [(lax.rem(here + k, rows), there) for k in order]


def grp_peers():
    here = lax.axis_index("rows")
    mine = lax.axis_index("grp")
    half, core = mine // 2, lax.rem(mine, 2)
    return (here, half * 2 + 1 - core), (here, (1 - half) * 2 + core)


def greet(peers):
    barrier = pltpu.get_barrier_semaphore()
    for peer in peers:
        pl.semaphore_signal(barrier, inc=1, device_id=peer, device_id_type=MESH)
    pl.semaphore_wait(barrier, len(peers))


def remote(src, dst, send, recv, peer):
    return pltpu.make_async_remote_copy(
        src_ref=src, dst_ref=dst, send_sem=send, recv_sem=recv, device_id=peer, device_id_type=MESH
    )


def sums_copies(rows, buf, send, recv):
    return [
        remote(buf.at[0], buf.at[k + 1], send.at[k], recv.at[k], peer) for k, peer in enumerate(row_peers(rows))
    ]


def send_sums(rows, own, buf, send, recv):
    buf[0] = own
    for copy in sums_copies(rows, buf, send, recv):
        copy.start()


def add_sums(rows, buf, send, recv):
    for copy in sums_copies(rows, buf, send, recv):
        copy.wait()
    total = buf[0]
    for k in range(1, rows):
        total = total + buf[k]
    return total


def row_parts(padded, count):
    tail = (count - EDGE) // 16 * 16
    inner, start, steps = [], EDGE, 3
    for k in range(steps):
        size = min(ceil_to(-(-(tail - start) // (steps - k)), 16), tail - start)
        inner.append((start, size))
        start += size
    return [(0, EDGE), (tail, padded - tail), inner[0], inner[2], inner[1]]


REACH = max(WIDTHS) + 1


def far_pieces(parts):
    low, size = parts[4]
    first, last = (low - REACH) // 8 * 8, ceil_to(low + size + REACH, 8)
    return [
        (2, parts[2][0], first - parts[2][0]),
        (3, last, parts[3][0] + parts[3][1] - last),
        (0, *parts[0]),
        (1, *parts[1]),
        (2, first, parts[2][0] + parts[2][1] - first),
        (3, parts[3][0], last - parts[3][0]),
        (4, low, size),
    ]


def lanes_of(block):
    return pl.ds(pl.multiple_of(block * LANE, LANE), LANE)


class Gather:
    def __init__(self, rows, shard, buf, send, recv, pass_send, pass_recv):
        self.shard, self.buf = shard, buf
        self.far = rows // 2
        here, there = lax.axis_index("rows"), lax.axis_index("grp")
        self.high, self.low = here // 2, lax.rem(here, 2)
        self.there = there
        self.send, self.recv, self.pass_send, self.pass_recv = send, recv, pass_send, pass_recv

    def rows_of(self, step, low):
        block = lax.rem(self.high + step, self.far) * 2 + low
        return pl.ds(pl.multiple_of(block * self.shard, 16), self.shard)

    def block(self, layer, step, piece):
        lanes = slice(None) if piece is None else slice(piece * 3 * LANE, (piece + 1) * 3 * LANE)
        slot = layer if piece is None else piece
        return self.buf.at[layer, self.rows_of(step, self.low), lanes], slot

    def spread(self, layer, step, piece=None):
        own, slot = self.block(layer, 0, piece)
        peer = (lax.rem(self.high + step, self.far) * 2 + self.low, self.there)
        k = step - 1
        return remote(own, own, self.send.at[slot, k], self.recv.at[slot, k], peer)

    def across(self, layer, step, piece=None):
        part, slot = self.block(layer, self.far - step, piece)
        peer = (self.high * 2 + 1 - self.low, self.there)
        return remote(part, part, self.pass_send.at[slot, step], self.pass_recv.at[slot, step], peer)

    def start(self, layer, piece=None):
        for step in range(1, self.far):
            self.spread(layer, step, piece).start()
        self.across(layer, 0, piece).start()

    def forward(self, layer, step, piece=None):
        self.spread(layer, step, piece).wait_recv()
        self.across(layer, step, piece).start()

    def wait(self, layer, piece=None):
        for step in range(self.far):
            self.across(layer, step, piece).wait_recv()

    def drain(self, layer, piece=None):
        for step in range(1, self.far):
            self.spread(layer, step, piece).wait_send()
        for step in range(self.far):
            self.across(layer, step, piece).wait_send()


class Scatter:
    def __init__(self, rows, shard, grads, first, second, third, total, outs, semaphores):
        self.shard, self.grads, self.first, self.second, self.third = shard, grads, first, second, third
        self.total, self.outs, self.far = total, outs, rows // 2
        here, self.there = lax.axis_index("rows"), lax.axis_index("grp")
        self.high, self.low = here // 2, lax.rem(here, 2)
        self.semaphores = semaphores

    def rows_of(self, step, low):
        block = lax.rem(self.high + step, self.far) * 2 + low
        return pl.ds(pl.multiple_of(block * self.shard, 16), self.shard)

    def across(self, turn, step):
        slot = lax.rem(turn, 3)
        send, recv, _, _ = self.semaphores
        peer = (self.high * 2 + 1 - self.low, self.there)
        return remote(
            self.grads.at[slot, self.rows_of(step, 1 - self.low), :], self.first.at[slot, step],
            send.at[slot, step], recv.at[slot, step], peer,
        )

    def spread(self, turn, step):
        slot = lax.rem(turn, 3)
        _, _, send, recv = self.semaphores
        peer = (lax.rem(self.high + step, self.far) * 2 + self.low, self.there)
        k = step - 1
        return remote(
            self.second.at[slot, k], self.third.at[slot, k],
            send.at[slot, k], recv.at[slot, k], peer,
        )

    def order(self):
        return list(range(1, self.far)) + [0]

    def start(self, turn, steps):
        for step in steps:
            self.across(turn, step).start()

    def forward(self, turn, step):
        slot = lax.rem(turn, 3)
        self.across(turn, step).wait_recv()
        own = self.grads[slot, self.rows_of(step, self.low), :]
        total = own.astype(F32) + self.first[slot, step].astype(F32)
        if step == 0:
            self.total[slot] = total
        else:
            self.second[slot, step - 1] = total.astype(BF16)
            self.spread(turn, step).start()

    def finish(self, turn, layer):
        slot = lax.rem(turn, 3)
        for step in range(1, self.far):
            self.spread(turn, step).wait_recv()
        total = self.total[slot]
        for step in range(1, self.far):
            total = total + self.third[slot, step - 1].astype(F32)
        depth = self.outs[0].shape[0]

        def put(out, index):
            for block in range(9):
                out[index, 8 - block] = total[:, block * LANE : (block + 1) * LANE]

        @pl.when(layer < depth)
        def _():
            put(self.outs[0], layer)

        @pl.when(layer >= depth)
        def _():
            put(self.outs[1], layer - depth)

    def drain(self, turn):
        for step in range(self.far):
            self.across(turn, step).wait_send()
        for step in range(1, self.far):
            self.spread(turn, step).wait_send()


def each(count, body):
    lax.fori_loop(0, count, lambda i, carry: (body(i), carry)[1], 0)


GATHER_PLAN = {
    "products": {0: [("pass", 1, 1)]},
    "parts": {0: [("pass", 1, 2)]},
    "outer": {},
    "sums": {0: [("pass", 1, 3)]},
    "norm": {},
}
for turn in range(4):
    GATHER_PLAN["norm"][turn] = [("out", turn + 2, 1), ("out", turn + 2, 2), ("own", turn + 2, 0)]
    GATHER_PLAN["parts"][turn + 1] = [("pass", turn + 2, 1)]
    GATHER_PLAN["outer"][turn + 1] = [("out", turn + 2, 3), ("pass", turn + 2, 2)]
    GATHER_PLAN["sums"][turn + 1] = [("pass", turn + 2, 3)]


def forward_kernel(
    inside, layers, rows, count, padded, pixels, group_ref, switch_ref, v_ref, gb_ref, *refs
):
    w_refs, refs = refs[: 1 + inside], refs[1 + inside :]
    (
        next_ref, stat_ref, mask_ref, z_out, full_out, w_out,
        vbuf, wbuf, zbuf, raw, coef, yext, over, under, wide, to_next, to_prev, from_prev, from_next, sums,
        core_s, core_r, x_s, x_r, fwd_s, fwd_r, halo_s, halo_r, sum_s, sum_r, out_sem,
        coef_s, coef_r, w_s, w_r, wp_s, wp_r, first_s, first_r, first_ps, first_pr,
    ) = refs
    mine, here = lax.axis_index("grp"), lax.axis_index("rows")
    half = mine // 2
    partner, across = grp_peers()
    diagonal = (here, across[1] + partner[1] - mine)
    parts = row_parts(padded, count)
    pieces = far_pieces(parts)
    own_lanes, far_lanes = lanes_of(mine), lanes_of(across[1])
    own_base = pl.multiple_of(half * 2 * LANE, 2 * LANE)
    far_base = pl.multiple_of((1 - half) * 2 * LANE, 2 * LANE)
    shard = wbuf.shape[1] // rows
    gather = Gather(rows, shard, wbuf, w_s, w_r, wp_s, wp_r)
    first_gather = Gather(rows, shard, wbuf, first_s, first_r, first_ps, first_pr)

    def slab(layer, k, lanes):
        low, size = parts[k]
        return raw.at[lax.rem(layer, 2), :, pl.ds(low, size), lanes]

    def to_core(layer):
        whole = raw.at[lax.rem(layer, 2), :, :, own_lanes]
        return remote(whole, whole, core_s.at[layer], core_r.at[layer], partner)

    def to_far(layer, k):
        _, low, size = pieces[k]
        piece = raw.at[lax.rem(layer, 2), :, pl.ds(low, size), own_lanes]
        return remote(piece, piece, x_s.at[layer, k], x_r.at[layer, k], across)

    def pass_on(layer, k):
        piece = slab(layer, k, far_lanes)
        return remote(piece, piece, fwd_s.at[layer, k], fwd_r.at[layer, k], partner)

    def coef_copy(layer, k):
        own = coef.at[lax.rem(layer, 2), mine]
        return remote(own, own, coef_s.at[layer, k], coef_r.at[layer, k], (partner, across, diagonal)[k])

    def load(layer):
        return pltpu.make_async_copy(w_refs[0].at[layer], wbuf.at[layer], w_s.at[layer, 0])

    def save(layer, which):
        pairs = [(vbuf, full_out), (zbuf, z_out), (wbuf, w_out)]
        src, dst = pairs[which]
        return pltpu.make_async_copy(src.at[layer], dst.at[layer], out_sem.at[layer, which])

    after = (lax.rem(here + 1, rows), mine)
    before = (lax.rem(here + rows - 1, rows), mine)
    down = remote(to_next, from_prev, halo_s.at[0], halo_r.at[0], after)
    up = remote(to_prev, from_next, halo_s.at[1], halo_r.at[1], before)

    def add_products(layer, low, size, base, touched):
        for q in range(4):
            a, b = q // 2, q % 2
            left = vbuf[layer, q, low : low + size, pl.ds(base, 2 * LANE)]
            for step in range(3):
                right = wbuf[layer, pl.ds(base, 2 * LANE), step * 3 * LANE : (step + 1) * 3 * LANE]
                product = jnp.dot(left, right, preferred_element_type=F32)
                for column in range(3):
                    spot = (a + step) * 4 + b + column
                    block = product[:, column * LANE : (column + 1) * LANE]
                    where = (slice(EDGE + low, EDGE + low + size), slice(spot * LANE, (spot + 1) * LANE))
                    if spot in touched:
                        yext[where] += block
                    else:
                        yext[where] = block
                        touched.add(spot)

    def fill(layer, k, chip):
        low, size = parts[k]
        side = lax.rem(layer, 2)
        rows_here = slice(low, low + size)
        lanes = pl.ds(pl.multiple_of(chip * 2 * LANE, 2 * LANE), 2 * LANE)

        def kept(which):
            return mask_of(mask_ref, which, EDGE + low, size)

        def activation(q):
            scale, offset = (
                jnp.concatenate([coef[side, chip * 2, n : n + 1], coef[side, chip * 2 + 1, n : n + 1]], axis=1)
                for n in range(2)
            )
            y = raw[side, q, rows_here, lanes].astype(F32) * scale + offset
            return y * jax.nn.sigmoid(y)

        @pl.when(layer == 0)
        def _():
            for q in range(4):
                vbuf[layer, q, rows_here, lanes] = raw[side, q, rows_here, lanes]

        @pl.when(jnp.logical_and(layer != 0, layer != POOL + 1))
        def _():
            for q in range(4):
                block = activation(q)
                if low + size > count:
                    block = jnp.where(kept(M_VALID), block, 0.0)
                vbuf[layer, q, rows_here, lanes] = block.astype(BF16)

        @pl.when(layer == POOL + 1)
        def _():
            pooled = smooth_max([activation(q) for q in range(4)])
            for q in range(4):
                vbuf[layer, q, rows_here, lanes] = jnp.where(kept(M_HIT + q), pooled, 0.0).astype(BF16)

    def at(low, size, spot):
        return yext[low : low + size, spot * LANE : (spot + 1) * LANE]

    greet([partner, across, diagonal] + row_peers(rows))
    if inside:
        own_rows = gather.rows_of(0, gather.low)
        for layer in range(layers):
            source = w_refs[layer // (layers // 2)]
            for block in range(9):
                lanes = slice(block * LANE, (block + 1) * LANE)
                wbuf[layer, own_rows, lanes] = source[layer % (layers // 2), 8 - block]
            if layer == 0:
                for piece in range(3):
                    first_gather.start(0, piece)
            elif layer <= 1:
                gather.start(layer)
    else:
        load(0).start()
    split_planes(v_ref, wide, count)
    for q in range(4):
        raw[0, q, :, own_lanes] = plane(wide, q).astype(BF16)
    to_core(0).start()
    for k in range(len(pieces)):
        to_far(0, k).start()
    yext[:EDGE, :] = jnp.zeros((EDGE, yext.shape[1]), F32)
    yext[EDGE + padded :, :] = jnp.zeros((EDGE, yext.shape[1]), F32)
    fill_masks(group_ref, here * count, count, padded, switch_ref, mask_ref)
    if inside:
        for piece in range(3):
            for step in range(1, rows // 2):
                first_gather.forward(0, step, piece)
        for piece in range(3):
            first_gather.wait(0, piece)

    def layer_step(layer):
        more = layer + 1 < layers
        def gather_at(point):
            if not inside:
                return
            for turn, actions in GATHER_PLAN[point].items():

                @pl.when(layer == turn)
                def _(actions=actions):
                    for action, which, step in actions:
                        if action == "pass":
                            gather.forward(which, step)
                        elif action == "out":
                            gather.spread(which, step).start()
                        else:
                            gather.across(which, 0).start()

        if not inside:
            load(layer).wait()

            @pl.when(more)
            def _():
                load(layer + 1).start()

        to_core(layer).wait_recv()

        @pl.when(layer > 0)
        def _():
            coef_copy(layer, 0).wait_recv()

        def take(part):
            for k, piece in enumerate(pieces):
                if piece[0] == part:
                    to_far(layer, k).wait_recv()
            pass_on(layer, part).start()

        for k in range(len(parts)):
            fill(layer, k, half)
        take(0)
        take(1)
        if inside:

            @pl.when(layer > 0)
            def _():
                gather.wait(layer)

            save(layer, 2).start()
        add_products(layer, 0, padded, own_base, set())

        @pl.when(layer > 0)
        def _():
            for k in range(1, 3):
                coef_copy(layer, k).wait_recv()

        def far_products(k):
            pass_on(layer, k).wait_recv()
            low, size = parts[k]
            fill(layer, k, 1 - half)
            add_products(layer, low, size, far_base, set(range(16)))
            if k != 1:
                return
            for lane, spot in enumerate((12, 13, 14, 15, 7, 11)):
                to_next[:, lane * LANE : (lane + 1) * LANE] = at(count, EDGE, spot).astype(BF16)
            for lane, spot in enumerate((0, 1, 2, 3, 4, 8)):
                to_prev[:, lane * LANE : (lane + 1) * LANE] = at(EDGE, EDGE, spot).astype(BF16)

            @pl.when(here + 1 < rows)
            def _():
                down.start()

            @pl.when(here > 0)
            def _():
                up.start()

        def receive_halos():
            @pl.when(here > 0)
            def _():
                down.wait_recv()
                up.wait_send()
                for lane, spot in enumerate((12, 13, 14, 15, 7, 11)):
                    received = from_prev[:, lane * LANE : (lane + 1) * LANE].astype(F32)
                    yext[:EDGE, spot * LANE : (spot + 1) * LANE] = received

            @pl.when(here + 1 < rows)
            def _():
                up.wait_recv()
                down.wait_send()
                for lane, spot in enumerate((0, 1, 2, 3, 4, 8)):
                    received = from_next[:, lane * LANE : (lane + 1) * LANE].astype(F32)
                    yext[EDGE + count : 2 * EDGE + count, spot * LANE : (spot + 1) * LANE] = received

        def over_columns(kept, first, begin, end):
            low, size = EDGE + begin, end - begin
            go_left = mask_of(mask_ref, M_LEFT, low, size)
            go_right = mask_of(mask_ref, M_RIGHT, low, size)
            kept[low : low + size, :LANE] = at(low, size, first + 1) + jnp.where(
                go_left, at(low - 1, size, first + 3), 0.0
            )
            kept[low : low + size, LANE:] = at(low, size, first + 2) + jnp.where(
                go_right, at(low + 1, size, first), 0.0
            )

        def assemble(begin, end, sums_so_far):
            low, size = EDGE + begin, end - begin
            go_left = mask_of(mask_ref, M_LEFT, low, size)
            go_right = mask_of(mask_ref, M_RIGHT, low, size)
            total, squares = sums_so_far
            for q in range(4):
                a, b = q // 2, q % 2
                lanes = slice(b * LANE, (b + 1) * LANE)
                kept, sign = (over, -1) if a == 0 else (under, 1)
                rowwise = by_width(
                    mask_ref, low, size, lambda w: kept[low + sign * w : low + sign * w + size, lanes]
                )
                z = at(low, size, (a + 1) * 4 + b + 1)
                z = z + jnp.where(mask_of(mask_ref, (M_UP, M_DOWN)[a], low, size), rowwise, 0.0)
                if b == 0:
                    z = z + jnp.where(go_left, at(low - 1, size, (a + 1) * 4 + 3), 0.0)
                else:
                    z = z + jnp.where(go_right, at(low + 1, size, (a + 1) * 4), 0.0)
                if end > count:
                    z = jnp.where(mask_of(mask_ref, M_VALID, low, size), z, 0.0)
                zbuf[layer, q, begin:end] = z
                total = total + jnp.sum(z, axis=0, keepdims=True)
                squares = squares + jnp.sum(z * z, axis=0, keepdims=True)
            return total, squares

        def prepare(k):
            _, low, size = pieces[k]
            for q in range(4):
                piece = zbuf[layer, q, low : low + size] - local
                raw[lax.rem(layer + 1, 2), q, low : low + size, own_lanes] = piece.astype(BF16)

        gather_at("products")
        take(2)
        far_products(0)
        far_products(1)
        take(3)
        far_products(2)
        far_products(3)
        take(4)
        gather_at("parts")
        near, widest = min(WIDTHS), max(WIDTHS)
        (_, top, size), (_, bottom, last_size) = pieces[:2]
        first = (top, top + size)
        last = (bottom, bottom + last_size)
        over_ready = [(n - widest, ceil_to(m - near, 8)) for n, m in (first, last)]
        under_ready = [((n + near) // 8 * 8, m + widest) for n, m in (first, last)]
        for kept, spot, ready in ((over, 12, over_ready), (under, 0, under_ready)):
            for begin, end in ready:
                over_columns(kept, spot, begin, end)
        none = (jnp.zeros((1, LANE), F32),) * 2
        inner = assemble(*last, assemble(*first, none))
        local = inner[0] / (4.0 * (size + last_size))

        @pl.when(more)
        def _():
            for k in range(2):
                prepare(k)
                to_far(layer + 1, k).start()

        gather_at("outer")
        far_products(4)
        save(layer, 0).start()
        receive_halos()
        over_rest = [(8 - EDGE, over_ready[0][0]), (over_ready[0][1], over_ready[1][0]), (over_ready[1][1], padded)]
        under_rest = [(0, under_ready[0][0]), (under_ready[0][1], under_ready[1][0]), (under_ready[1][1], padded + EDGE - 8)]
        for kept, spot, rest in ((over, 12, over_rest), (under, 0, under_rest)):
            for begin, end in rest:
                over_columns(kept, spot, begin, end)
        total, squares = assemble(last[1], padded, assemble(first[1], last[0], assemble(0, first[0], inner)))
        save(layer, 1).start()
        own = jnp.concatenate([total, squares, jnp.zeros((6, LANE), F32)], axis=0)
        channel = (sums.at[layer], sum_s.at[layer], sum_r.at[layer])
        send_sums(rows, own, *channel)

        @pl.when(more)
        def _():
            for k in range(2, len(pieces)):
                prepare(k)
                if k < 4:
                    to_far(layer + 1, k).start()
            to_core(layer + 1).start()

        for k in range(len(pieces)):
            to_far(layer, k).wait_send()
        for k in range(len(parts)):
            pass_on(layer, k).wait_send()
        to_core(layer).wait_send()

        @pl.when(layer > 0)
        def _():
            for k in range(3):
                coef_copy(layer, k).wait_send()

        gather_at("sums")
        both = add_sums(rows, *channel)
        mean = both[0:1] / pixels
        inverse = lax.rsqrt(both[1:2] / pixels - mean * mean + EPSILON)
        stat_ref[layer] = jnp.concatenate([mean, inverse, jnp.zeros((6, LANE), F32)], axis=0)
        scale = gb_ref[layer, 0:1] * inverse

        @pl.when(more)
        def _():
            offset = scale * (local - mean) + gb_ref[layer, 1:2]
            coef[lax.rem(layer + 1, 2), mine] = jnp.concatenate([scale, offset, jnp.zeros((6, LANE), F32)], axis=0)
            for k in range(3):
                coef_copy(layer + 1, k).start()
            for k in range(4, len(pieces)):
                to_far(layer + 1, k).start()

        gather_at("norm")

        @pl.when(layer + 1 == layers)
        def _():
            for q in range(4):
                y = scale * (zbuf[layer, q] - mean) + gb_ref[layer, 1:2]
                set_plane(wide, q, 0, y * jax.nn.sigmoid(y))
            next_ref[...] = wide[: 4 * count].astype(BF16)

    each(layers, layer_step)

    def drain(layer):
        if inside:

            @pl.when(layer > 0)
            def _():
                gather.drain(layer)

        for which in range(3 if inside else 2):
            save(layer, which).wait()

    each(layers, drain)
    if inside:
        for piece in range(3):
            first_gather.drain(0, piece)


def backward_kernel(inside, layers, rows, count, padded, pixels, *refs):
    refs = list(refs)
    g_ref, stat_ref, gb_ref, mask_ref, z_in, full_in, w_in = refs[:7]
    del refs[:7]
    out_ref, gbgrad_ref = refs[:2]
    wgrad_refs = refs[2 : 3 + inside]
    del refs[: 3 + inside]
    (
        grad_ref, wide, partial, zbuf, fbuf, wbuf, dk, gy, gext, above, below, patch, part, keep, core_out, core_in, x_out, x_in,
        to_next, to_prev, from_prev, from_next, sums,
        core_s, core_r, x_s, x_r, halo_s, halo_r, sum_s, sum_r, load_sem, out_sem,
    ) = refs[:33]
    mine, here = lax.axis_index("grp"), lax.axis_index("rows")
    half, core = mine // 2, lax.rem(mine, 2)
    partner, across = grp_peers()
    own_lanes, other_lanes = lanes_of(core), lanes_of(1 - core)
    own_base = pl.multiple_of(half * 2 * LANE, 2 * LANE)
    far_base = pl.multiple_of((1 - half) * 2 * LANE, 2 * LANE)
    if inside:
        first, second, third, total_ref = refs[33:37]
        shard = dk.shape[1] // rows
        scatter = Scatter(rows, shard, dk, first, second, third, total_ref, wgrad_refs, refs[37:41])

    def load(turn, which):
        src, dst = ((z_in, zbuf), (w_in, wbuf), (full_in, fbuf))[which]
        side = lax.rem(turn, 2)
        return pltpu.make_async_copy(src.at[layers - 1 - turn], dst.at[side], load_sem.at[side, which])

    def save(turn):
        slot = lax.rem(turn, 3)
        return pltpu.make_async_copy(dk.at[slot], wgrad_refs[0].at[layers - 1 - turn], out_sem.at[slot])

    for turn in range(2):
        for which in range(3):
            load(turn, which).start()
    after = (lax.rem(here + 1, rows), mine)
    before = (lax.rem(here + rows - 1, rows), mine)
    split_planes(g_ref, wide, count)
    gext[:EDGE, :] = jnp.zeros((EDGE, 4 * LANE), F32)
    gext[EDGE + padded :, :] = jnp.zeros((EDGE, 4 * LANE), F32)
    greet([partner, across] + row_peers(rows))
    load(0, 0).wait()
    partial[...] = jnp.zeros_like(partial)

    def norm_of(layer):
        return stat_ref[layer, 0:1], stat_ref[layer, 1:2], gb_ref[layer, 0:1], gb_ref[layer, 1:2]

    def shifted(turn, q):
        mean, inverse, gain, shift = norm_of(layers - 1 - turn)
        normed = (zbuf[lax.rem(turn, 2), q] - mean) * inverse
        return normed, gain * normed + shift

    def begin(turn, q, grad):
        normed, y = shifted(turn, q)
        s = jax.nn.sigmoid(y)
        grad = jnp.where(mask_of(mask_ref, M_VALID, EDGE, padded), grad * s * (1.0 + y * (1.0 - s)), 0.0)
        gy[q] = grad
        partial[0:1] += jnp.sum(grad, axis=0, keepdims=True)
        partial[1:2] += jnp.sum(grad * normed, axis=0, keepdims=True)

    def taps(q, step):
        first = (q // 2 + step) * 4 + q % 2
        return patch[:, first * LANE : (first + 3) * LANE]

    def layer_step(turn):
        layer = layers - 1 - turn
        side, slot = lax.rem(turn, 2), lax.rem(turn, 3)
        last = turn + 1 == layers
        down = remote(to_next, from_prev.at[side], halo_s.at[0], halo_r.at[side, 0], after)
        up = remote(to_prev, from_next.at[side], halo_s.at[1], halo_r.at[side, 1], before)
        mean, inverse, gain, _ = norm_of(layer)
        valid = mask_of(mask_ref, M_VALID, EDGE, padded)

        @pl.when(layer == POOL)
        def _():
            load(turn, 0).wait()
            pooled_grad = jnp.zeros((padded, LANE), F32)
            for q in range(4):
                pooled_grad = jnp.where(mask_of(mask_ref, M_HIT + q, EDGE, padded), grad_ref[q], pooled_grad)
            for q in range(4):
                _, y = shifted(turn, q)
                gy[q] = y * jax.nn.sigmoid(y)
            pooled = smooth_max([gy[q] for q in range(4)])
            partial[...] = jnp.zeros_like(partial)
            for q in range(4):
                begin(turn, q, pooled_grad * (jnp.exp(gy[q] - pooled) * 0.25))

        def spread(buf, low, planes):
            for lane, q in enumerate(planes):
                piece = slice(low, low + EDGE)
                normed = (zbuf[side, q, piece] - mean) * inverse
                buf[:, 2 * lane * LANE : (2 * lane + 1) * LANE] = gy[q, piece].astype(BF16)
                buf[:, (2 * lane + 1) * LANE : (2 * lane + 2) * LANE] = normed.astype(BF16)

        spread(to_next, count - EDGE, (2, 3, 1))
        spread(to_prev, 0, (0, 1, 2))

        @pl.when(here + 1 < rows)
        def _():
            down.start()

        @pl.when(here > 0)
        def _():
            up.start()

        own = partial[...]
        channel = (sums.at[side], sum_s.at[side], sum_r.at[side])
        send_sums(rows, own, *channel)
        both = add_sums(rows, *channel)
        gbgrad_ref[layer] = both
        if inside:

            @pl.when(turn > 0)
            def _():
                scatter.start(turn - 1, scatter.order()[2:])
                for step in scatter.order()[:2]:
                    scatter.forward(turn - 1, step)


        def conv_grad(grad, normed):
            out = inverse * gain * (grad - both[0:1] / pixels - normed * both[1:2] / pixels)
            return out.astype(BF16).astype(F32)

        for q in range(4):
            normed, _ = shifted(turn, q)
            gext[EDGE : EDGE + padded, q * LANE : (q + 1) * LANE] = jnp.where(
                valid, conv_grad(gy[q], normed), 0.0
            )

        def receive(buf, low, planes):
            for lane, q in enumerate(planes):
                grad = buf[side, :, 2 * lane * LANE : (2 * lane + 1) * LANE].astype(F32)
                normed = buf[side, :, (2 * lane + 1) * LANE : (2 * lane + 2) * LANE].astype(F32)
                gext[low : low + EDGE, q * LANE : (q + 1) * LANE] = conv_grad(grad, normed)

        @pl.when(here > 0)
        def _():
            down.wait_recv()
            up.wait_send()
            receive(from_prev, 0, (2, 3, 1))

        @pl.when(here + 1 < rows)
        def _():
            up.wait_recv()
            down.wait_send()
            receive(from_next, EDGE + count, (0, 1, 2))

        low, size = EDGE - 8, padded + 16
        for kept, which, sign, lanes in (
            (above, M_UP, -1, slice(2 * LANE, 4 * LANE)),
            (below, M_DOWN, 1, slice(0, 2 * LANE)),
        ):
            rowwise = by_width(
                mask_ref, low, size, lambda w: gext[low + sign * w : low + sign * w + size, lanes]
            )
            kept[...] = jnp.where(mask_of(mask_ref, which, low, size), rowwise, 0.0)
        go_left = mask_of(mask_ref, M_LEFT, EDGE, padded)
        go_right = mask_of(mask_ref, M_RIGHT, EDGE, padded)
        for step, (kept, top, lane) in enumerate(
            ((above, 8, 0), (gext, EDGE, 0), (gext, EDGE, 2 * LANE), (below, 8, 0))
        ):
            even, odd = slice(lane, lane + LANE), slice(lane + LANE, lane + 2 * LANE)
            blocks = [
                jnp.where(go_left, kept[top - 1 : top - 1 + padded, odd], 0.0),
                kept[top : top + padded, even],
                kept[top : top + padded, odd],
                jnp.where(go_right, kept[top + 1 : top + 1 + padded, even], 0.0),
            ]
            for column, block in enumerate(blocks):
                spot = step * 4 + column
                patch[:, spot * LANE : (spot + 1) * LANE] = block.astype(BF16)

        def kernel_grad():
            for step in range(3):
                total = None
                for q in range(4):
                    product = lax.dot_general(
                        fbuf[side, q], taps(q, step), (((0,), (0,)), ((), ())), preferred_element_type=F32
                    )
                    total = product if total is None else total + product
                dk[slot, :, step * 3 * LANE : (step + 1) * 3 * LANE] = total.astype(BF16)
            if not inside:
                save(turn).start()

        def scatter_forward(step):
            @pl.when(turn > 0)
            def _():
                scatter.forward(turn - 1, step)

        if inside:

            @pl.when(turn > 1)
            def _():
                scatter.finish(turn - 2, layer + 2)
                scatter.drain(turn - 2)

        load(turn, 1).wait()
        load(turn, 2).wait()
        if not inside:

            @pl.when(turn > 2)
            def _():
                save(turn - 3).wait()

        @pl.when(last)
        def _():
            kernel_grad()
            if inside:
                scatter.start(turn, scatter.order())

        def input_grad(q, base):
            total = None
            for step in range(3):
                right = wbuf[side, pl.ds(base, 2 * LANE), step * 3 * LANE : (step + 1) * 3 * LANE]
                product = lax.dot_general(
                    taps(q, step), right, (((1,), (1,)), ((), ())), preferred_element_type=F32
                )
                total = product if total is None else total + product
            part[...] = total

        def to_core(spot):
            return remote(
                core_out.at[side, spot], core_in.at[side, spot],
                core_s.at[side, spot], core_r.at[side, spot], partner,
            )

        def to_far(q):
            return remote(x_out.at[side, q], x_in.at[side, q], x_s.at[side, q], x_r.at[side, q], across)

        def send_across(q):
            to_core(q).wait_recv()
            x_out[side, q] = (keep[q] + core_in[side, q].astype(F32)).astype(BF16)
            to_far(q).start()

        for spot in range(8):
            input_grad(spot % 4, far_base if spot < 4 else own_base)
            core_out[side, spot] = part[:, other_lanes].astype(BF16)
            keep[spot] = part[:, own_lanes]
            to_core(spot).start()
            if 2 <= spot < 6:
                send_across(spot - 2)
            if inside and spot == 3:
                for step in scatter.order()[2:-1]:
                    scatter_forward(step)

        @pl.when(jnp.logical_not(last))
        def _():
            kernel_grad()
            if inside:
                scatter.start(turn, scatter.order()[:2])

        @pl.when(turn + 2 < layers)
        def _():
            for which in range(3):
                load(turn + 2, which).start()

        if inside:
            scatter_forward(0)
        if inside:

            pass

        def arrived(q):
            to_core(4 + q).wait_recv()
            to_far(q).wait_recv()
            return keep[4 + q] + core_in[side, 4 + q].astype(F32) + x_in[side, q].astype(F32)

        begin_next = jnp.logical_and(jnp.logical_not(last), layer - 1 != POOL)

        @pl.when(begin_next)
        def _():
            load(turn + 1, 0).wait()
            partial[...] = jnp.zeros_like(partial)
            for q in range(4):
                begin(turn + 1, q, arrived(q))

        @pl.when(layer - 1 == POOL)
        def _():
            for q in range(4):
                grad_ref[q] = arrived(q)

        @pl.when(last)
        def _():
            for q in range(4):
                if inside:
                    scatter.forward(turn, scatter.order()[q])
                grad_ref[q] = arrived(q)

        for spot in range(8):
            to_core(spot).wait_send()
        for q in range(4):
            to_far(q).wait_send()

    for q in range(4):
        begin(0, q, plane(wide, q))
    each(layers, layer_step)
    for q in range(4):
        set_plane(wide, q, 0, grad_ref[q])
    out_ref[...] = wide[: 4 * count].astype(BF16)
    if inside:
        for turn in (layers - 2, layers - 1):
            scatter.finish(turn, layers - 1 - turn)
            scatter.drain(turn)
    else:
        for turn in range(layers - 3, layers):
            save(turn).wait()


VM = pl.BlockSpec(memory_space=pltpu.VMEM)
HBM = pl.BlockSpec(memory_space=pl.ANY)
LIMIT = 56 * 1024 * 1024
DMA = pltpu.SemaphoreType.DMA


def forward_block(inside, rows, count, padded, pixels, image_group, switches, features, pairs, weights):
    layers, channels, taps = pairs.shape[0], 4 * LANE, 9 * LANE
    ext = padded + 2 * EDGE
    n_parts = len(row_parts(padded, count))
    far = rows // 2
    shape = jax.ShapeDtypeStruct
    out = pl.pallas_call(
        functools.partial(forward_kernel, inside, layers, rows, count, padded, pixels),
        name="forward_block",
        out_shape=(
            shape((4 * count, LANE), BF16),
            shape((layers, 8, LANE), F32),
            shape((ext, LANE), F32),
            shape((layers, 4, padded, LANE), F32),
            shape((layers, 4, padded, channels), BF16),
            shape((layers, channels, taps) if inside else (1, 16, LANE), BF16),
        ),
        in_specs=[pl.BlockSpec(memory_space=pltpu.SMEM), VM, VM, VM] + [VM if inside else HBM] * len(weights),
        out_specs=(VM, VM, VM, HBM, HBM, HBM),
        scratch_shapes=[
            pltpu.VMEM((layers, 4, padded, channels), BF16),
            pltpu.VMEM((layers, channels, taps), BF16),
            pltpu.VMEM((layers, 4, padded, LANE), F32),
            pltpu.VMEM((2, 4, padded, channels), BF16),
            pltpu.VMEM((2, 4, 8, LANE), F32),
            pltpu.VMEM((ext, 16 * LANE), F32),
            pltpu.VMEM((ext, 2 * LANE), F32),
            pltpu.VMEM((ext, 2 * LANE), F32),
            pltpu.VMEM((4 * padded, LANE), F32),
        ]
        + [pltpu.VMEM((EDGE, 6 * LANE), BF16)] * 4
        + [pltpu.VMEM((layers, rows, 8, LANE), F32)]
        + [DMA((layers,))] * 2
        + [DMA((layers, len(far_pieces(row_parts(padded, count)))))] * 2
        + [DMA((layers, n_parts))] * 2
        + [DMA((2,))] * 2
        + [DMA((layers, rows - 1))] * 2
        + [DMA((layers, 3))] * 3
        + [DMA((layers, far - 1))] * 2
        + [DMA((layers, far))] * 2
        + [DMA((3, far - 1))] * 2
        + [DMA((3, far))] * 2,
        compiler_params=pltpu.CompilerParams(
            collective_id=0, has_side_effects=True, vmem_limit_bytes=LIMIT
        ),
    )(image_group, switches, features, pairs, *weights)
    return out[:5] + ((out[5] if inside else weights[0]),)


def backward_block(inside, rows, count, padded, pixels, grad, z, stat, pairs, masks, full, weight):
    layers, channels, taps = weight.shape
    ext = padded + 2 * EDGE
    shard = channels // rows
    far = rows // 2
    shape = jax.ShapeDtypeStruct
    scratch = [
        pltpu.VMEM((4, padded, LANE), F32),
        pltpu.VMEM((4 * padded, LANE), F32),
        pltpu.VMEM((8, LANE), F32),
        pltpu.VMEM((2, 4, padded, LANE), F32),
        pltpu.VMEM((2, 4, padded, channels), BF16),
        pltpu.VMEM((2, channels, taps), BF16),
        pltpu.VMEM((3, channels, taps), BF16),
        pltpu.VMEM((4, padded, LANE), F32),
        pltpu.VMEM((ext, 4 * LANE), F32),
        pltpu.VMEM((padded + 16, 2 * LANE), F32),
        pltpu.VMEM((padded + 16, 2 * LANE), F32),
        pltpu.VMEM((padded, 16 * LANE), BF16),
        pltpu.VMEM((padded, 2 * LANE), F32),
        pltpu.VMEM((8, padded, LANE), F32),
        pltpu.VMEM((2, 8, padded, LANE), BF16),
        pltpu.VMEM((2, 8, padded, LANE), BF16),
        pltpu.VMEM((2, 4, padded, LANE), BF16),
        pltpu.VMEM((2, 4, padded, LANE), BF16),
    ]
    scratch += [pltpu.VMEM((EDGE, 6 * LANE), BF16)] * 2 + [pltpu.VMEM((2, EDGE, 6 * LANE), BF16)] * 2
    scratch += [pltpu.VMEM((2, rows, 8, LANE), F32)]
    scratch += [DMA((2, 8))] * 2 + [DMA((2, 4))] * 2 + [DMA((2,)), DMA((2, 2))] + [DMA((2, rows - 1))] * 2
    scratch += [DMA((2, 3)), DMA((3,))]
    wgrads = [shape((layers, channels, taps), BF16)]
    if inside:
        wgrads = [shape((layers // 2, 9, shard, LANE), F32)] * 2
        scratch += [
            pltpu.VMEM((3, far, shard, taps), BF16),
            pltpu.VMEM((3, far - 1, shard, taps), BF16),
            pltpu.VMEM((3, far - 1, shard, taps), BF16),
            pltpu.VMEM((3, shard, taps), F32),
        ]
        scratch += [DMA((3, far))] * 2 + [DMA((3, far - 1))] * 2
    return pl.pallas_call(
        functools.partial(backward_kernel, inside, layers, rows, count, padded, pixels),
        name="backward_block",
        out_shape=[shape((4 * count, LANE), BF16), shape((layers, 8, LANE), F32)] + wgrads,
        in_specs=[VM] * 4 + [HBM] * 3,
        out_specs=[VM, VM] + [VM if inside else HBM] * len(wgrads),
        scratch_shapes=scratch,
        compiler_params=pltpu.CompilerParams(
            collective_id=1, has_side_effects=True, vmem_limit_bytes=LIMIT
        ),
    )(grad, stat, pairs, masks, z, full, weight)


def shards(
    features, image_group, switches, enc_weight, dec_weight,
    enc_gain, enc_bias, dec_gain, dec_bias, d_decoded,
):
    rows = lax.axis_size("rows")
    count = features.shape[0] // 4
    padded = ceil_to(count, 16)
    pixels = float(features.shape[0] * rows)
    depth, shard = enc_weight.shape[0], enc_weight.shape[2]
    inside = shard % 16 == 0 and rows == 8 and 2 * depth == 6
    sizes = (rows, count, padded, pixels)
    weights = [enc_weight, dec_weight]
    if not inside:
        both = jnp.concatenate(weights)
        flat = jnp.transpose(both[:, ::-1], (0, 2, 1, 3)).reshape(both.shape[0], shard, -1)
        weights = [lax.all_gather(flat, "rows", axis=1, tiled=True)]
    pairs = jnp.stack([jnp.concatenate([enc_gain, dec_gain]), jnp.concatenate([enc_bias, dec_bias])], axis=1)
    pairs = jnp.pad(pairs, ((0, 0), (0, 6), (0, 0)))

    hits = jnp.pad(switches, (EDGE, padded - count + EDGE), constant_values=-LANE)[:, None]
    decoded, stat, masks, z, full, weight = forward_block(
        inside, *sizes, image_group, hits, features, pairs, weights
    )
    grad, pair_grads, *wgrads = backward_block(
        inside, *sizes, d_decoded, z, stat, pairs, masks, full, weight
    )
    if not inside:
        wgrad = lax.psum_scatter(wgrads[0], "rows", scatter_dimension=1, tiled=True).astype(F32)
        wgrad = jnp.transpose(wgrad.reshape(2 * depth, shard, 9, -1)[:, :, ::-1], (0, 2, 1, 3))
        wgrads = [wgrad[:depth], wgrad[depth:]]
    return (
        decoded,
        grad,
        *wgrads,
        pair_grads[:depth, 1],
        pair_grads[:depth, 0],
        pair_grads[depth:, 1],
        pair_grads[depth:, 0],
    )


def solution(mesh):
    wide = P("rows", "grp")
    kernels = P(None, None, "rows", "grp")
    vector = P(None, "grp")
    return jax.shard_map(
        shards,
        mesh=mesh,
        in_specs=(wide, P(), P("rows"), kernels, kernels, vector, vector, vector, vector, wide),
        out_specs=(wide, wide, kernels, kernels, vector, vector, vector, vector),
        check_vma=False,
    )
```

```python
import functools

import jax
import jax.numpy as jnp
from jax import lax
from jax.experimental import pallas as pl
from jax.experimental.pallas import tpu as pltpu
from jax.sharding import PartitionSpec as P

SIZES = ((15, 20), (18, 24), (30, 40))
WIDTHS = tuple(w for _, w in SIZES)
EDGE = 48
EPSILON = 1e-05
MESH = pl.DeviceIdType.MESH
F32 = jnp.float32
BF16 = jnp.bfloat16
LANE = 128
(M_W0, M_W1, M_UP, M_DOWN, M_LEFT, M_RIGHT, M_VALID, M_HIT) = range(8)
POOL = 2


def ceil_to(value, step):
    return -(-value // step) * step


def fill_masks(group_ref, first_window, count, padded, switch_ref, mask_ref):
    shape = (padded + 2 * EDGE, 1)
    local = lax.broadcasted_iota(jnp.int32, shape, 0) - EDGE
    windows = local + first_window

    start = jnp.int32(0)
    base = height = width = jnp.zeros(shape, jnp.int32)
    for image in range(group_ref.shape[0]):
        group = group_ref[image]
        tall, wide = (
            jnp.where(group == 0, SIZES[0][k], jnp.where(group == 1, SIZES[1][k], SIZES[2][k])) for k in range(2)
        )
        end = start + tall * wide
        member = (windows >= start) & (windows < end)
        base, height, width = (
            jnp.where(member, new, old) for new, old in ((start, base), (tall, height), (wide, width))
        )
        start = end
    inside = width > 0
    position = windows - base
    row = jnp.zeros(shape, jnp.int32)
    for tall, wide in SIZES:
        quotient = jnp.floor((position.astype(F32) + 0.5) * (1.0 / wide)).astype(jnp.int32)
        row = jnp.where(width == wide, quotient, row)
    column = position - row * width
    masks = [
        width == WIDTHS[0],
        width == WIDTHS[1],
        inside & (row > 0),
        inside & (row < height - 1),
        inside & (column > 0),
        inside & (column < width - 1),
        (local >= 0) & (local < count),
    ]
    lane = lax.broadcasted_iota(jnp.int32, (shape[0], LANE), 1)
    table = (lane - M_HIT == switch_ref[...]).astype(F32)
    for k, mask in enumerate(masks):
        table = jnp.where((lane == k) & mask, 1.0, table)
    mask_ref[...] = table


def split_planes(stream_ref, wide_ref, count):
    wide_ref[: 4 * count] = stream_ref[...].astype(F32)
    wide_ref[4 * count :] = jnp.zeros((wide_ref.shape[0] - 4 * count, LANE), F32)


def plane(wide_ref, q):
    return wide_ref[pl.ds(q, wide_ref.shape[0] // 4, stride=4), :]


def set_plane(wide_ref, q, low, block):
    wide_ref[pl.ds(4 * low + q, block.shape[0], stride=4), :] = block


def mask_of(mask_ref, which, low, count):
    return mask_ref[low : low + count, which : which + 1] > 0.5


def by_width(mask_ref, low, count, shifted):
    return jnp.where(
        mask_of(mask_ref, M_W0, low, count),
        shifted(WIDTHS[0]),
        jnp.where(mask_of(mask_ref, M_W1, low, count), shifted(WIDTHS[1]), shifted(WIDTHS[2])),
    )


def smooth_max(blocks):
    total = sum(jnp.exp(block) for block in blocks)
    return jnp.log(total * 0.25)


def row_peers(rows):
    here = lax.axis_index("rows")
    there = lax.axis_index("grp")
    order = sorted(range(1, rows), key=lambda k: -min(k, rows - k))
    return [(lax.rem(here + k, rows), there) for k in order]


def grp_peers():
    here = lax.axis_index("rows")
    mine = lax.axis_index("grp")
    half, core = mine // 2, lax.rem(mine, 2)
    return (here, half * 2 + 1 - core), (here, (1 - half) * 2 + core)


def greet(peers):
    barrier = pltpu.get_barrier_semaphore()
    for peer in peers:
        pl.semaphore_signal(barrier, inc=1, device_id=peer, device_id_type=MESH)
    pl.semaphore_wait(barrier, len(peers))


def remote(src, dst, send, recv, peer):
    return pltpu.make_async_remote_copy(
        src_ref=src, dst_ref=dst, send_sem=send, recv_sem=recv, device_id=peer, device_id_type=MESH
    )


def sums_copies(rows, buf, send, recv):
    return [
        remote(buf.at[0], buf.at[k + 1], send.at[k], recv.at[k], peer) for k, peer in enumerate(row_peers(rows))
    ]


def send_sums(rows, own, buf, send, recv):
    buf[0] = own
    for copy in sums_copies(rows, buf, send, recv):
        copy.start()


def add_sums(rows, buf, send, recv):
    for copy in sums_copies(rows, buf, send, recv):
        copy.wait()
    total = buf[0]
    for k in range(1, rows):
        total = total + buf[k]
    return total


def row_parts(padded, count):
    tail = (count - EDGE) // 16 * 16
    inner, start, steps = [], EDGE, 3
    for k in range(steps):
        size = min(ceil_to(-(-(tail - start) // (steps - k)), 16), tail - start)
        inner.append((start, size))
        start += size
    return [(0, EDGE), (tail, padded - tail), inner[0], inner[2], inner[1]]


REACH = max(WIDTHS) + 1


def far_pieces(parts):
    low, size = parts[4]
    first, last = (low - REACH) // 8 * 8, ceil_to(low + size + REACH, 8)
    return [
        (2, parts[2][0], first - parts[2][0]),
        (3, last, parts[3][0] + parts[3][1] - last),
        (0, *parts[0]),
        (1, *parts[1]),
        (2, first, parts[2][0] + parts[2][1] - first),
        (3, parts[3][0], last - parts[3][0]),
        (4, low, size),
    ]


def lanes_of(block):
    return pl.ds(pl.multiple_of(block * LANE, LANE), LANE)


class Gather:
    def __init__(self, rows, shard, buf, send, recv, pass_send, pass_recv):
        self.shard, self.buf = shard, buf
        self.far = rows // 2
        here, there = lax.axis_index("rows"), lax.axis_index("grp")
        self.high, self.low = here // 2, lax.rem(here, 2)
        self.there = there
        self.send, self.recv, self.pass_send, self.pass_recv = send, recv, pass_send, pass_recv

    def rows_of(self, step, low):
        block = lax.rem(self.high + step, self.far) * 2 + low
        return pl.ds(pl.multiple_of(block * self.shard, 16), self.shard)

    def block(self, layer, step, piece):
        lanes = slice(None) if piece is None else slice(piece * 3 * LANE, (piece + 1) * 3 * LANE)
        slot = layer if piece is None else piece
        return self.buf.at[layer, self.rows_of(step, self.low), lanes], slot

    def spread(self, layer, step, piece=None):
        own, slot = self.block(layer, 0, piece)
        peer = (lax.rem(self.high + step, self.far) * 2 + self.low, self.there)
        k = step - 1
        return remote(own, own, self.send.at[slot, k], self.recv.at[slot, k], peer)

    def across(self, layer, step, piece=None):
        part, slot = self.block(layer, self.far - step, piece)
        peer = (self.high * 2 + 1 - self.low, self.there)
        return remote(part, part, self.pass_send.at[slot, step], self.pass_recv.at[slot, step], peer)

    def start(self, layer, piece=None):
        for step in range(1, self.far):
            self.spread(layer, step, piece).start()
        self.across(layer, 0, piece).start()

    def forward(self, layer, step, piece=None):
        self.spread(layer, step, piece).wait_recv()
        self.across(layer, step, piece).start()

    def wait(self, layer, piece=None):
        for step in range(self.far):
            self.across(layer, step, piece).wait_recv()

    def drain(self, layer, piece=None):
        for step in range(1, self.far):
            self.spread(layer, step, piece).wait_send()
        for step in range(self.far):
            self.across(layer, step, piece).wait_send()


class Scatter:
    def __init__(self, rows, shard, grads, first, second, third, total, outs, semaphores):
        self.shard, self.grads, self.first, self.second, self.third = shard, grads, first, second, third
        self.total, self.outs, self.far = total, outs, rows // 2
        here, self.there = lax.axis_index("rows"), lax.axis_index("grp")
        self.high, self.low = here // 2, lax.rem(here, 2)
        self.semaphores = semaphores

    def rows_of(self, step, low):
        block = lax.rem(self.high + step, self.far) * 2 + low
        return pl.ds(pl.multiple_of(block * self.shard, 16), self.shard)

    def across(self, turn, step):
        slot = lax.rem(turn, 3)
        send, recv, _, _ = self.semaphores
        peer = (self.high * 2 + 1 - self.low, self.there)
        return remote(
            self.grads.at[slot, self.rows_of(step, 1 - self.low), :], self.first.at[slot, step],
            send.at[slot, step], recv.at[slot, step], peer,
        )

    def spread(self, turn, step):
        slot = lax.rem(turn, 3)
        _, _, send, recv = self.semaphores
        peer = (lax.rem(self.high + step, self.far) * 2 + self.low, self.there)
        k = step - 1
        return remote(
            self.second.at[slot, k], self.third.at[slot, k],
            send.at[slot, k], recv.at[slot, k], peer,
        )

    def order(self):
        return list(range(1, self.far)) + [0]

    def start(self, turn, steps):
        for step in steps:
            self.across(turn, step).start()

    def forward(self, turn, step):
        slot = lax.rem(turn, 3)
        self.across(turn, step).wait_recv()
        own = self.grads[slot, self.rows_of(step, self.low), :]
        total = own.astype(F32) + self.first[slot, step].astype(F32)
        if step == 0:
            self.total[slot] = total
        else:
            self.second[slot, step - 1] = total.astype(BF16)
            self.spread(turn, step).start()

    def finish(self, turn, layer):
        slot = lax.rem(turn, 3)
        for step in range(1, self.far):
            self.spread(turn, step).wait_recv()
        total = self.total[slot]
        for step in range(1, self.far):
            total = total + self.third[slot, step - 1].astype(F32)
        depth = self.outs[0].shape[0]

        def put(out, index):
            for block in range(9):
                out[index, 8 - block] = total[:, block * LANE : (block + 1) * LANE]

        @pl.when(layer < depth)
        def _():
            put(self.outs[0], layer)

        @pl.when(layer >= depth)
        def _():
            put(self.outs[1], layer - depth)

    def drain(self, turn):
        for step in range(self.far):
            self.across(turn, step).wait_send()
        for step in range(1, self.far):
            self.spread(turn, step).wait_send()


def each(count, body):
    lax.fori_loop(0, count, lambda i, carry: (body(i), carry)[1], 0)


GATHER_PLAN = {
    "products": {0: [("pass", 1, 1)]},
    "parts": {0: [("pass", 1, 2)]},
    "outer": {},
    "sums": {0: [("pass", 1, 3)]},
    "norm": {},
}
for turn in range(4):
    GATHER_PLAN["norm"][turn] = [("out", turn + 2, 1), ("out", turn + 2, 2), ("own", turn + 2, 0)]
    GATHER_PLAN["parts"][turn + 1] = [("pass", turn + 2, 1)]
    GATHER_PLAN["outer"][turn + 1] = [("out", turn + 2, 3), ("pass", turn + 2, 2)]
    GATHER_PLAN["sums"][turn + 1] = [("pass", turn + 2, 3)]


def forward_kernel(
    inside, layers, rows, count, padded, pixels, group_ref, switch_ref, v_ref, gb_ref, *refs
):
    w_refs, refs = refs[: 1 + inside], refs[1 + inside :]
    (
        next_ref, stat_ref, mask_ref, z_out, full_out, w_out,
        vbuf, wbuf, zbuf, raw, coef, yext, over, under, wide, to_next, to_prev, from_prev, from_next, sums,
        core_s, core_r, x_s, x_r, fwd_s, fwd_r, halo_s, halo_r, sum_s, sum_r, out_sem,
        coef_s, coef_r, w_s, w_r, wp_s, wp_r, first_s, first_r, first_ps, first_pr,
    ) = refs
    mine, here = lax.axis_index("grp"), lax.axis_index("rows")
    half = mine // 2
    partner, across = grp_peers()
    diagonal = (here, across[1] + partner[1] - mine)
    parts = row_parts(padded, count)
    pieces = far_pieces(parts)
    own_lanes, far_lanes = lanes_of(mine), lanes_of(across[1])
    own_base = pl.multiple_of(half * 2 * LANE, 2 * LANE)
    far_base = pl.multiple_of((1 - half) * 2 * LANE, 2 * LANE)
    shard = wbuf.shape[1] // rows
    gather = Gather(rows, shard, wbuf, w_s, w_r, wp_s, wp_r)
    first_gather = Gather(rows, shard, wbuf, first_s, first_r, first_ps, first_pr)

    def slab(layer, k, lanes):
        low, size = parts[k]
        return raw.at[lax.rem(layer, 2), :, pl.ds(low, size), lanes]

    def to_core(layer):
        whole = raw.at[lax.rem(layer, 2), :, :, own_lanes]
        return remote(whole, whole, core_s.at[layer], core_r.at[layer], partner)

    def to_far(layer, k):
        _, low, size = pieces[k]
        piece = raw.at[lax.rem(layer, 2), :, pl.ds(low, size), own_lanes]
        return remote(piece, piece, x_s.at[layer, k], x_r.at[layer, k], across)

    def pass_on(layer, k):
        piece = slab(layer, k, far_lanes)
        return remote(piece, piece, fwd_s.at[layer, k], fwd_r.at[layer, k], partner)

    def coef_copy(layer, k):
        own = coef.at[lax.rem(layer, 2), mine]
        return remote(own, own, coef_s.at[layer, k], coef_r.at[layer, k], (partner, across, diagonal)[k])

    def load(layer):
        return pltpu.make_async_copy(w_refs[0].at[layer], wbuf.at[layer], w_s.at[layer, 0])

    def save(layer, which):
        pairs = [(vbuf, full_out), (zbuf, z_out), (wbuf, w_out)]
        src, dst = pairs[which]
        return pltpu.make_async_copy(src.at[layer], dst.at[layer], out_sem.at[layer, which])

    after = (lax.rem(here + 1, rows), mine)
    before = (lax.rem(here + rows - 1, rows), mine)
    down = remote(to_next, from_prev, halo_s.at[0], halo_r.at[0], after)
    up = remote(to_prev, from_next, halo_s.at[1], halo_r.at[1], before)

    def add_products(layer, low, size, base, touched):
        for q in range(4):
            a, b = q // 2, q % 2
            left = vbuf[layer, q, low : low + size, pl.ds(base, 2 * LANE)]
            for step in range(3):
                right = wbuf[layer, pl.ds(base, 2 * LANE), step * 3 * LANE : (step + 1) * 3 * LANE]
                product = jnp.dot(left, right, preferred_element_type=F32)
                for column in range(3):
                    spot = (a + step) * 4 + b + column
                    block = product[:, column * LANE : (column + 1) * LANE]
                    where = (slice(EDGE + low, EDGE + low + size), slice(spot * LANE, (spot + 1) * LANE))
                    if spot in touched:
                        yext[where] += block
                    else:
                        yext[where] = block
                        touched.add(spot)

    def fill(layer, k, chip):
        low, size = parts[k]
        side = lax.rem(layer, 2)
        rows_here = slice(low, low + size)
        lanes = pl.ds(pl.multiple_of(chip * 2 * LANE, 2 * LANE), 2 * LANE)

        def kept(which):
            return mask_of(mask_ref, which, EDGE + low, size)

        def activation(q):
            scale, offset = (
                jnp.concatenate([coef[side, chip * 2, n : n + 1], coef[side, chip * 2 + 1, n : n + 1]], axis=1)
                for n in range(2)
            )
            y = raw[side, q, rows_here, lanes].astype(F32) * scale + offset
            return y * jax.nn.sigmoid(y)

        @pl.when(layer == 0)
        def _():
            for q in range(4):
                vbuf[layer, q, rows_here, lanes] = raw[side, q, rows_here, lanes]

        @pl.when(jnp.logical_and(layer != 0, layer != POOL + 1))
        def _():
            for q in range(4):
                block = activation(q)
                if low + size > count:
                    block = jnp.where(kept(M_VALID), block, 0.0)
                vbuf[layer, q, rows_here, lanes] = block.astype(BF16)

        @pl.when(layer == POOL + 1)
        def _():
            pooled = smooth_max([activation(q) for q in range(4)])
            for q in range(4):
                vbuf[layer, q, rows_here, lanes] = jnp.where(kept(M_HIT + q), pooled, 0.0).astype(BF16)

    def at(low, size, spot):
        return yext[low : low + size, spot * LANE : (spot + 1) * LANE]

    greet([partner, across, diagonal] + row_peers(rows))
    if inside:
        own_rows = gather.rows_of(0, gather.low)
        for layer in range(layers):
            source = w_refs[layer // (layers // 2)]
            for block in range(9):
                lanes = slice(block * LANE, (block + 1) * LANE)
                wbuf[layer, own_rows, lanes] = source[layer % (layers // 2), 8 - block]
            if layer == 0:
                for piece in range(3):
                    first_gather.start(0, piece)
            elif layer <= 1:
                gather.start(layer)
    else:
        load(0).start()
    split_planes(v_ref, wide, count)
    for q in range(4):
        raw[0, q, :, own_lanes] = plane(wide, q).astype(BF16)
    to_core(0).start()
    for k in range(len(pieces)):
        to_far(0, k).start()
    yext[:EDGE, :] = jnp.zeros((EDGE, yext.shape[1]), F32)
    yext[EDGE + padded :, :] = jnp.zeros((EDGE, yext.shape[1]), F32)
    fill_masks(group_ref, here * count, count, padded, switch_ref, mask_ref)
    if inside:
        for piece in range(3):
            for step in range(1, rows // 2):
                first_gather.forward(0, step, piece)
        for piece in range(3):
            first_gather.wait(0, piece)

    def layer_step(layer):
        more = layer + 1 < layers
        def gather_at(point):
            if not inside:
                return
            for turn, actions in GATHER_PLAN[point].items():

                @pl.when(layer == turn)
                def _(actions=actions):
                    for action, which, step in actions:
                        if action == "pass":
                            gather.forward(which, step)
                        elif action == "out":
                            gather.spread(which, step).start()
                        else:
                            gather.across(which, 0).start()

        if not inside:
            load(layer).wait()

            @pl.when(more)
            def _():
                load(layer + 1).start()

        to_core(layer).wait_recv()

        @pl.when(layer > 0)
        def _():
            coef_copy(layer, 0).wait_recv()

        def take(part):
            for k, piece in enumerate(pieces):
                if piece[0] == part:
                    to_far(layer, k).wait_recv()
            pass_on(layer, part).start()

        for k in range(len(parts)):
            fill(layer, k, half)
        take(0)
        take(1)
        if inside:

            @pl.when(layer > 0)
            def _():
                gather.wait(layer)

            save(layer, 2).start()
        add_products(layer, 0, padded, own_base, set())

        @pl.when(layer > 0)
        def _():
            for k in range(1, 3):
                coef_copy(layer, k).wait_recv()

        def far_products(k):
            pass_on(layer, k).wait_recv()
            low, size = parts[k]
            fill(layer, k, 1 - half)
            add_products(layer, low, size, far_base, set(range(16)))
            if k != 1:
                return
            for lane, spot in enumerate((12, 13, 14, 15, 7, 11)):
                to_next[:, lane * LANE : (lane + 1) * LANE] = at(count, EDGE, spot).astype(BF16)
            for lane, spot in enumerate((0, 1, 2, 3, 4, 8)):
                to_prev[:, lane * LANE : (lane + 1) * LANE] = at(EDGE, EDGE, spot).astype(BF16)

            @pl.when(here + 1 < rows)
            def _():
                down.start()

            @pl.when(here > 0)
            def _():
                up.start()

        def receive_halos():
            @pl.when(here > 0)
            def _():
                down.wait_recv()
                up.wait_send()
                for lane, spot in enumerate((12, 13, 14, 15, 7, 11)):
                    received = from_prev[:, lane * LANE : (lane + 1) * LANE].astype(F32)
                    yext[:EDGE, spot * LANE : (spot + 1) * LANE] = received

            @pl.when(here + 1 < rows)
            def _():
                up.wait_recv()
                down.wait_send()
                for lane, spot in enumerate((0, 1, 2, 3, 4, 8)):
                    received = from_next[:, lane * LANE : (lane + 1) * LANE].astype(F32)
                    yext[EDGE + count : 2 * EDGE + count, spot * LANE : (spot + 1) * LANE] = received

        def over_columns(kept, first, begin, end):
            low, size = EDGE + begin, end - begin
            go_left = mask_of(mask_ref, M_LEFT, low, size)
            go_right = mask_of(mask_ref, M_RIGHT, low, size)
            kept[low : low + size, :LANE] = at(low, size, first + 1) + jnp.where(
                go_left, at(low - 1, size, first + 3), 0.0
            )
            kept[low : low + size, LANE:] = at(low, size, first + 2) + jnp.where(
                go_right, at(low + 1, size, first), 0.0
            )

        def assemble(begin, end, sums_so_far):
            low, size = EDGE + begin, end - begin
            go_left = mask_of(mask_ref, M_LEFT, low, size)
            go_right = mask_of(mask_ref, M_RIGHT, low, size)
            total, squares = sums_so_far
            for q in range(4):
                a, b = q // 2, q % 2
                lanes = slice(b * LANE, (b + 1) * LANE)
                kept, sign = (over, -1) if a == 0 else (under, 1)
                rowwise = by_width(
                    mask_ref, low, size, lambda w: kept[low + sign * w : low + sign * w + size, lanes]
                )
                z = at(low, size, (a + 1) * 4 + b + 1)
                z = z + jnp.where(mask_of(mask_ref, (M_UP, M_DOWN)[a], low, size), rowwise, 0.0)
                if b == 0:
                    z = z + jnp.where(go_left, at(low - 1, size, (a + 1) * 4 + 3), 0.0)
                else:
                    z = z + jnp.where(go_right, at(low + 1, size, (a + 1) * 4), 0.0)
                if end > count:
                    z = jnp.where(mask_of(mask_ref, M_VALID, low, size), z, 0.0)
                zbuf[layer, q, begin:end] = z
                total = total + jnp.sum(z, axis=0, keepdims=True)
                squares = squares + jnp.sum(z * z, axis=0, keepdims=True)
            return total, squares

        def prepare(k):
            _, low, size = pieces[k]
            for q in range(4):
                piece = zbuf[layer, q, low : low + size] - local
                raw[lax.rem(layer + 1, 2), q, low : low + size, own_lanes] = piece.astype(BF16)

        gather_at("products")
        take(2)
        far_products(0)
        far_products(1)
        take(3)
        far_products(2)
        far_products(3)
        take(4)
        gather_at("parts")
        near, widest = min(WIDTHS), max(WIDTHS)
        (_, top, size), (_, bottom, last_size) = pieces[:2]
        first = (top, top + size)
        last = (bottom, bottom + last_size)
        over_ready = [(n - widest, ceil_to(m - near, 8)) for n, m in (first, last)]
        under_ready = [((n + near) // 8 * 8, m + widest) for n, m in (first, last)]
        for kept, spot, ready in ((over, 12, over_ready), (under, 0, under_ready)):
            for begin, end in ready:
                over_columns(kept, spot, begin, end)
        none = (jnp.zeros((1, LANE), F32),) * 2
        inner = assemble(*last, assemble(*first, none))
        local = inner[0] / (4.0 * (size + last_size))

        @pl.when(more)
        def _():
            for k in range(2):
                prepare(k)
                to_far(layer + 1, k).start()

        gather_at("outer")
        far_products(4)
        save(layer, 0).start()
        receive_halos()
        over_rest = [(8 - EDGE, over_ready[0][0]), (over_ready[0][1], over_ready[1][0]), (over_ready[1][1], padded)]
        under_rest = [(0, under_ready[0][0]), (under_ready[0][1], under_ready[1][0]), (under_ready[1][1], padded + EDGE - 8)]
        for kept, spot, rest in ((over, 12, over_rest), (under, 0, under_rest)):
            for begin, end in rest:
                over_columns(kept, spot, begin, end)
        total, squares = assemble(last[1], padded, assemble(first[1], last[0], assemble(0, first[0], inner)))
        save(layer, 1).start()
        own = jnp.concatenate([total, squares, jnp.zeros((6, LANE), F32)], axis=0)
        channel = (sums.at[layer], sum_s.at[layer], sum_r.at[layer])
        send_sums(rows, own, *channel)

        @pl.when(more)
        def _():
            for k in range(2, len(pieces)):
                prepare(k)
                if k < 4:
                    to_far(layer + 1, k).start()
            to_core(layer + 1).start()

        for k in range(len(pieces)):
            to_far(layer, k).wait_send()
        for k in range(len(parts)):
            pass_on(layer, k).wait_send()
        to_core(layer).wait_send()

        @pl.when(layer > 0)
        def _():
            for k in range(3):
                coef_copy(layer, k).wait_send()

        gather_at("sums")
        both = add_sums(rows, *channel)
        mean = both[0:1] / pixels
        inverse = lax.rsqrt(both[1:2] / pixels - mean * mean + EPSILON)
        stat_ref[layer] = jnp.concatenate([mean, inverse, jnp.zeros((6, LANE), F32)], axis=0)
        scale = gb_ref[layer, 0:1] * inverse

        @pl.when(more)
        def _():
            offset = scale * (local - mean) + gb_ref[layer, 1:2]
            coef[lax.rem(layer + 1, 2), mine] = jnp.concatenate([scale, offset, jnp.zeros((6, LANE), F32)], axis=0)
            for k in range(3):
                coef_copy(layer + 1, k).start()
            for k in range(4, len(pieces)):
                to_far(layer + 1, k).start()

        gather_at("norm")

        @pl.when(layer + 1 == layers)
        def _():
            for q in range(4):
                y = scale * (zbuf[layer, q] - mean) + gb_ref[layer, 1:2]
                set_plane(wide, q, 0, y * jax.nn.sigmoid(y))
            next_ref[...] = wide[: 4 * count].astype(BF16)

    each(layers, layer_step)

    def drain(layer):
        if inside:

            @pl.when(layer > 0)
            def _():
                gather.drain(layer)

        for which in range(3 if inside else 2):
            save(layer, which).wait()

    each(layers, drain)
    if inside:
        for piece in range(3):
            first_gather.drain(0, piece)


def backward_kernel(inside, layers, rows, count, padded, pixels, *refs):
    refs = list(refs)
    g_ref, stat_ref, gb_ref, mask_ref, z_in, full_in, w_in = refs[:7]
    del refs[:7]
    out_ref, gbgrad_ref = refs[:2]
    wgrad_refs = refs[2 : 3 + inside]
    del refs[: 3 + inside]
    (
        grad_ref, wide, partial, zbuf, fbuf, wbuf, dk, gy, gext, above, below, patch, part, keep, core_out, core_in, x_out, x_in,
        to_next, to_prev, from_prev, from_next, sums,
        core_s, core_r, x_s, x_r, halo_s, halo_r, sum_s, sum_r, load_sem, out_sem,
    ) = refs[:33]
    mine, here = lax.axis_index("grp"), lax.axis_index("rows")
    half, core = mine // 2, lax.rem(mine, 2)
    partner, across = grp_peers()
    own_lanes, other_lanes = lanes_of(core), lanes_of(1 - core)
    own_base = pl.multiple_of(half * 2 * LANE, 2 * LANE)
    far_base = pl.multiple_of((1 - half) * 2 * LANE, 2 * LANE)
    if inside:
        first, second, third, total_ref = refs[33:37]
        shard = dk.shape[1] // rows
        scatter = Scatter(rows, shard, dk, first, second, third, total_ref, wgrad_refs, refs[37:41])

    def load(turn, which):
        src, dst = ((z_in, zbuf), (w_in, wbuf), (full_in, fbuf))[which]
        side = lax.rem(turn, 2)
        return pltpu.make_async_copy(src.at[layers - 1 - turn], dst.at[side], load_sem.at[side, which])

    def save(turn):
        slot = lax.rem(turn, 3)
        return pltpu.make_async_copy(dk.at[slot], wgrad_refs[0].at[layers - 1 - turn], out_sem.at[slot])

    for turn in range(2):
        for which in range(3):
            load(turn, which).start()
    after = (lax.rem(here + 1, rows), mine)
    before = (lax.rem(here + rows - 1, rows), mine)
    split_planes(g_ref, wide, count)
    gext[:EDGE, :] = jnp.zeros((EDGE, 4 * LANE), F32)
    gext[EDGE + padded :, :] = jnp.zeros((EDGE, 4 * LANE), F32)
    greet([partner, across] + row_peers(rows))
    load(0, 0).wait()
    partial[...] = jnp.zeros_like(partial)

    def norm_of(layer):
        return stat_ref[layer, 0:1], stat_ref[layer, 1:2], gb_ref[layer, 0:1], gb_ref[layer, 1:2]

    def shifted(turn, q):
        mean, inverse, gain, shift = norm_of(layers - 1 - turn)
        normed = (zbuf[lax.rem(turn, 2), q] - mean) * inverse
        return normed, gain * normed + shift

    def begin(turn, q, grad):
        normed, y = shifted(turn, q)
        s = jax.nn.sigmoid(y)
        grad = jnp.where(mask_of(mask_ref, M_VALID, EDGE, padded), grad * s * (1.0 + y * (1.0 - s)), 0.0)
        gy[q] = grad
        partial[0:1] += jnp.sum(grad, axis=0, keepdims=True)
        partial[1:2] += jnp.sum(grad * normed, axis=0, keepdims=True)

    def taps(q, step):
        first = (q // 2 + step) * 4 + q % 2
        return patch[:, first * LANE : (first + 3) * LANE]

    def layer_step(turn):
        layer = layers - 1 - turn
        side, slot = lax.rem(turn, 2), lax.rem(turn, 3)
        last = turn + 1 == layers
        down = remote(to_next, from_prev.at[side], halo_s.at[0], halo_r.at[side, 0], after)
        up = remote(to_prev, from_next.at[side], halo_s.at[1], halo_r.at[side, 1], before)
        mean, inverse, gain, _ = norm_of(layer)
        valid = mask_of(mask_ref, M_VALID, EDGE, padded)

        @pl.when(layer == POOL)
        def _():
            load(turn, 0).wait()
            pooled_grad = jnp.zeros((padded, LANE), F32)
            for q in range(4):
                pooled_grad = jnp.where(mask_of(mask_ref, M_HIT + q, EDGE, padded), grad_ref[q], pooled_grad)
            for q in range(4):
                _, y = shifted(turn, q)
                gy[q] = y * jax.nn.sigmoid(y)
            pooled = smooth_max([gy[q] for q in range(4)])
            partial[...] = jnp.zeros_like(partial)
            for q in range(4):
                begin(turn, q, pooled_grad * (jnp.exp(gy[q] - pooled) * 0.25))

        def spread(buf, low, planes):
            for lane, q in enumerate(planes):
                piece = slice(low, low + EDGE)
                normed = (zbuf[side, q, piece] - mean) * inverse
                buf[:, 2 * lane * LANE : (2 * lane + 1) * LANE] = gy[q, piece].astype(BF16)
                buf[:, (2 * lane + 1) * LANE : (2 * lane + 2) * LANE] = normed.astype(BF16)

        spread(to_next, count - EDGE, (2, 3, 1))
        spread(to_prev, 0, (0, 1, 2))

        @pl.when(here + 1 < rows)
        def _():
            down.start()

        @pl.when(here > 0)
        def _():
            up.start()

        own = partial[...]
        channel = (sums.at[side], sum_s.at[side], sum_r.at[side])
        send_sums(rows, own, *channel)
        both = add_sums(rows, *channel)
        gbgrad_ref[layer] = both
        if inside:

            @pl.when(turn > 0)
            def _():
                scatter.start(turn - 1, scatter.order()[2:])
                for step in scatter.order()[:2]:
                    scatter.forward(turn - 1, step)


        def conv_grad(grad, normed):
            out = inverse * gain * (grad - both[0:1] / pixels - normed * both[1:2] / pixels)
            return out.astype(BF16).astype(F32)

        for q in range(4):
            normed, _ = shifted(turn, q)
            gext[EDGE : EDGE + padded, q * LANE : (q + 1) * LANE] = jnp.where(
                valid, conv_grad(gy[q], normed), 0.0
            )

        def receive(buf, low, planes):
            for lane, q in enumerate(planes):
                grad = buf[side, :, 2 * lane * LANE : (2 * lane + 1) * LANE].astype(F32)
                normed = buf[side, :, (2 * lane + 1) * LANE : (2 * lane + 2) * LANE].astype(F32)
                gext[low : low + EDGE, q * LANE : (q + 1) * LANE] = conv_grad(grad, normed)

        @pl.when(here > 0)
        def _():
            down.wait_recv()
            up.wait_send()
            receive(from_prev, 0, (2, 3, 1))

        @pl.when(here + 1 < rows)
        def _():
            up.wait_recv()
            down.wait_send()
            receive(from_next, EDGE + count, (0, 1, 2))

        low, size = EDGE - 8, padded + 16
        for kept, which, sign, lanes in (
            (above, M_UP, -1, slice(2 * LANE, 4 * LANE)),
            (below, M_DOWN, 1, slice(0, 2 * LANE)),
        ):
            rowwise = by_width(
                mask_ref, low, size, lambda w: gext[low + sign * w : low + sign * w + size, lanes]
            )
            kept[...] = jnp.where(mask_of(mask_ref, which, low, size), rowwise, 0.0)
        go_left = mask_of(mask_ref, M_LEFT, EDGE, padded)
        go_right = mask_of(mask_ref, M_RIGHT, EDGE, padded)
        for step, (kept, top, lane) in enumerate(
            ((above, 8, 0), (gext, EDGE, 0), (gext, EDGE, 2 * LANE), (below, 8, 0))
        ):
            even, odd = slice(lane, lane + LANE), slice(lane + LANE, lane + 2 * LANE)
            blocks = [
                jnp.where(go_left, kept[top - 1 : top - 1 + padded, odd], 0.0),
                kept[top : top + padded, even],
                kept[top : top + padded, odd],
                jnp.where(go_right, kept[top + 1 : top + 1 + padded, even], 0.0),
            ]
            for column, block in enumerate(blocks):
                spot = step * 4 + column
                patch[:, spot * LANE : (spot + 1) * LANE] = block.astype(BF16)

        def kernel_grad():
            for step in range(3):
                total = None
                for q in range(4):
                    product = lax.dot_general(
                        fbuf[side, q], taps(q, step), (((0,), (0,)), ((), ())), preferred_element_type=F32
                    )
                    total = product if total is None else total + product
                dk[slot, :, step * 3 * LANE : (step + 1) * 3 * LANE] = total.astype(BF16)
            if not inside:
                save(turn).start()

        def scatter_forward(step):
            @pl.when(turn > 0)
            def _():
                scatter.forward(turn - 1, step)

        if inside:

            @pl.when(turn > 1)
            def _():
                scatter.finish(turn - 2, layer + 2)
                scatter.drain(turn - 2)

        load(turn, 1).wait()
        load(turn, 2).wait()
        if not inside:

            @pl.when(turn > 2)
            def _():
                save(turn - 3).wait()

        @pl.when(last)
        def _():
            kernel_grad()
            if inside:
                scatter.start(turn, scatter.order())

        def input_grad(q, base):
            total = None
            for step in range(3):
                right = wbuf[side, pl.ds(base, 2 * LANE), step * 3 * LANE : (step + 1) * 3 * LANE]
                product = lax.dot_general(
                    taps(q, step), right, (((1,), (1,)), ((), ())), preferred_element_type=F32
                )
                total = product if total is None else total + product
            part[...] = total

        def to_core(spot):
            which = spot if spot < 4 else pl.ds(4, 4)
            return remote(
                core_out.at[side, which], core_in.at[side, which],
                core_s.at[side, spot], core_r.at[side, spot], partner,
            )

        def to_far(q):
            return remote(x_out.at[side, q], x_in.at[side, q], x_s.at[side, q], x_r.at[side, q], across)

        def send_across(q):
            to_core(q).wait_recv()
            x_out[side, q] = (keep[q] + core_in[side, q].astype(F32)).astype(BF16)
            to_far(q).start()

        for spot in range(8):
            input_grad(spot % 4, far_base if spot < 4 else own_base)
            core_out[side, spot] = part[:, other_lanes].astype(BF16)
            keep[spot] = part[:, own_lanes]
            if spot < 4:
                to_core(spot).start()
            if 2 <= spot < 6:
                send_across(spot - 2)
            if inside and spot == 3:
                for step in scatter.order()[2:-1]:
                    scatter_forward(step)

        to_core(4).start()

        @pl.when(jnp.logical_not(last))
        def _():
            kernel_grad()
            if inside:
                scatter.start(turn, scatter.order()[:2])

        @pl.when(turn + 2 < layers)
        def _():
            for which in range(3):
                load(turn + 2, which).start()

        if inside:
            scatter_forward(0)
        if inside:

            pass

        def arrived(q):
            if q == 0:
                to_core(4).wait_recv()
            to_far(q).wait_recv()
            return keep[4 + q] + core_in[side, 4 + q].astype(F32) + x_in[side, q].astype(F32)

        begin_next = jnp.logical_and(jnp.logical_not(last), layer - 1 != POOL)

        @pl.when(begin_next)
        def _():
            load(turn + 1, 0).wait()
            partial[...] = jnp.zeros_like(partial)
            for q in range(4):
                begin(turn + 1, q, arrived(q))

        @pl.when(layer - 1 == POOL)
        def _():
            for q in range(4):
                grad_ref[q] = arrived(q)

        @pl.when(last)
        def _():
            for q in range(4):
                if inside:
                    scatter.forward(turn, scatter.order()[q])
                grad_ref[q] = arrived(q)

        for spot in range(5):
            to_core(spot).wait_send()
        for q in range(4):
            to_far(q).wait_send()

    for q in range(4):
        begin(0, q, plane(wide, q))
    each(layers, layer_step)
    for q in range(4):
        set_plane(wide, q, 0, grad_ref[q])
    out_ref[...] = wide[: 4 * count].astype(BF16)
    if inside:
        for turn in (layers - 2, layers - 1):
            scatter.finish(turn, layers - 1 - turn)
            scatter.drain(turn)
    else:
        for turn in range(layers - 3, layers):
            save(turn).wait()


VM = pl.BlockSpec(memory_space=pltpu.VMEM)
HBM = pl.BlockSpec(memory_space=pl.ANY)
LIMIT = 56 * 1024 * 1024
DMA = pltpu.SemaphoreType.DMA


def forward_block(inside, rows, count, padded, pixels, image_group, switches, features, pairs, weights):
    layers, channels, taps = pairs.shape[0], 4 * LANE, 9 * LANE
    ext = padded + 2 * EDGE
    n_parts = len(row_parts(padded, count))
    far = rows // 2
    shape = jax.ShapeDtypeStruct
    out = pl.pallas_call(
        functools.partial(forward_kernel, inside, layers, rows, count, padded, pixels),
        name="forward_block",
        out_shape=(
            shape((4 * count, LANE), BF16),
            shape((layers, 8, LANE), F32),
            shape((ext, LANE), F32),
            shape((layers, 4, padded, LANE), F32),
            shape((layers, 4, padded, channels), BF16),
            shape((layers, channels, taps) if inside else (1, 16, LANE), BF16),
        ),
        in_specs=[pl.BlockSpec(memory_space=pltpu.SMEM), VM, VM, VM] + [VM if inside else HBM] * len(weights),
        out_specs=(VM, VM, VM, HBM, HBM, HBM),
        scratch_shapes=[
            pltpu.VMEM((layers, 4, padded, channels), BF16),
            pltpu.VMEM((layers, channels, taps), BF16),
            pltpu.VMEM((layers, 4, padded, LANE), F32),
            pltpu.VMEM((2, 4, padded, channels), BF16),
            pltpu.VMEM((2, 4, 8, LANE), F32),
            pltpu.VMEM((ext, 16 * LANE), F32),
            pltpu.VMEM((ext, 2 * LANE), F32),
            pltpu.VMEM((ext, 2 * LANE), F32),
            pltpu.VMEM((4 * padded, LANE), F32),
        ]
        + [pltpu.VMEM((EDGE, 6 * LANE), BF16)] * 4
        + [pltpu.VMEM((layers, rows, 8, LANE), F32)]
        + [DMA((layers,))] * 2
        + [DMA((layers, len(far_pieces(row_parts(padded, count)))))] * 2
        + [DMA((layers, n_parts))] * 2
        + [DMA((2,))] * 2
        + [DMA((layers, rows - 1))] * 2
        + [DMA((layers, 3))] * 3
        + [DMA((layers, far - 1))] * 2
        + [DMA((layers, far))] * 2
        + [DMA((3, far - 1))] * 2
        + [DMA((3, far))] * 2,
        compiler_params=pltpu.CompilerParams(
            collective_id=0, has_side_effects=True, vmem_limit_bytes=LIMIT
        ),
    )(image_group, switches, features, pairs, *weights)
    return out[:5] + ((out[5] if inside else weights[0]),)


def backward_block(inside, rows, count, padded, pixels, grad, z, stat, pairs, masks, full, weight):
    layers, channels, taps = weight.shape
    ext = padded + 2 * EDGE
    shard = channels // rows
    far = rows // 2
    shape = jax.ShapeDtypeStruct
    scratch = [
        pltpu.VMEM((4, padded, LANE), F32),
        pltpu.VMEM((4 * padded, LANE), F32),
        pltpu.VMEM((8, LANE), F32),
        pltpu.VMEM((2, 4, padded, LANE), F32),
        pltpu.VMEM((2, 4, padded, channels), BF16),
        pltpu.VMEM((2, channels, taps), BF16),
        pltpu.VMEM((3, channels, taps), BF16),
        pltpu.VMEM((4, padded, LANE), F32),
        pltpu.VMEM((ext, 4 * LANE), F32),
        pltpu.VMEM((padded + 16, 2 * LANE), F32),
        pltpu.VMEM((padded + 16, 2 * LANE), F32),
        pltpu.VMEM((padded, 16 * LANE), BF16),
        pltpu.VMEM((padded, 2 * LANE), F32),
        pltpu.VMEM((8, padded, LANE), F32),
        pltpu.VMEM((2, 8, padded, LANE), BF16),
        pltpu.VMEM((2, 8, padded, LANE), BF16),
        pltpu.VMEM((2, 4, padded, LANE), BF16),
        pltpu.VMEM((2, 4, padded, LANE), BF16),
    ]
    scratch += [pltpu.VMEM((EDGE, 6 * LANE), BF16)] * 2 + [pltpu.VMEM((2, EDGE, 6 * LANE), BF16)] * 2
    scratch += [pltpu.VMEM((2, rows, 8, LANE), F32)]
    scratch += [DMA((2, 8))] * 2 + [DMA((2, 4))] * 2 + [DMA((2,)), DMA((2, 2))] + [DMA((2, rows - 1))] * 2
    scratch += [DMA((2, 3)), DMA((3,))]
    wgrads = [shape((layers, channels, taps), BF16)]
    if inside:
        wgrads = [shape((layers // 2, 9, shard, LANE), F32)] * 2
        scratch += [
            pltpu.VMEM((3, far, shard, taps), BF16),
            pltpu.VMEM((3, far - 1, shard, taps), BF16),
            pltpu.VMEM((3, far - 1, shard, taps), BF16),
            pltpu.VMEM((3, shard, taps), F32),
        ]
        scratch += [DMA((3, far))] * 2 + [DMA((3, far - 1))] * 2
    return pl.pallas_call(
        functools.partial(backward_kernel, inside, layers, rows, count, padded, pixels),
        name="backward_block",
        out_shape=[shape((4 * count, LANE), BF16), shape((layers, 8, LANE), F32)] + wgrads,
        in_specs=[VM] * 4 + [HBM] * 3,
        out_specs=[VM, VM] + [VM if inside else HBM] * len(wgrads),
        scratch_shapes=scratch,
        compiler_params=pltpu.CompilerParams(
            collective_id=1, has_side_effects=True, vmem_limit_bytes=LIMIT
        ),
    )(grad, stat, pairs, masks, z, full, weight)


def shards(
    features, image_group, switches, enc_weight, dec_weight,
    enc_gain, enc_bias, dec_gain, dec_bias, d_decoded,
):
    rows = lax.axis_size("rows")
    count = features.shape[0] // 4
    padded = ceil_to(count, 16)
    pixels = float(features.shape[0] * rows)
    depth, shard = enc_weight.shape[0], enc_weight.shape[2]
    inside = shard % 16 == 0 and rows == 8 and 2 * depth == 6
    sizes = (rows, count, padded, pixels)
    weights = [enc_weight, dec_weight]
    if not inside:
        both = jnp.concatenate(weights)
        flat = jnp.transpose(both[:, ::-1], (0, 2, 1, 3)).reshape(both.shape[0], shard, -1)
        weights = [lax.all_gather(flat, "rows", axis=1, tiled=True)]
    pairs = jnp.stack([jnp.concatenate([enc_gain, dec_gain]), jnp.concatenate([enc_bias, dec_bias])], axis=1)
    pairs = jnp.pad(pairs, ((0, 0), (0, 6), (0, 0)))

    hits = jnp.pad(switches, (EDGE, padded - count + EDGE), constant_values=-LANE)[:, None]
    decoded, stat, masks, z, full, weight = forward_block(
        inside, *sizes, image_group, hits, features, pairs, weights
    )
    grad, pair_grads, *wgrads = backward_block(
        inside, *sizes, d_decoded, z, stat, pairs, masks, full, weight
    )
    if not inside:
        wgrad = lax.psum_scatter(wgrads[0], "rows", scatter_dimension=1, tiled=True).astype(F32)
        wgrad = jnp.transpose(wgrad.reshape(2 * depth, shard, 9, -1)[:, :, ::-1], (0, 2, 1, 3))
        wgrads = [wgrad[:depth], wgrad[depth:]]
    return (
        decoded,
        grad,
        *wgrads,
        pair_grads[:depth, 1],
        pair_grads[:depth, 0],
        pair_grads[depth:, 1],
        pair_grads[depth:, 0],
    )


def solution(mesh):
    wide = P("rows", "grp")
    kernels = P(None, None, "rows", "grp")
    vector = P(None, "grp")
    return jax.shard_map(
        shards,
        mesh=mesh,
        in_specs=(wide, P(), P("rows"), kernels, kernels, vector, vector, vector, vector, wide),
        out_specs=(wide, wide, kernels, kernels, vector, vector, vector, vector),
        check_vma=False,
    )
```

```python
import functools

import jax
import jax.numpy as jnp
from jax import lax
from jax.experimental import pallas as pl
from jax.experimental.pallas import tpu as pltpu
from jax.sharding import PartitionSpec as P

SIZES = ((15, 20), (18, 24), (30, 40))
WIDTHS = tuple(w for _, w in SIZES)
EDGE = 48
EPSILON = 1e-05
MESH = pl.DeviceIdType.MESH
F32 = jnp.float32
BF16 = jnp.bfloat16
LANE = 128
(M_W0, M_W1, M_UP, M_DOWN, M_LEFT, M_RIGHT, M_VALID, M_HIT) = range(8)
POOL = 2


def ceil_to(value, step):
    return -(-value // step) * step


def fill_masks(group_ref, first_window, count, padded, switch_ref, mask_ref):
    shape = (padded + 2 * EDGE, 1)
    local = lax.broadcasted_iota(jnp.int32, shape, 0) - EDGE
    windows = local + first_window

    start = jnp.int32(0)
    base = height = width = jnp.zeros(shape, jnp.int32)
    for image in range(group_ref.shape[0]):
        group = group_ref[image]
        tall, wide = (
            jnp.where(group == 0, SIZES[0][k], jnp.where(group == 1, SIZES[1][k], SIZES[2][k])) for k in range(2)
        )
        end = start + tall * wide
        member = (windows >= start) & (windows < end)
        base, height, width = (
            jnp.where(member, new, old) for new, old in ((start, base), (tall, height), (wide, width))
        )
        start = end
    inside = width > 0
    position = windows - base
    row = jnp.zeros(shape, jnp.int32)
    for tall, wide in SIZES:
        quotient = jnp.floor((position.astype(F32) + 0.5) * (1.0 / wide)).astype(jnp.int32)
        row = jnp.where(width == wide, quotient, row)
    column = position - row * width
    masks = [
        width == WIDTHS[0],
        width == WIDTHS[1],
        inside & (row > 0),
        inside & (row < height - 1),
        inside & (column > 0),
        inside & (column < width - 1),
        (local >= 0) & (local < count),
    ]
    lane = lax.broadcasted_iota(jnp.int32, (shape[0], LANE), 1)
    table = (lane - M_HIT == switch_ref[...]).astype(F32)
    for k, mask in enumerate(masks):
        table = jnp.where((lane == k) & mask, 1.0, table)
    mask_ref[...] = table


def split_planes(stream_ref, wide_ref, count):
    wide_ref[: 4 * count] = stream_ref[...].astype(F32)
    wide_ref[4 * count :] = jnp.zeros((wide_ref.shape[0] - 4 * count, LANE), F32)


def plane(wide_ref, q):
    return wide_ref[pl.ds(q, wide_ref.shape[0] // 4, stride=4), :]


def set_plane(wide_ref, q, low, block):
    wide_ref[pl.ds(4 * low + q, block.shape[0], stride=4), :] = block


def mask_of(mask_ref, which, low, count):
    return mask_ref[low : low + count, which : which + 1] > 0.5


def by_width(mask_ref, low, count, shifted):
    return jnp.where(
        mask_of(mask_ref, M_W0, low, count),
        shifted(WIDTHS[0]),
        jnp.where(mask_of(mask_ref, M_W1, low, count), shifted(WIDTHS[1]), shifted(WIDTHS[2])),
    )


def smooth_max(blocks):
    total = sum(jnp.exp(block) for block in blocks)
    return jnp.log(total * 0.25)


def row_peers(rows):
    here = lax.axis_index("rows")
    there = lax.axis_index("grp")
    order = sorted(range(1, rows), key=lambda k: -min(k, rows - k))
    return [(lax.rem(here + k, rows), there) for k in order]


def grp_peers():
    here = lax.axis_index("rows")
    mine = lax.axis_index("grp")
    half, core = mine // 2, lax.rem(mine, 2)
    return (here, half * 2 + 1 - core), (here, (1 - half) * 2 + core)


def greet(peers):
    for peer in peers:
        pl.semaphore_signal(pltpu.get_barrier_semaphore(), inc=1, device_id=peer, device_id_type=MESH)


def meet(peers):
    pl.semaphore_wait(pltpu.get_barrier_semaphore(), len(peers))


def remote(src, dst, send, recv, peer):
    return pltpu.make_async_remote_copy(
        src_ref=src, dst_ref=dst, send_sem=send, recv_sem=recv, device_id=peer, device_id_type=MESH
    )


def sums_copies(rows, buf, send, recv):
    return [
        remote(buf.at[0], buf.at[k + 1], send.at[k], recv.at[k], peer) for k, peer in enumerate(row_peers(rows))
    ]


def send_sums(rows, own, buf, send, recv):
    buf[0] = own
    for copy in sums_copies(rows, buf, send, recv):
        copy.start()


def add_sums(rows, buf, send, recv):
    for copy in sums_copies(rows, buf, send, recv):
        copy.wait()
    total = buf[0]
    for k in range(1, rows):
        total = total + buf[k]
    return total


def row_parts(padded, count):
    tail = (count - EDGE) // 16 * 16
    inner, start, steps = [], EDGE, 3
    for k in range(steps):
        size = min(ceil_to(-(-(tail - start) // (steps - k)), 16), tail - start)
        inner.append((start, size))
        start += size
    return [(0, EDGE), (tail, padded - tail), inner[0], inner[2], inner[1]]


REACH = max(WIDTHS) + 1


def far_pieces(parts):
    low, size = parts[4]
    first, last = (low - REACH) // 8 * 8, ceil_to(low + size + REACH, 8)
    return [
        (2, parts[2][0], first - parts[2][0]),
        (3, last, parts[3][0] + parts[3][1] - last),
        (0, *parts[0]),
        (1, *parts[1]),
        (2, first, parts[2][0] + parts[2][1] - first),
        (3, parts[3][0], last - parts[3][0]),
        (4, low, size),
    ]


def lanes_of(block):
    return pl.ds(pl.multiple_of(block * LANE, LANE), LANE)


class Gather:
    def __init__(self, rows, shard, buf, send, recv, pass_send, pass_recv):
        self.shard, self.buf = shard, buf
        self.far = rows // 2
        here, there = lax.axis_index("rows"), lax.axis_index("grp")
        self.high, self.low = here // 2, lax.rem(here, 2)
        self.there = there
        self.send, self.recv, self.pass_send, self.pass_recv = send, recv, pass_send, pass_recv

    def rows_of(self, step, low):
        block = lax.rem(self.high + step, self.far) * 2 + low
        return pl.ds(pl.multiple_of(block * self.shard, 16), self.shard)

    def block(self, layer, step, piece):
        lanes = slice(None) if piece is None else slice(piece * 3 * LANE, (piece + 1) * 3 * LANE)
        slot = layer if piece is None else piece
        return self.buf.at[layer, self.rows_of(step, self.low), lanes], slot

    def spread(self, layer, step, piece=None):
        own, slot = self.block(layer, 0, piece)
        peer = (lax.rem(self.high + step, self.far) * 2 + self.low, self.there)
        k = step - 1
        return remote(own, own, self.send.at[slot, k], self.recv.at[slot, k], peer)

    def across(self, layer, step, piece=None):
        part, slot = self.block(layer, self.far - step, piece)
        peer = (self.high * 2 + 1 - self.low, self.there)
        return remote(part, part, self.pass_send.at[slot, step], self.pass_recv.at[slot, step], peer)

    def start(self, layer, piece=None):
        for step in range(1, self.far):
            self.spread(layer, step, piece).start()
        self.across(layer, 0, piece).start()

    def forward(self, layer, step, piece=None):
        self.spread(layer, step, piece).wait_recv()
        self.across(layer, step, piece).start()

    def wait(self, layer, piece=None):
        for step in range(self.far):
            self.across(layer, step, piece).wait_recv()

    def drain(self, layer, piece=None):
        for step in range(1, self.far):
            self.spread(layer, step, piece).wait_send()
        for step in range(self.far):
            self.across(layer, step, piece).wait_send()


class Scatter:
    def __init__(self, rows, shard, grads, first, second, third, total, outs, semaphores):
        self.shard, self.grads, self.first, self.second, self.third = shard, grads, first, second, third
        self.total, self.outs, self.far = total, outs, rows // 2
        here, self.there = lax.axis_index("rows"), lax.axis_index("grp")
        self.high, self.low = here // 2, lax.rem(here, 2)
        self.semaphores = semaphores

    def rows_of(self, step, low):
        block = lax.rem(self.high + step, self.far) * 2 + low
        return pl.ds(pl.multiple_of(block * self.shard, 16), self.shard)

    def across(self, turn, step):
        slot = lax.rem(turn, 3)
        send, recv, _, _ = self.semaphores
        peer = (self.high * 2 + 1 - self.low, self.there)
        return remote(
            self.grads.at[slot, self.rows_of(step, 1 - self.low), :], self.first.at[slot, step],
            send.at[slot, step], recv.at[slot, step], peer,
        )

    def spread(self, turn, step):
        slot = lax.rem(turn, 3)
        _, _, send, recv = self.semaphores
        peer = (lax.rem(self.high + step, self.far) * 2 + self.low, self.there)
        k = step - 1
        return remote(
            self.second.at[slot, k], self.third.at[slot, k],
            send.at[slot, k], recv.at[slot, k], peer,
        )

    def order(self):
        return list(range(1, self.far)) + [0]

    def start(self, turn, steps):
        for step in steps:
            self.across(turn, step).start()

    def forward(self, turn, step):
        slot = lax.rem(turn, 3)
        self.across(turn, step).wait_recv()
        own = self.grads[slot, self.rows_of(step, self.low), :]
        total = own.astype(F32) + self.first[slot, step].astype(F32)
        if step == 0:
            self.total[slot] = total
        else:
            self.second[slot, step - 1] = total.astype(BF16)
            self.spread(turn, step).start()

    def finish(self, turn, layer):
        slot = lax.rem(turn, 3)
        for step in range(1, self.far):
            self.spread(turn, step).wait_recv()
        total = self.total[slot]
        for step in range(1, self.far):
            total = total + self.third[slot, step - 1].astype(F32)
        depth = self.outs[0].shape[0]

        def put(out, index):
            for block in range(9):
                out[index, 8 - block] = total[:, block * LANE : (block + 1) * LANE]

        @pl.when(layer < depth)
        def _():
            put(self.outs[0], layer)

        @pl.when(layer >= depth)
        def _():
            put(self.outs[1], layer - depth)

    def drain(self, turn):
        for step in range(self.far):
            self.across(turn, step).wait_send()
        for step in range(1, self.far):
            self.spread(turn, step).wait_send()


def each(count, body):
    lax.fori_loop(0, count, lambda i, carry: (body(i), carry)[1], 0)


GATHER_PLAN = {
    "products": {0: [("pass", 1, 1)]},
    "parts": {0: [("pass", 1, 2)]},
    "outer": {},
    "sums": {0: [("pass", 1, 3)]},
    "norm": {},
}
for turn in range(4):
    GATHER_PLAN["norm"][turn] = [("out", turn + 2, 1), ("out", turn + 2, 2), ("own", turn + 2, 0)]
    GATHER_PLAN["parts"][turn + 1] = [("pass", turn + 2, 1)]
    GATHER_PLAN["outer"][turn + 1] = [("out", turn + 2, 3), ("pass", turn + 2, 2)]
    GATHER_PLAN["sums"][turn + 1] = [("pass", turn + 2, 3)]


def forward_kernel(
    inside, layers, rows, count, padded, pixels, group_ref, switch_ref, v_ref, gb_ref, *refs
):
    w_refs, refs = refs[: 1 + inside], refs[1 + inside :]
    (
        next_ref, stat_ref, mask_ref, z_out, full_out, w_out,
        vbuf, wbuf, zbuf, raw, coef, yext, over, under, wide, to_next, to_prev, from_prev, from_next, sums,
        core_s, core_r, x_s, x_r, fwd_s, fwd_r, halo_s, halo_r, sum_s, sum_r, out_sem,
        coef_s, coef_r, w_s, w_r, wp_s, wp_r, first_s, first_r, first_ps, first_pr,
    ) = refs
    mine, here = lax.axis_index("grp"), lax.axis_index("rows")
    half = mine // 2
    partner, across = grp_peers()
    diagonal = (here, across[1] + partner[1] - mine)
    parts = row_parts(padded, count)
    pieces = far_pieces(parts)
    own_lanes, far_lanes = lanes_of(mine), lanes_of(across[1])
    own_base = pl.multiple_of(half * 2 * LANE, 2 * LANE)
    far_base = pl.multiple_of((1 - half) * 2 * LANE, 2 * LANE)
    shard = wbuf.shape[1] // rows
    gather = Gather(rows, shard, wbuf, w_s, w_r, wp_s, wp_r)
    first_gather = Gather(rows, shard, wbuf, first_s, first_r, first_ps, first_pr)

    def slab(layer, k, lanes):
        low, size = parts[k]
        return raw.at[lax.rem(layer, 2), :, pl.ds(low, size), lanes]

    def to_core(layer):
        whole = raw.at[lax.rem(layer, 2), :, :, own_lanes]
        return remote(whole, whole, core_s.at[layer], core_r.at[layer], partner)

    def to_far(layer, k):
        _, low, size = pieces[k]
        piece = raw.at[lax.rem(layer, 2), :, pl.ds(low, size), own_lanes]
        return remote(piece, piece, x_s.at[layer, k], x_r.at[layer, k], across)

    def pass_on(layer, k):
        piece = slab(layer, k, far_lanes)
        return remote(piece, piece, fwd_s.at[layer, k], fwd_r.at[layer, k], partner)

    def coef_copy(layer, k):
        own = coef.at[lax.rem(layer, 2), mine]
        return remote(own, own, coef_s.at[layer, k], coef_r.at[layer, k], (partner, across, diagonal)[k])

    def load(layer):
        return pltpu.make_async_copy(w_refs[0].at[layer], wbuf.at[layer], w_s.at[layer, 0])

    def save(layer, which):
        pairs = [(vbuf, full_out), (zbuf, z_out), (wbuf, w_out)]
        src, dst = pairs[which]
        return pltpu.make_async_copy(src.at[layer], dst.at[layer], out_sem.at[layer, which])

    after = (lax.rem(here + 1, rows), mine)
    before = (lax.rem(here + rows - 1, rows), mine)
    down = remote(to_next, from_prev, halo_s.at[0], halo_r.at[0], after)
    up = remote(to_prev, from_next, halo_s.at[1], halo_r.at[1], before)

    def add_products(layer, low, size, base, touched):
        for q in range(4):
            a, b = q // 2, q % 2
            left = vbuf[layer, q, low : low + size, pl.ds(base, 2 * LANE)]
            for step in range(3):
                right = wbuf[layer, pl.ds(base, 2 * LANE), step * 3 * LANE : (step + 1) * 3 * LANE]
                product = jnp.dot(left, right, preferred_element_type=F32)
                for column in range(3):
                    spot = (a + step) * 4 + b + column
                    block = product[:, column * LANE : (column + 1) * LANE]
                    where = (slice(EDGE + low, EDGE + low + size), slice(spot * LANE, (spot + 1) * LANE))
                    if spot in touched:
                        yext[where] += block
                    else:
                        yext[where] = block
                        touched.add(spot)

    def fill(layer, k, chip):
        low, size = parts[k]
        side = lax.rem(layer, 2)
        rows_here = slice(low, low + size)
        lanes = pl.ds(pl.multiple_of(chip * 2 * LANE, 2 * LANE), 2 * LANE)

        def kept(which):
            return mask_of(mask_ref, which, EDGE + low, size)

        def activation(q):
            scale, offset = (
                jnp.concatenate([coef[side, chip * 2, n : n + 1], coef[side, chip * 2 + 1, n : n + 1]], axis=1)
                for n in range(2)
            )
            y = raw[side, q, rows_here, lanes].astype(F32) * scale + offset
            return y * jax.nn.sigmoid(y)

        @pl.when(layer == 0)
        def _():
            for q in range(4):
                vbuf[layer, q, rows_here, lanes] = raw[side, q, rows_here, lanes]

        @pl.when(jnp.logical_and(layer != 0, layer != POOL + 1))
        def _():
            for q in range(4):
                block = activation(q)
                if low + size > count:
                    block = jnp.where(kept(M_VALID), block, 0.0)
                vbuf[layer, q, rows_here, lanes] = block.astype(BF16)

        @pl.when(layer == POOL + 1)
        def _():
            pooled = smooth_max([activation(q) for q in range(4)])
            for q in range(4):
                vbuf[layer, q, rows_here, lanes] = jnp.where(kept(M_HIT + q), pooled, 0.0).astype(BF16)

    def at(low, size, spot):
        return yext[low : low + size, spot * LANE : (spot + 1) * LANE]

    everyone = [partner, across, diagonal] + row_peers(rows)
    greet(everyone)
    split_planes(v_ref, wide, count)
    for q in range(4):
        raw[0, q, :, own_lanes] = plane(wide, q).astype(BF16)
    meet(everyone)
    if inside:
        own_rows = gather.rows_of(0, gather.low)
        for layer in range(layers):
            source = w_refs[layer // (layers // 2)]
            for block in range(9):
                lanes = slice(block * LANE, (block + 1) * LANE)
                wbuf[layer, own_rows, lanes] = source[layer % (layers // 2), 8 - block]
            if layer == 0:
                for piece in range(3):
                    first_gather.start(0, piece)
            elif layer <= 1:
                gather.start(layer)
    else:
        load(0).start()
    to_core(0).start()
    for k in range(len(pieces)):
        to_far(0, k).start()
    yext[:EDGE, :] = jnp.zeros((EDGE, yext.shape[1]), F32)
    yext[EDGE + padded :, :] = jnp.zeros((EDGE, yext.shape[1]), F32)
    fill_masks(group_ref, here * count, count, padded, switch_ref, mask_ref)
    if inside:
        for piece in range(3):
            for step in range(1, rows // 2):
                first_gather.forward(0, step, piece)
        for piece in range(3):
            first_gather.wait(0, piece)

    def layer_step(layer):
        more = layer + 1 < layers
        def gather_at(point):
            if not inside:
                return
            for turn, actions in GATHER_PLAN[point].items():

                @pl.when(layer == turn)
                def _(actions=actions):
                    for action, which, step in actions:
                        if action == "pass":
                            gather.forward(which, step)
                        elif action == "out":
                            gather.spread(which, step).start()
                        else:
                            gather.across(which, 0).start()

        if not inside:
            load(layer).wait()

            @pl.when(more)
            def _():
                load(layer + 1).start()

        to_core(layer).wait_recv()

        @pl.when(layer > 0)
        def _():
            coef_copy(layer, 0).wait_recv()

        def take(part):
            for k, piece in enumerate(pieces):
                if piece[0] == part:
                    to_far(layer, k).wait_recv()
            pass_on(layer, part).start()

        for k in range(len(parts)):
            fill(layer, k, half)
        take(0)
        take(1)
        if inside:

            @pl.when(layer > 0)
            def _():
                gather.wait(layer)

            save(layer, 2).start()
        add_products(layer, 0, padded, own_base, set())

        @pl.when(layer > 0)
        def _():
            for k in range(1, 3):
                coef_copy(layer, k).wait_recv()

        def far_products(k):
            pass_on(layer, k).wait_recv()
            low, size = parts[k]
            fill(layer, k, 1 - half)
            add_products(layer, low, size, far_base, set(range(16)))
            if k != 1:
                return
            for lane, spot in enumerate((12, 13, 14, 15, 7, 11)):
                to_next[:, lane * LANE : (lane + 1) * LANE] = at(count, EDGE, spot).astype(BF16)
            for lane, spot in enumerate((0, 1, 2, 3, 4, 8)):
                to_prev[:, lane * LANE : (lane + 1) * LANE] = at(EDGE, EDGE, spot).astype(BF16)

            @pl.when(here + 1 < rows)
            def _():
                down.start()

            @pl.when(here > 0)
            def _():
                up.start()

        def receive_halos():
            @pl.when(here > 0)
            def _():
                down.wait_recv()
                up.wait_send()
                for lane, spot in enumerate((12, 13, 14, 15, 7, 11)):
                    received = from_prev[:, lane * LANE : (lane + 1) * LANE].astype(F32)
                    yext[:EDGE, spot * LANE : (spot + 1) * LANE] = received

            @pl.when(here + 1 < rows)
            def _():
                up.wait_recv()
                down.wait_send()
                for lane, spot in enumerate((0, 1, 2, 3, 4, 8)):
                    received = from_next[:, lane * LANE : (lane + 1) * LANE].astype(F32)
                    yext[EDGE + count : 2 * EDGE + count, spot * LANE : (spot + 1) * LANE] = received

        def over_columns(kept, first, begin, end):
            low, size = EDGE + begin, end - begin
            go_left = mask_of(mask_ref, M_LEFT, low, size)
            go_right = mask_of(mask_ref, M_RIGHT, low, size)
            kept[low : low + size, :LANE] = at(low, size, first + 1) + jnp.where(
                go_left, at(low - 1, size, first + 3), 0.0
            )
            kept[low : low + size, LANE:] = at(low, size, first + 2) + jnp.where(
                go_right, at(low + 1, size, first), 0.0
            )

        def assemble(begin, end, sums_so_far):
            low, size = EDGE + begin, end - begin
            go_left = mask_of(mask_ref, M_LEFT, low, size)
            go_right = mask_of(mask_ref, M_RIGHT, low, size)
            total, squares = sums_so_far
            for q in range(4):
                a, b = q // 2, q % 2
                lanes = slice(b * LANE, (b + 1) * LANE)
                kept, sign = (over, -1) if a == 0 else (under, 1)
                rowwise = by_width(
                    mask_ref, low, size, lambda w: kept[low + sign * w : low + sign * w + size, lanes]
                )
                z = at(low, size, (a + 1) * 4 + b + 1)
                z = z + jnp.where(mask_of(mask_ref, (M_UP, M_DOWN)[a], low, size), rowwise, 0.0)
                if b == 0:
                    z = z + jnp.where(go_left, at(low - 1, size, (a + 1) * 4 + 3), 0.0)
                else:
                    z = z + jnp.where(go_right, at(low + 1, size, (a + 1) * 4), 0.0)
                if end > count:
                    z = jnp.where(mask_of(mask_ref, M_VALID, low, size), z, 0.0)
                zbuf[layer, q, begin:end] = z
                total = total + jnp.sum(z, axis=0, keepdims=True)
                squares = squares + jnp.sum(z * z, axis=0, keepdims=True)
            return total, squares

        def prepare(k):
            _, low, size = pieces[k]
            for q in range(4):
                piece = zbuf[layer, q, low : low + size] - local
                raw[lax.rem(layer + 1, 2), q, low : low + size, own_lanes] = piece.astype(BF16)

        gather_at("products")
        take(2)
        far_products(0)
        far_products(1)
        take(3)
        far_products(2)
        far_products(3)
        take(4)
        gather_at("parts")
        near, widest = min(WIDTHS), max(WIDTHS)
        (_, top, size), (_, bottom, last_size) = pieces[:2]
        first = (top, top + size)
        last = (bottom, bottom + last_size)
        over_ready = [(n - widest, ceil_to(m - near, 8)) for n, m in (first, last)]
        under_ready = [((n + near) // 8 * 8, m + widest) for n, m in (first, last)]
        for kept, spot, ready in ((over, 12, over_ready), (under, 0, under_ready)):
            for begin, end in ready:
                over_columns(kept, spot, begin, end)
        none = (jnp.zeros((1, LANE), F32),) * 2
        inner = assemble(*last, assemble(*first, none))
        local = inner[0] / (4.0 * (size + last_size))

        @pl.when(more)
        def _():
            for k in range(2):
                prepare(k)
                to_far(layer + 1, k).start()

        gather_at("outer")
        far_products(4)
        save(layer, 0).start()
        receive_halos()
        over_rest = [(8 - EDGE, over_ready[0][0]), (over_ready[0][1], over_ready[1][0]), (over_ready[1][1], padded)]
        under_rest = [(0, under_ready[0][0]), (under_ready[0][1], under_ready[1][0]), (under_ready[1][1], padded + EDGE - 8)]
        for kept, spot, rest in ((over, 12, over_rest), (under, 0, under_rest)):
            for begin, end in rest:
                over_columns(kept, spot, begin, end)
        total, squares = assemble(last[1], padded, assemble(first[1], last[0], assemble(0, first[0], inner)))
        save(layer, 1).start()
        own = jnp.concatenate([total, squares, jnp.zeros((6, LANE), F32)], axis=0)
        channel = (sums.at[layer], sum_s.at[layer], sum_r.at[layer])
        send_sums(rows, own, *channel)

        @pl.when(more)
        def _():
            for k in range(2, len(pieces)):
                prepare(k)
                if k < 4:
                    to_far(layer + 1, k).start()
            to_core(layer + 1).start()

        for k in range(len(pieces)):
            to_far(layer, k).wait_send()
        for k in range(len(parts)):
            pass_on(layer, k).wait_send()
        to_core(layer).wait_send()

        @pl.when(layer > 0)
        def _():
            for k in range(3):
                coef_copy(layer, k).wait_send()

        gather_at("sums")
        both = add_sums(rows, *channel)
        mean = both[0:1] / pixels
        inverse = lax.rsqrt(both[1:2] / pixels - mean * mean + EPSILON)
        stat_ref[layer] = jnp.concatenate([mean, inverse, jnp.zeros((6, LANE), F32)], axis=0)
        scale = gb_ref[layer, 0:1] * inverse

        @pl.when(more)
        def _():
            offset = scale * (local - mean) + gb_ref[layer, 1:2]
            coef[lax.rem(layer + 1, 2), mine] = jnp.concatenate([scale, offset, jnp.zeros((6, LANE), F32)], axis=0)
            for k in range(3):
                coef_copy(layer + 1, k).start()
            for k in range(4, len(pieces)):
                to_far(layer + 1, k).start()

        gather_at("norm")

        @pl.when(layer + 1 == layers)
        def _():
            for q in range(4):
                y = scale * (zbuf[layer, q] - mean) + gb_ref[layer, 1:2]
                set_plane(wide, q, 0, y * jax.nn.sigmoid(y))
            next_ref[...] = wide[: 4 * count].astype(BF16)

    each(layers, layer_step)

    def drain(layer):
        if inside:

            @pl.when(layer > 0)
            def _():
                gather.drain(layer)

        for which in range(3 if inside else 2):
            save(layer, which).wait()

    each(layers, drain)
    if inside:
        for piece in range(3):
            first_gather.drain(0, piece)


def backward_kernel(inside, layers, rows, count, padded, pixels, *refs):
    refs = list(refs)
    g_ref, stat_ref, gb_ref, mask_ref, z_in, full_in, w_in = refs[:7]
    del refs[:7]
    out_ref, gbgrad_ref = refs[:2]
    wgrad_refs = refs[2 : 3 + inside]
    del refs[: 3 + inside]
    (
        grad_ref, wide, partial, zbuf, fbuf, wbuf, dk, gy, gext, above, below, patch, part, keep, core_out, core_in, x_out, x_in,
        to_next, to_prev, from_prev, from_next, sums,
        core_s, core_r, x_s, x_r, halo_s, halo_r, sum_s, sum_r, load_sem, out_sem,
    ) = refs[:33]
    mine, here = lax.axis_index("grp"), lax.axis_index("rows")
    half, core = mine // 2, lax.rem(mine, 2)
    partner, across = grp_peers()
    own_lanes, other_lanes = lanes_of(core), lanes_of(1 - core)
    own_base = pl.multiple_of(half * 2 * LANE, 2 * LANE)
    far_base = pl.multiple_of((1 - half) * 2 * LANE, 2 * LANE)
    if inside:
        first, second, third, total_ref = refs[33:37]
        shard = dk.shape[1] // rows
        scatter = Scatter(rows, shard, dk, first, second, third, total_ref, wgrad_refs, refs[37:41])

    def load(turn, which):
        src, dst = ((z_in, zbuf), (w_in, wbuf), (full_in, fbuf))[which]
        side = lax.rem(turn, 2)
        return pltpu.make_async_copy(src.at[layers - 1 - turn], dst.at[side], load_sem.at[side, which])

    def save(turn):
        slot = lax.rem(turn, 3)
        return pltpu.make_async_copy(dk.at[slot], wgrad_refs[0].at[layers - 1 - turn], out_sem.at[slot])

    everyone = [partner, across] + row_peers(rows)
    greet(everyone)
    for turn in range(2):
        for which in range(3):
            load(turn, which).start()
    after = (lax.rem(here + 1, rows), mine)
    before = (lax.rem(here + rows - 1, rows), mine)
    split_planes(g_ref, wide, count)
    gext[:EDGE, :] = jnp.zeros((EDGE, 4 * LANE), F32)
    gext[EDGE + padded :, :] = jnp.zeros((EDGE, 4 * LANE), F32)
    load(0, 0).wait()
    partial[...] = jnp.zeros_like(partial)

    def norm_of(layer):
        return stat_ref[layer, 0:1], stat_ref[layer, 1:2], gb_ref[layer, 0:1], gb_ref[layer, 1:2]

    def shifted(turn, q):
        mean, inverse, gain, shift = norm_of(layers - 1 - turn)
        normed = (zbuf[lax.rem(turn, 2), q] - mean) * inverse
        return normed, gain * normed + shift

    def begin(turn, q, grad):
        normed, y = shifted(turn, q)
        s = jax.nn.sigmoid(y)
        grad = jnp.where(mask_of(mask_ref, M_VALID, EDGE, padded), grad * s * (1.0 + y * (1.0 - s)), 0.0)
        gy[q] = grad
        partial[0:1] += jnp.sum(grad, axis=0, keepdims=True)
        partial[1:2] += jnp.sum(grad * normed, axis=0, keepdims=True)

    def taps(q, step):
        first = (q // 2 + step) * 4 + q % 2
        return patch[:, first * LANE : (first + 3) * LANE]

    def layer_step(turn):
        layer = layers - 1 - turn
        side, slot = lax.rem(turn, 2), lax.rem(turn, 3)
        last = turn + 1 == layers
        down = remote(to_next, from_prev.at[side], halo_s.at[0], halo_r.at[side, 0], after)
        up = remote(to_prev, from_next.at[side], halo_s.at[1], halo_r.at[side, 1], before)
        mean, inverse, gain, _ = norm_of(layer)
        valid = mask_of(mask_ref, M_VALID, EDGE, padded)

        @pl.when(layer == POOL)
        def _():
            load(turn, 0).wait()
            pooled_grad = jnp.zeros((padded, LANE), F32)
            for q in range(4):
                pooled_grad = jnp.where(mask_of(mask_ref, M_HIT + q, EDGE, padded), grad_ref[q], pooled_grad)
            for q in range(4):
                _, y = shifted(turn, q)
                gy[q] = y * jax.nn.sigmoid(y)
            pooled = smooth_max([gy[q] for q in range(4)])
            partial[...] = jnp.zeros_like(partial)
            for q in range(4):
                begin(turn, q, pooled_grad * (jnp.exp(gy[q] - pooled) * 0.25))

        def spread(buf, low, planes):
            for lane, q in enumerate(planes):
                piece = slice(low, low + EDGE)
                normed = (zbuf[side, q, piece] - mean) * inverse
                buf[:, 2 * lane * LANE : (2 * lane + 1) * LANE] = gy[q, piece].astype(BF16)
                buf[:, (2 * lane + 1) * LANE : (2 * lane + 2) * LANE] = normed.astype(BF16)

        spread(to_next, count - EDGE, (2, 3, 1))
        spread(to_prev, 0, (0, 1, 2))

        @pl.when(here + 1 < rows)
        def _():
            down.start()

        @pl.when(here > 0)
        def _():
            up.start()

        own = partial[...]
        channel = (sums.at[side], sum_s.at[side], sum_r.at[side])
        send_sums(rows, own, *channel)
        both = add_sums(rows, *channel)
        gbgrad_ref[layer] = both
        if inside:

            @pl.when(turn > 0)
            def _():
                scatter.start(turn - 1, scatter.order()[2:])
                for step in scatter.order()[:2]:
                    scatter.forward(turn - 1, step)


        def conv_grad(grad, normed):
            out = inverse * gain * (grad - both[0:1] / pixels - normed * both[1:2] / pixels)
            return out.astype(BF16).astype(F32)

        for q in range(4):
            normed, _ = shifted(turn, q)
            gext[EDGE : EDGE + padded, q * LANE : (q + 1) * LANE] = jnp.where(
                valid, conv_grad(gy[q], normed), 0.0
            )

        def receive(buf, low, planes):
            for lane, q in enumerate(planes):
                grad = buf[side, :, 2 * lane * LANE : (2 * lane + 1) * LANE].astype(F32)
                normed = buf[side, :, (2 * lane + 1) * LANE : (2 * lane + 2) * LANE].astype(F32)
                gext[low : low + EDGE, q * LANE : (q + 1) * LANE] = conv_grad(grad, normed)

        @pl.when(here > 0)
        def _():
            down.wait_recv()
            up.wait_send()
            receive(from_prev, 0, (2, 3, 1))

        @pl.when(here + 1 < rows)
        def _():
            up.wait_recv()
            down.wait_send()
            receive(from_next, EDGE + count, (0, 1, 2))

        low, size = EDGE - 8, padded + 16
        for kept, which, sign, lanes in (
            (above, M_UP, -1, slice(2 * LANE, 4 * LANE)),
            (below, M_DOWN, 1, slice(0, 2 * LANE)),
        ):
            rowwise = by_width(
                mask_ref, low, size, lambda w: gext[low + sign * w : low + sign * w + size, lanes]
            )
            kept[...] = jnp.where(mask_of(mask_ref, which, low, size), rowwise, 0.0)
        go_left = mask_of(mask_ref, M_LEFT, EDGE, padded)
        go_right = mask_of(mask_ref, M_RIGHT, EDGE, padded)
        for step, (kept, top, lane) in enumerate(
            ((above, 8, 0), (gext, EDGE, 0), (gext, EDGE, 2 * LANE), (below, 8, 0))
        ):
            even, odd = slice(lane, lane + LANE), slice(lane + LANE, lane + 2 * LANE)
            blocks = [
                jnp.where(go_left, kept[top - 1 : top - 1 + padded, odd], 0.0),
                kept[top : top + padded, even],
                kept[top : top + padded, odd],
                jnp.where(go_right, kept[top + 1 : top + 1 + padded, even], 0.0),
            ]
            for column, block in enumerate(blocks):
                spot = step * 4 + column
                patch[:, spot * LANE : (spot + 1) * LANE] = block.astype(BF16)

        def kernel_grad():
            for step in range(3):
                total = None
                for q in range(4):
                    product = lax.dot_general(
                        fbuf[side, q], taps(q, step), (((0,), (0,)), ((), ())), preferred_element_type=F32
                    )
                    total = product if total is None else total + product
                dk[slot, :, step * 3 * LANE : (step + 1) * 3 * LANE] = total.astype(BF16)
            if not inside:
                save(turn).start()

        def scatter_forward(step):
            @pl.when(turn > 0)
            def _():
                scatter.forward(turn - 1, step)

        if inside:

            @pl.when(turn > 1)
            def _():
                scatter.finish(turn - 2, layer + 2)
                scatter.drain(turn - 2)

        load(turn, 1).wait()
        load(turn, 2).wait()
        if not inside:

            @pl.when(turn > 2)
            def _():
                save(turn - 3).wait()

        @pl.when(last)
        def _():
            kernel_grad()
            if inside:
                scatter.start(turn, scatter.order())

        def input_grad(q, base):
            total = None
            for step in range(3):
                right = wbuf[side, pl.ds(base, 2 * LANE), step * 3 * LANE : (step + 1) * 3 * LANE]
                product = lax.dot_general(
                    taps(q, step), right, (((1,), (1,)), ((), ())), preferred_element_type=F32
                )
                total = product if total is None else total + product
            part[...] = total

        def to_core(spot):
            which = spot if spot < 4 else pl.ds(4, 4)
            return remote(
                core_out.at[side, which], core_in.at[side, which],
                core_s.at[side, spot], core_r.at[side, spot], partner,
            )

        def to_far(q):
            return remote(x_out.at[side, q], x_in.at[side, q], x_s.at[side, q], x_r.at[side, q], across)

        def send_across(q):
            to_core(q).wait_recv()
            x_out[side, q] = (keep[q] + core_in[side, q].astype(F32)).astype(BF16)
            to_far(q).start()

        for spot in range(8):
            input_grad(spot % 4, far_base if spot < 4 else own_base)
            core_out[side, spot] = part[:, other_lanes].astype(BF16)
            keep[spot] = part[:, own_lanes]
            if spot < 4:
                to_core(spot).start()
            if 2 <= spot < 6:
                send_across(spot - 2)
            if inside and spot == 3:
                for step in scatter.order()[2:-1]:
                    scatter_forward(step)

        to_core(4).start()

        @pl.when(jnp.logical_not(last))
        def _():
            kernel_grad()
            if inside:
                scatter.start(turn, scatter.order()[:2])

        @pl.when(turn + 2 < layers)
        def _():
            for which in range(3):
                load(turn + 2, which).start()

        if inside:
            scatter_forward(0)
        if inside:

            pass

        def arrived(q):
            if q == 0:
                to_core(4).wait_recv()
            to_far(q).wait_recv()
            return keep[4 + q] + core_in[side, 4 + q].astype(F32) + x_in[side, q].astype(F32)

        begin_next = jnp.logical_and(jnp.logical_not(last), layer - 1 != POOL)

        @pl.when(begin_next)
        def _():
            load(turn + 1, 0).wait()
            partial[...] = jnp.zeros_like(partial)
            for q in range(4):
                begin(turn + 1, q, arrived(q))

        @pl.when(layer - 1 == POOL)
        def _():
            for q in range(4):
                grad_ref[q] = arrived(q)

        @pl.when(last)
        def _():
            for q in range(4):
                if inside:
                    scatter.forward(turn, scatter.order()[q])
                grad_ref[q] = arrived(q)

        for spot in range(5):
            to_core(spot).wait_send()
        for q in range(4):
            to_far(q).wait_send()

    for q in range(4):
        begin(0, q, plane(wide, q))
    meet(everyone)
    each(layers, layer_step)
    for q in range(4):
        set_plane(wide, q, 0, grad_ref[q])
    out_ref[...] = wide[: 4 * count].astype(BF16)
    if inside:
        for turn in (layers - 2, layers - 1):
            scatter.finish(turn, layers - 1 - turn)
            scatter.drain(turn)
    else:
        for turn in range(layers - 3, layers):
            save(turn).wait()


VM = pl.BlockSpec(memory_space=pltpu.VMEM)
HBM = pl.BlockSpec(memory_space=pl.ANY)
LIMIT = 56 * 1024 * 1024
DMA = pltpu.SemaphoreType.DMA


def forward_block(inside, rows, count, padded, pixels, image_group, switches, features, pairs, weights):
    layers, channels, taps = pairs.shape[0], 4 * LANE, 9 * LANE
    ext = padded + 2 * EDGE
    n_parts = len(row_parts(padded, count))
    far = rows // 2
    shape = jax.ShapeDtypeStruct
    out = pl.pallas_call(
        functools.partial(forward_kernel, inside, layers, rows, count, padded, pixels),
        name="forward_block",
        out_shape=(
            shape((4 * count, LANE), BF16),
            shape((layers, 8, LANE), F32),
            shape((ext, LANE), F32),
            shape((layers, 4, padded, LANE), F32),
            shape((layers, 4, padded, channels), BF16),
            shape((layers, channels, taps) if inside else (1, 16, LANE), BF16),
        ),
        in_specs=[pl.BlockSpec(memory_space=pltpu.SMEM), VM, VM, VM] + [VM if inside else HBM] * len(weights),
        out_specs=(VM, VM, VM, HBM, HBM, HBM),
        scratch_shapes=[
            pltpu.VMEM((layers, 4, padded, channels), BF16),
            pltpu.VMEM((layers, channels, taps), BF16),
            pltpu.VMEM((layers, 4, padded, LANE), F32),
            pltpu.VMEM((2, 4, padded, channels), BF16),
            pltpu.VMEM((2, 4, 8, LANE), F32),
            pltpu.VMEM((ext, 16 * LANE), F32),
            pltpu.VMEM((ext, 2 * LANE), F32),
            pltpu.VMEM((ext, 2 * LANE), F32),
            pltpu.VMEM((4 * padded, LANE), F32),
        ]
        + [pltpu.VMEM((EDGE, 6 * LANE), BF16)] * 4
        + [pltpu.VMEM((layers, rows, 8, LANE), F32)]
        + [DMA((layers,))] * 2
        + [DMA((layers, len(far_pieces(row_parts(padded, count)))))] * 2
        + [DMA((layers, n_parts))] * 2
        + [DMA((2,))] * 2
        + [DMA((layers, rows - 1))] * 2
        + [DMA((layers, 3))] * 3
        + [DMA((layers, far - 1))] * 2
        + [DMA((layers, far))] * 2
        + [DMA((3, far - 1))] * 2
        + [DMA((3, far))] * 2,
        compiler_params=pltpu.CompilerParams(
            collective_id=0, has_side_effects=True, vmem_limit_bytes=LIMIT
        ),
    )(image_group, switches, features, pairs, *weights)
    return out[:5] + ((out[5] if inside else weights[0]),)


def backward_block(inside, rows, count, padded, pixels, grad, z, stat, pairs, masks, full, weight):
    layers, channels, taps = weight.shape
    ext = padded + 2 * EDGE
    shard = channels // rows
    far = rows // 2
    shape = jax.ShapeDtypeStruct
    scratch = [
        pltpu.VMEM((4, padded, LANE), F32),
        pltpu.VMEM((4 * padded, LANE), F32),
        pltpu.VMEM((8, LANE), F32),
        pltpu.VMEM((2, 4, padded, LANE), F32),
        pltpu.VMEM((2, 4, padded, channels), BF16),
        pltpu.VMEM((2, channels, taps), BF16),
        pltpu.VMEM((3, channels, taps), BF16),
        pltpu.VMEM((4, padded, LANE), F32),
        pltpu.VMEM((ext, 4 * LANE), F32),
        pltpu.VMEM((padded + 16, 2 * LANE), F32),
        pltpu.VMEM((padded + 16, 2 * LANE), F32),
        pltpu.VMEM((padded, 16 * LANE), BF16),
        pltpu.VMEM((padded, 2 * LANE), F32),
        pltpu.VMEM((8, padded, LANE), F32),
        pltpu.VMEM((2, 8, padded, LANE), BF16),
        pltpu.VMEM((2, 8, padded, LANE), BF16),
        pltpu.VMEM((2, 4, padded, LANE), BF16),
        pltpu.VMEM((2, 4, padded, LANE), BF16),
    ]
    scratch += [pltpu.VMEM((EDGE, 6 * LANE), BF16)] * 2 + [pltpu.VMEM((2, EDGE, 6 * LANE), BF16)] * 2
    scratch += [pltpu.VMEM((2, rows, 8, LANE), F32)]
    scratch += [DMA((2, 8))] * 2 + [DMA((2, 4))] * 2 + [DMA((2,)), DMA((2, 2))] + [DMA((2, rows - 1))] * 2
    scratch += [DMA((2, 3)), DMA((3,))]
    wgrads = [shape((layers, channels, taps), BF16)]
    if inside:
        wgrads = [shape((layers // 2, 9, shard, LANE), F32)] * 2
        scratch += [
            pltpu.VMEM((3, far, shard, taps), BF16),
            pltpu.VMEM((3, far - 1, shard, taps), BF16),
            pltpu.VMEM((3, far - 1, shard, taps), BF16),
            pltpu.VMEM((3, shard, taps), F32),
        ]
        scratch += [DMA((3, far))] * 2 + [DMA((3, far - 1))] * 2
    return pl.pallas_call(
        functools.partial(backward_kernel, inside, layers, rows, count, padded, pixels),
        name="backward_block",
        out_shape=[shape((4 * count, LANE), BF16), shape((layers, 8, LANE), F32)] + wgrads,
        in_specs=[VM] * 4 + [HBM] * 3,
        out_specs=[VM, VM] + [VM if inside else HBM] * len(wgrads),
        scratch_shapes=scratch,
        compiler_params=pltpu.CompilerParams(
            collective_id=1, has_side_effects=True, vmem_limit_bytes=LIMIT
        ),
    )(grad, stat, pairs, masks, z, full, weight)


def shards(
    features, image_group, switches, enc_weight, dec_weight,
    enc_gain, enc_bias, dec_gain, dec_bias, d_decoded,
):
    rows = lax.axis_size("rows")
    count = features.shape[0] // 4
    padded = ceil_to(count, 16)
    pixels = float(features.shape[0] * rows)
    depth, shard = enc_weight.shape[0], enc_weight.shape[2]
    inside = shard % 16 == 0 and rows == 8 and 2 * depth == 6
    sizes = (rows, count, padded, pixels)
    weights = [enc_weight, dec_weight]
    if not inside:
        both = jnp.concatenate(weights)
        flat = jnp.transpose(both[:, ::-1], (0, 2, 1, 3)).reshape(both.shape[0], shard, -1)
        weights = [lax.all_gather(flat, "rows", axis=1, tiled=True)]
    pairs = jnp.stack([jnp.concatenate([enc_gain, dec_gain]), jnp.concatenate([enc_bias, dec_bias])], axis=1)
    pairs = jnp.pad(pairs, ((0, 0), (0, 6), (0, 0)))

    hits = jnp.pad(switches, (EDGE, padded - count + EDGE), constant_values=-LANE)[:, None]
    decoded, stat, masks, z, full, weight = forward_block(
        inside, *sizes, image_group, hits, features, pairs, weights
    )
    grad, pair_grads, *wgrads = backward_block(
        inside, *sizes, d_decoded, z, stat, pairs, masks, full, weight
    )
    if not inside:
        wgrad = lax.psum_scatter(wgrads[0], "rows", scatter_dimension=1, tiled=True).astype(F32)
        wgrad = jnp.transpose(wgrad.reshape(2 * depth, shard, 9, -1)[:, :, ::-1], (0, 2, 1, 3))
        wgrads = [wgrad[:depth], wgrad[depth:]]
    return (
        decoded,
        grad,
        *wgrads,
        pair_grads[:depth, 1],
        pair_grads[:depth, 0],
        pair_grads[depth:, 1],
        pair_grads[depth:, 0],
    )


def solution(mesh):
    wide = P("rows", "grp")
    kernels = P(None, None, "rows", "grp")
    vector = P(None, "grp")
    return jax.shard_map(
        shards,
        mesh=mesh,
        in_specs=(wide, P(), P("rows"), kernels, kernels, vector, vector, vector, vector, wide),
        out_specs=(wide, wide, kernels, kernels, vector, vector, vector, vector),
        check_vma=False,
    )
```
